32 devices in a mesh: fsdp: 16 (over z, y, x), rep: 2 (over core).
Axes of the slice: x: 2, y: 2, z: 4, core: 2. Of those that a mesh axis runs over, the one named last changes fastest.
Arguments:
- tokens: bfloat16 [2, 64, 512, 768], P(None, ('fsdp', 'rep')), may hold values from -6 to 6
- masked: int32 [2, 64, 512], P(None, ('fsdp', 'rep')), may hold values from 0 to 1, as said below
- cotangent: bfloat16 [2, 64, 512, 768], P(None, ('fsdp', 'rep')), may hold values from -6 to 6
- mask_vector: bfloat16 [768], P('fsdp'), may hold values from -6 to 6
- heads_weight: bfloat16 [768, 2304], P('fsdp'), may hold values from -0.21875 to 0.21875
- query_bias: bfloat16 [768], P('fsdp'), may hold values from -3 to 3
- value_bias: bfloat16 [768], P('fsdp'), may hold values from -3 to 3
- output_weight: bfloat16 [768, 768], P('fsdp'), may hold values from -0.875 to 0.875
- output_bias: bfloat16 [768], P('fsdp'), may hold values from -3 to 3
- first_gain: bfloat16 [768], P('fsdp'), may hold values from 0.5 to 1.5
- first_shift: bfloat16 [768], P('fsdp'), may hold values from -3 to 3
- expand_weight: bfloat16 [768, 3072], P('fsdp'), may hold values from -0.21875 to 0.21875
- expand_bias: bfloat16 [3072], P('fsdp'), may hold values from -3 to 3
- reduce_weight: bfloat16 [3072, 768], P('fsdp'), may hold values from -0.109375 to 0.109375
- reduce_bias: bfloat16 [768], P('fsdp'), may hold values from -3 to 3
- second_gain: bfloat16 [768], P('fsdp'), may hold values from 0.5 to 1.5
- second_shift: bfloat16 [768], P('fsdp'), may hold values from -3 to 3
Outputs:
- outputs: bfloat16 [2, 64, 512, 768], P(None, ('fsdp', 'rep'))
- grad_tokens: bfloat16 [2, 64, 512, 768], P(None, ('fsdp', 'rep'))
- grad_mask_vector: float32 [768], P('fsdp')
- grad_heads_weight: float32 [768, 2304], P('fsdp')
- grad_query_bias: float32 [768], P('fsdp')
- grad_value_bias: float32 [768], P('fsdp')
- grad_output_weight: float32 [768, 768], P('fsdp')
- grad_output_bias: float32 [768], P('fsdp')
- grad_first_gain: float32 [768], P('fsdp')
- grad_first_shift: float32 [768], P('fsdp')
- grad_expand_weight: float32 [768, 3072], P('fsdp')
- grad_expand_bias: float32 [3072], P('fsdp')
- grad_reduce_weight: float32 [3072, 768], P('fsdp')
- grad_reduce_bias: float32 [768], P('fsdp')
- grad_second_gain: float32 [768], P('fsdp')
- grad_second_shift: float32 [768], P('fsdp')
The draws below stay inside these ranges and needn't reach their ends.
Inputs may be any that keep to these rules, and one draw needn't show every extreme that they name: 1 marks a masked position; masked positions come in runs of consecutive positions, and the share of masked positions differs from sequence to sequence.
All inputs are finite; a program needn't handle non-finite values.
Results may differ from the reference program's by a relative error of at most 0.022.
Values may be sent and summed in bfloat16 or wider, within the bound.
No kernel may reach another device: no remote copies, remote signals or barrier semaphores. Data moves between devices by JAX's collectives and lax.ppermute only.
A program may use at most 256 MiB of HBM per device.

```python
import jax
import jax.numpy as jnp
from jax import lax

D = 768
HEADS = 12
HEAD_DIM = 64
FF = 3072
LENGTH = 512
MICRO = 2
SEQ_DEV = 2
NSEQ = 64


def draw_masked(key, part):
    key = jax.random.fold_in(key, 7)
    rate_key, start_key, span_key = jax.random.split(key, 3)
    layout = (MICRO, NSEQ, LENGTH)
    start_rates = jax.random.randint(rate_key, (MICRO, NSEQ, 1), 2, 8)
    starts = jax.random.randint(start_key, layout, 0, 100) < start_rates
    uniform_draws = jax.random.randint(span_key, layout, 0, 1 << 20)
    limits = [int((1 << 20) * 0.8 ** power) for power in range(1, 10)]
    span_lengths = jnp.ones(layout, jnp.int32)
    for threshold in limits:
        span_lengths = span_lengths + (uniform_draws < threshold).astype(jnp.int32)
    covered = jnp.zeros(layout, bool)
    for offset in range(10):
        begins = starts & (span_lengths > offset)
        shifted = jnp.pad(begins, ((0, 0), (0, 0), (offset, 0)))[:, :, :LENGTH]
        covered = covered | shifted
    return covered.astype(jnp.int32)


def block_scale(rng, extent, cuts, least, top_value):
    loudness = 1.0
    for position, parts in cuts:
        steps = jax.random.uniform(jax.random.fold_in(jax.random.fold_in(rng, 6), position), (parts,), jnp.float32, least / len(cuts), top_value / len(cuts))
        loudness = loudness * jnp.repeat(jnp.exp(steps), extent[position] // parts).reshape((-1,) + (1,) * (len(extent) - 1 - position))
    return loudness


def normal_values(key, extent, deviation, limit, cuts=(), dtype=jnp.bfloat16):
    level = block_scale(key, extent, cuts, -0.22, 0.18) if cuts else 1.0
    drawn = jax.random.normal(key, extent, jnp.float32) * deviation * level
    return jnp.minimum(jnp.maximum(drawn, -limit), limit).astype(dtype)


def setup_inputs(seed: int = 0) -> dict:
    arg_keys = jax.random.split(jax.random.key(seed), 18)
    return {
        "tokens": normal_values(arg_keys[0], (MICRO, NSEQ, LENGTH, D), 1.0, 6.0, ((1, 32),)),
        "masked": draw_masked(jax.random.fold_in(arg_keys[17], 71), 0),
        "cotangent": normal_values(arg_keys[2], (MICRO, NSEQ, LENGTH, D), 1.0, 6.0, ((1, 32),)),
        "mask_vector": normal_values(arg_keys[3], (D,), 1.0, 6.0, ((0, 16),)),
        "heads_weight": normal_values(arg_keys[4], (D, 3 * D), D ** -0.5, 0.21875, ((0, 16),)),
        "query_bias": normal_values(arg_keys[5], (D,), 0.5, 3.0, ((0, 16),)),
        "value_bias": normal_values(arg_keys[6], (D,), 0.5, 3.0, ((0, 16),)),
        "output_weight": normal_values(arg_keys[7], (D, D), (D // 16) ** -0.5, 0.875, ((0, 16),)),
        "output_bias": normal_values(arg_keys[8], (D,), 0.5, 3.0, ((0, 16),)),
        "first_gain": jnp.clip(1.0 + 0.1 * jax.random.normal(arg_keys[9], (D,), jnp.float32), 0.5, 1.5).astype(jnp.bfloat16),
        "first_shift": normal_values(arg_keys[10], (D,), 0.5, 3.0, ((0, 16),)),
        "expand_weight": normal_values(arg_keys[11], (D, FF), D ** -0.5, 0.21875, ((0, 16),)),
        "expand_bias": normal_values(arg_keys[12], (FF,), 0.5, 3.0, ((0, 16),)),
        "reduce_weight": normal_values(arg_keys[13], (FF, D), FF ** -0.5, 0.109375, ((0, 16),)),
        "reduce_bias": normal_values(arg_keys[14], (D,), 0.5, 3.0, ((0, 16),)),
        "second_gain": jnp.clip(1.0 + 0.1 * jax.random.normal(arg_keys[15], (D,), jnp.float32), 0.5, 1.5).astype(jnp.bfloat16),
        "second_shift": normal_values(arg_keys[16], (D,), 0.5, 3.0, ((0, 16),)),
    }


@jax.custom_vjp
def low(v):
    return lax.optimization_barrier(v.astype(jnp.bfloat16)).astype(jnp.float32)

@jax.custom_vjp
def low_back(v):
    return v

def low_keep(v):
    return (low(v), None)

def low_pass(kept, grad):
    return (grad,)

def back_keep(v):
    return (v, None)

def back_low(kept, grad):
    return (low(grad),)
low.defvjp(low_keep, low_pass)
low_back.defvjp(back_keep, back_low)
epsilon = 1e-06
highest = lax.Precision.HIGHEST

def layer_norm(values, scaling, offset):
    centred = values - lax.optimization_barrier(jnp.mean(values, axis=-1, keepdims=True))
    spread = lax.optimization_barrier(jnp.mean(centred * centred, axis=-1, keepdims=True))
    return centred * lax.rsqrt(spread + epsilon) * scaling + offset

def exact_gelu(values):
    return jax.nn.gelu(values, approximate=False)

def attend(triple):
    queries, key_rows, value_rows = triple
    layout = (LENGTH, HEADS, HEAD_DIM)
    scores = jnp.einsum('qhd,khd->hqk', queries.reshape(layout), key_rows.reshape(layout), precision=highest) * HEAD_DIM ** (-0.5)
    probs = low(jax.nn.softmax(low_back(scores), axis=-1))
    context = jnp.einsum('hqk,khd->qhd', probs, value_rows.reshape(layout), precision=highest)
    return context.reshape(LENGTH, D)

def forward(params, tokens, masked):
    mask_vector, heads_weight, query_bias, value_bias, output_weight, output_bias, first_gain, first_shift, expand_weight, expand_bias, reduce_weight, reduce_bias, second_gain, second_shift = params
    chosen = masked.reshape(-1, 1) == 1
    inputs = jnp.where(chosen, mask_vector[None, :], tokens.reshape(-1, D))
    projected = jnp.dot(inputs, heads_weight, precision=highest)
    queries = low(low_back(projected[:, :D] + query_bias))
    key_rows = low(low_back(projected[:, D:2 * D]))
    value_rows = low(low_back(projected[:, 2 * D:] + value_bias))
    layout = (-1, LENGTH, D)
    context = lax.map(jax.checkpoint(attend), (queries.reshape(layout), key_rows.reshape(layout), value_rows.reshape(layout)))
    context = low(low_back(context.reshape(-1, D)))
    branch = low_back(jnp.dot(context, output_weight, precision=highest) + output_bias)
    normed = layer_norm(inputs + branch, first_gain, first_shift)
    hidden = low_back(jnp.dot(low(normed), expand_weight, precision=highest) + expand_bias)
    active = low(exact_gelu(hidden))
    second = low_back(jnp.dot(active, reduce_weight, precision=highest) + reduce_bias)
    return layer_norm(normed + second, second_gain, second_shift).reshape(tokens.shape)

def reference(tokens, masked, cotangent, mask_vector, heads_weight, query_bias, value_bias, output_weight, output_bias, first_gain, first_shift, expand_weight, expand_bias, reduce_weight, reduce_bias, second_gain, second_shift):
    params = tuple((member.astype(jnp.float32) for member in (mask_vector, heads_weight, query_bias, value_bias, output_weight, output_bias, first_gain, first_shift, expand_weight, expand_bias, reduce_weight, reduce_bias, second_gain, second_shift)))
    blocks = tokens.reshape(-1, SEQ_DEV, LENGTH, D).astype(jnp.float32)
    mask_blocks = masked.reshape(-1, SEQ_DEV, LENGTH)
    cot_blocks = cotangent.reshape(-1, SEQ_DEV, LENGTH, D).astype(jnp.float32)

    def accumulate(totals, item):
        block_rows, mask_block, cot_block = item

        def inner(param_set, token_rows):
            return forward(param_set, token_rows, mask_block)
        result, pullback = jax.vjp(inner, params, block_rows)
        upstream = cot_block * (mask_block[..., None] == 1).astype(jnp.float32)
        grad_params, grad_block = pullback(upstream)
        return (jax.tree.map(jnp.add, totals, grad_params), (result.astype(jnp.bfloat16), grad_block.astype(jnp.bfloat16)))
    zeros = tuple((jnp.zeros_like(member) for member in params))
    totals, (results, grad_blocks) = lax.scan(accumulate, zeros, (blocks, mask_blocks, cot_blocks))
    return (results.reshape(tokens.shape), grad_blocks.reshape(tokens.shape), totals[0], totals[1], totals[2], totals[3], totals[4], totals[5], totals[6], totals[7], totals[8], totals[9], totals[10], totals[11], totals[12], totals[13])
```

```python
import functools

import jax
import jax.numpy as jnp
import numpy as np
from jax import lax
from jax.experimental import pallas as pl
from jax.experimental.pallas import tpu as pltpu
from jax.sharding import PartitionSpec as P

D = 768
HEADS = 12
HEAD_DIM = 64
FF = 3072
L = 512
QKV = 3 * D
LANES = 128
BLOCKS = 16
EPSILON = 1e-06
ALL = ("fsdp", "rep")
VECTORS = 13

bf16 = jnp.bfloat16
f32 = jnp.float32

NN = ((1,), (0,))
NT = ((1,), (1,))
TN = ((0,), (0,))


def dot(left, right, dims):
    return lax.dot_general(left, right, (dims, ((), ())), preferred_element_type=f32)


def params():
    return pltpu.CompilerParams(vmem_limit_bytes=60 << 20)


def shaped(shape, dtype):
    return jax.ShapeDtypeStruct(shape, dtype)


def rows(size, width, shift=0):
    return pl.BlockSpec((size, width), lambda i: (i + shift, 0))


def whole(shape):
    return pl.BlockSpec(shape, lambda i: (0,) * len(shape), pipeline_mode=pl.Buffered(1))


SMEM = pl.BlockSpec(memory_space=pltpu.SMEM)
ANY = pl.BlockSpec(memory_space=pl.ANY)


def fetch_copies(table, mine, other, target, sems, height, source_column, width):
    core = table[64]
    copies = []
    for half, source in ((0, mine), (1, other)):
        place = core if half == 0 else 1 - core
        column = pl.multiple_of(place * width, LANES)
        for block in range(BLOCKS):
            owner = table[16 * half + block]
            copies.append(
                pltpu.make_async_copy(
                    source.at[pl.ds(block * height, height), pl.ds(source_column, width)],
                    target.at[pl.ds(pl.multiple_of(owner * height, 16), height), pl.ds(column, width)],
                    sems.at[16 * half + block],
                )
            )
    return copies


def spread_copies(table, staged, keep, send, sems, height, target_column, width):
    core = table[64]
    copies = []
    for half, target in ((0, keep), (1, send)):
        place = core if half == 0 else 1 - core
        column = pl.multiple_of(place * width, LANES)
        for block in range(BLOCKS):
            owner = table[32 + 16 * half + block]
            copies.append(
                pltpu.make_async_copy(
                    staged.at[pl.ds(pl.multiple_of(owner * height, 16), height), pl.ds(column, width)],
                    target.at[pl.ds(block * height, height), pl.ds(target_column, width)],
                    sems.at[16 * half + block],
                )
            )
    return copies


def start_all(copies):
    for copy in copies:
        copy.start()


def wait_all(copies):
    for copy in copies:
        copy.wait()


def fold(values):
    height, width = values.shape
    return jnp.sum(values.reshape(height // 8, 8, width), axis=0)


def six(column):
    return jnp.concatenate([column] * (D // LANES), axis=1)


def lane_first(height):
    return lax.broadcasted_iota(jnp.int32, (height, LANES), 1) < HEAD_DIM


def normalise(values):
    mean = jnp.mean(values, axis=1, keepdims=True)
    centred = values - mean
    spread = jnp.mean(centred * centred, axis=1, keepdims=True)
    rate = lax.rsqrt(spread + EPSILON)
    return centred * rate, rate


def norm_back(weighted, unit, rate):
    return rate * (
        weighted
        - jnp.mean(weighted, axis=1, keepdims=True)
        - unit * jnp.mean(weighted * unit, axis=1, keepdims=True)
    )


def attend_kernel(
    table, tokens, mask, mine, other, *refs
):
    x_out, qkv_out, raised_out, inverse_out, context_out, turned_out, vec_out = refs[-12:-5]
    weight, columns, vectors, sems, vec_sems = refs[-5:]

    @pl.when(pl.program_id(0) == 0)
    def _():
        copies = fetch_copies(table, mine, other, weight, sems, D // BLOCKS, 0, QKV // 2)
        height = D // BLOCKS
        for block in range(BLOCKS):
            copies.append(
                pltpu.make_async_copy(
                    mine.at[pl.ds(block * height, height), pl.ds(QKV // 2, LANES)],
                    columns.at[pl.ds(pl.multiple_of(table[block] * height, 16), height), :],
                    vec_sems.at[block],
                )
            )
        start_all(copies)
        wait_all(copies)
        vectors[...] = columns[...].astype(f32).T[:16]
        vec_out[...] = vectors[...]

    chosen = six(mask[...]) > 0
    x = jnp.where(chosen, jnp.broadcast_to(vectors[0:1, :].astype(bf16), (L, D)), tokens[...])
    x_out[...] = x
    queries = dot(x, weight[:, :D], NN) + vectors[1:2, :]
    qkv_out[:, :D] = queries.astype(bf16) * jnp.asarray(HEAD_DIM**-0.5, bf16)
    qkv_out[:, D : 2 * D] = dot(x, weight[:, D : 2 * D], NN).astype(bf16)
    qkv_out[:, 2 * D :] = (dot(x, weight[:, 2 * D :], NN) + vectors[2:3, :]).astype(bf16)
    first = lane_first(L)
    for pair in range(HEADS // 2):
        low = LANES * pair
        queries = qkv_out[:, low : low + LANES]
        keys = qkv_out[:, D + low : D + low + LANES]
        values = qkv_out[:, 2 * D + low : 2 * D + low + LANES].T
        for part in range(2):
            head = 2 * pair + part
            lanes = first if part == 0 else ~first
            scores = dot(keys, jnp.where(lanes, queries, jnp.zeros_like(queries)), NT)
            raised = jnp.exp(scores - jnp.max(scores, axis=0, keepdims=True)).astype(bf16)
            raised_out[head] = raised
            stacked = jnp.concatenate(
                [values[HEAD_DIM * part : HEAD_DIM * (part + 1)], jnp.ones((16, L), bf16)], axis=0
            )
            mixed = dot(stacked, raised, NN)
            inverse = 1.0 / mixed[HEAD_DIM : HEAD_DIM + 1]
            inverse_out[head : head + 1, :] = inverse
            turned_out[HEAD_DIM * head : HEAD_DIM * (head + 1), :] = (mixed[:HEAD_DIM] * inverse).astype(bf16)
    context_out[...] = turned_out[...].T


def attend(table, tokens, mask, mine, other, earlier, start, count):
    height = tokens.shape[0]
    total = height // L
    shapes = [
        shaped((height, D), bf16),
        shaped((height, QKV), bf16),
        shaped((total, HEADS, L, L), bf16),
        shaped((total, 16, L), f32),
        shaped((height, D), bf16),
        shaped((total, D, L), bf16),
        shaped((16, D), f32),
    ]
    passed = list(earlier[:6]) if earlier else []
    return pl.pallas_call(
        attend_kernel,
        name="attend",
        grid=(count,),
        in_specs=[SMEM, rows(L, D, start), rows(L, LANES, start), ANY, ANY] + [ANY] * len(passed),
        out_specs=[
            rows(L, D, start),
            rows(L, QKV, start),
            pl.BlockSpec((None, HEADS, L, L), lambda i: (i + start, 0, 0, 0)),
            pl.BlockSpec((None, 16, L), lambda i: (i + start, 0, 0)),
            rows(L, D, start),
            pl.BlockSpec((None, D, L), lambda i: (i + start, 0, 0)),
            whole((16, D)),
        ],
        out_shape=shapes,
        scratch_shapes=[
            pltpu.VMEM((D, QKV), bf16),
            pltpu.VMEM((D, LANES), bf16),
            pltpu.VMEM((16, D), f32),
            pltpu.SemaphoreType.DMA((32,)),
            pltpu.SemaphoreType.DMA((16,)),
        ],
        input_output_aliases={5 + i: i for i in range(len(passed))},
        compiler_params=params(),
        cost_estimate=pl.CostEstimate(
            flops=count * (2 * L * D * QKV + 16 * L * L * D), bytes_accessed=count * 14_000_000, transcendentals=0
        ),
    )(table, tokens, mask, mine, other, *passed)


def expand_kernel(table, context, x, vec, bias, mine, other, *refs):
    unit_out, rate_out, low_out, active_out, slope_out = refs[-9:-4]
    out_weight, weight, sems, more_sems = refs[-4:]

    @pl.when(pl.program_id(0) == 0)
    def _():
        copies = fetch_copies(table, mine, other, out_weight, sems, D // BLOCKS, 0, D // 2)
        copies += fetch_copies(table, mine, other, weight, more_sems, D // BLOCKS, D // 2, FF // 2)
        start_all(copies)
        wait_all(copies)

    first_sum = x[...].astype(f32) + (dot(context[...], out_weight[...], NN) + vec[3:4, :])
    unit, rate = normalise(first_sum)
    unit_out[...] = unit
    rate_out[...] = jnp.broadcast_to(rate, rate_out.shape)
    low = (unit * vec[4:5, :] + vec[5:6, :]).astype(bf16)
    low_out[...] = low
    step = 512
    for part in range(FF // step):
        span = slice(step * part, step * (part + 1))
        hidden = dot(low, weight[:, span], NN) + bias[0:1, span]
        share = 0.5 * (1.0 + lax.erf(hidden * (2.0**-0.5)))
        density = jnp.exp(-0.5 * hidden * hidden) * ((2.0 * np.pi) ** -0.5)
        active_out[:, span] = (hidden * share).astype(bf16)
        slope_out[:, span] = (share + hidden * density).astype(bf16)


def expand(table, context, x, vec, bias, mine, other, earlier, start, count, size):
    height = x.shape[0]
    shapes = [
        shaped((height, D), f32),
        shaped((height, LANES), f32),
        shaped((height, D), bf16),
        shaped((height, FF), bf16),
        shaped((height, FF), bf16),
    ]
    passed = list(earlier) if earlier else []
    return pl.pallas_call(
        expand_kernel,
        name="expand",
        grid=(count,),
        in_specs=[SMEM, rows(size, D, start), rows(size, D, start), whole((16, D)), whole((1, FF)), ANY, ANY]
        + [ANY] * len(passed),
        out_specs=[
            rows(size, D, start),
            rows(size, LANES, start),
            rows(size, D, start),
            rows(size, FF, start),
            rows(size, FF, start),
        ],
        out_shape=shapes,
        scratch_shapes=[
            pltpu.VMEM((D, D), bf16),
            pltpu.VMEM((D, FF), bf16),
            pltpu.SemaphoreType.DMA((32,)),
            pltpu.SemaphoreType.DMA((32,)),
        ],
        input_output_aliases={7 + i: i for i in range(len(passed))},
        compiler_params=params(),
        cost_estimate=pl.CostEstimate(
            flops=count * size * 2 * D * (D + FF), bytes_accessed=count * size * 20_000, transcendentals=0
        ),
    )(table, context, x, vec, bias, mine, other, *passed)


def reduce_kernel(
    table, active, slope, unit_in, cotangent, mask, vec, mine, other,
    outputs, outer_out, hidden_out, sums, bias_sums, keep, send,
    weight, total, staged, sems, out_sems,
):
    step = pl.program_id(0)

    @pl.when(step == 0)
    def _():
        copies = fetch_copies(table, mine, other, weight, sems, FF // BLOCKS, 0, D // 2)
        start_all(copies)
        sums[...] = jnp.zeros_like(sums)
        bias_sums[...] = jnp.zeros_like(bias_sums)
        total[...] = jnp.zeros_like(total)
        wait_all(copies)

    height = active.shape[0]
    parts = 2
    share = height // parts
    lows = []
    for part in range(parts):
        span = slice(share * part, share * (part + 1))
        normed = unit_in[span, :] * vec[4:5, :] + vec[5:6, :]
        second = normed + (dot(active[span, :], weight[...], NN) + vec[10:11, :])
        unit, rate = normalise(second)
        outputs[span, :] = (unit * vec[11:12, :] + vec[12:13, :]).astype(bf16)
        upstream = jnp.where(six(mask[span, :]) > 0, cotangent[span, :].astype(f32), 0.0)
        outer = norm_back(upstream * vec[11:12, :], unit, rate)
        outer_out[span, :] = outer
        low = outer.astype(bf16)
        sums[0:8, :] += fold(upstream * unit)
        sums[8:16, :] += fold(upstream)
        sums[16:24, :] += fold(low.astype(f32))
        width = 512
        for piece in range(FF // width):
            units = slice(width * piece, width * (piece + 1))
            grad = dot(low, weight[units, :], NT) * slope[span, units].astype(f32)
            grad_low = grad.astype(bf16)
            hidden_out[span, units] = grad_low
            bias_sums[:, units] += fold(grad_low.astype(f32))
        lows.append(low)
    low = jnp.concatenate(lows, axis=0)
    for piece in range(FF // D):
        units = slice(D * piece, D * (piece + 1))
        total[units, :] += dot(active[:, units], low, TN)

    @pl.when(step == pl.num_programs(0) - 1)
    def _():
        staged[...] = total[...].astype(bf16)
        copies = spread_copies(table, staged, keep, send, out_sems, FF // BLOCKS, 0, D // 2)
        start_all(copies)
        wait_all(copies)


def reduce(table, active, slope, unit, cotangent, mask, vec, mine, other, size):
    height = active.shape[0]
    return pl.pallas_call(
        reduce_kernel,
        name="reduce",
        grid=(height // size,),
        in_specs=[
            SMEM,
            rows(size, FF),
            rows(size, FF),
            rows(size, D),
            rows(size, D),
            rows(size, LANES),
            whole((16, D)),
            ANY,
            ANY,
        ],
        out_specs=[rows(size, D), rows(size, D), rows(size, FF), whole((24, D)), whole((8, FF)), ANY, ANY],
        out_shape=[
            shaped((height, D), bf16),
            shaped((height, D), f32),
            shaped((height, FF), bf16),
            shaped((24, D), f32),
            shaped((8, FF), f32),
            shaped((FF, D // 2), bf16),
            shaped((FF, D // 2), bf16),
        ],
        scratch_shapes=[
            pltpu.VMEM((FF, D), bf16),
            pltpu.VMEM((FF, D), f32),
            pltpu.VMEM((FF, D), bf16),
            pltpu.SemaphoreType.DMA((32,)),
            pltpu.SemaphoreType.DMA((32,)),
        ],
        compiler_params=params(),
        cost_estimate=pl.CostEstimate(flops=height * 6 * D * FF, bytes_accessed=height * 30_000, transcendentals=0),
    )(table, active, slope, unit, cotangent, mask, vec, mine, other)


def inner_kernel(
    table, hidden, outer, unit_in, rate_in, low_in, context, mask, vec, mine, other,
    inner_out, context_out, sums, keep, send,
    out_weight, weight, out_total, total, out_staged, staged, sems, more_sems, out_sems, more_out_sems,
):
    step = pl.program_id(0)

    @pl.when(step == 0)
    def _():
        copies = fetch_copies(table, mine, other, out_weight, sems, D // BLOCKS, 0, D // 2)
        copies += fetch_copies(table, mine, other, weight, more_sems, D // BLOCKS, D // 2, FF // 2)
        start_all(copies)
        sums[...] = jnp.zeros_like(sums)
        out_total[...] = jnp.zeros_like(out_total)
        total[...] = jnp.zeros_like(total)
        wait_all(copies)

    grad_normed = outer[...] + dot(hidden[...], weight[...], NT)
    low = low_in[...]
    for piece in range(FF // D):
        units = slice(D * piece, D * (piece + 1))
        total[:, units] += dot(low, hidden[:, units], TN)
    unit = unit_in[...]
    sums[0:8, :] += fold(grad_normed * unit)
    sums[8:16, :] += fold(grad_normed)
    inner = norm_back(grad_normed * vec[4:5, :], unit, six(rate_in[...]))
    inner_out[...] = inner
    branch = inner.astype(bf16)
    sums[16:24, :] += fold(branch.astype(f32))
    sums[24:32, :] += fold(jnp.where(six(mask[...]) > 0, inner, 0.0))
    context_out[...] = dot(branch, out_weight[...], NT).astype(bf16)
    out_total[...] += dot(context[...], branch, TN)

    @pl.when(step == pl.num_programs(0) - 1)
    def _():
        out_staged[...] = out_total[...].astype(bf16)
        staged[...] = total[...].astype(bf16)
        copies = spread_copies(table, out_staged, keep, send, out_sems, D // BLOCKS, 0, D // 2)
        copies += spread_copies(table, staged, keep, send, more_out_sems, D // BLOCKS, D // 2, FF // 2)
        start_all(copies)
        wait_all(copies)


def inner_pass(table, hidden, outer, unit, rate, low, context, mask, vec, mine, other, size):
    height = hidden.shape[0]
    return pl.pallas_call(
        inner_kernel,
        name="inner",
        grid=(height // size,),
        in_specs=[
            SMEM,
            rows(size, FF),
            rows(size, D),
            rows(size, D),
            rows(size, LANES),
            rows(size, D),
            rows(size, D),
            rows(size, LANES),
            whole((16, D)),
            ANY,
            ANY,
        ],
        out_specs=[rows(size, D), rows(size, D), whole((32, D)), ANY, ANY],
        out_shape=[
            shaped((height, D), f32),
            shaped((height, D), bf16),
            shaped((32, D), f32),
            shaped((D, (D + FF) // 2), bf16),
            shaped((D, (D + FF) // 2), bf16),
        ],
        scratch_shapes=[
            pltpu.VMEM((D, D), bf16),
            pltpu.VMEM((D, FF), bf16),
            pltpu.VMEM((D, D), f32),
            pltpu.VMEM((D, FF), f32),
            pltpu.VMEM((D, D), bf16),
            pltpu.VMEM((D, FF), bf16),
            pltpu.SemaphoreType.DMA((32,)),
            pltpu.SemaphoreType.DMA((32,)),
            pltpu.SemaphoreType.DMA((32,)),
            pltpu.SemaphoreType.DMA((32,)),
        ],
        compiler_params=params(),
        cost_estimate=pl.CostEstimate(
            flops=height * 4 * D * (D + FF), bytes_accessed=height * 20_000, transcendentals=0
        ),
    )(table, hidden, outer, unit, rate, low, context, mask, vec, mine, other)


def attend_back_kernel(qkv, raised_in, inverse_in, turned, grad_context, *refs):
    mixed_out, turned_grad = refs[-2:]
    first = lane_first(L)
    blank = jnp.zeros((HEAD_DIM, L), bf16)
    for pair in range(HEADS // 2):
        low = LANES * pair
        queries = qkv[:, low : low + LANES]
        keys = qkv[:, D + low : D + low + LANES]
        values = qkv[:, 2 * D + low : 2 * D + low + LANES]
        grads = grad_context[:, low : low + LANES].T.astype(f32)
        turned_keys = keys.T
        grad_values = None
        grad_keys = None
        for part in range(2):
            head = 2 * pair + part
            span = slice(HEAD_DIM * part, HEAD_DIM * (part + 1))
            outer_span = slice(HEAD_DIM * head, HEAD_DIM * (head + 1))
            grad = grads[span] * inverse_in[head : head + 1, :]
            level = jnp.sum(grad * turned[outer_span, :].astype(f32), axis=0, keepdims=True)
            grad_low = grad.astype(bf16)
            padded = jnp.concatenate([grad_low, blank] if part == 0 else [blank, grad_low], axis=0)
            raised = raised_in[head]
            grad_scores = (raised.astype(f32) * (dot(values, padded, NN) - level)).astype(bf16)
            lanes = first if part == 0 else ~first
            chosen = jnp.where(lanes, queries, jnp.zeros_like(queries))
            value_term = dot(raised, padded, NT)
            key_term = dot(grad_scores, chosen, NN)
            grad_values = value_term if part == 0 else grad_values + value_term
            grad_keys = key_term if part == 0 else grad_keys + key_term
            turned_grad[outer_span, :] = dot(turned_keys[span], grad_scores, NN) * HEAD_DIM**-0.5
        mixed_out[:, low : low + LANES] = turned_grad[low : low + LANES, :].T.astype(bf16)
        mixed_out[:, D + low : D + low + LANES] = grad_keys.astype(bf16)
        mixed_out[:, 2 * D + low : 2 * D + low + LANES] = grad_values.astype(bf16)


def attend_back(qkv, raised, inverse, turned, grad_context, earlier, start, count):
    height = qkv.shape[0]
    passed = [earlier] if earlier is not None else []
    return pl.pallas_call(
        attend_back_kernel,
        name="attend_back",
        grid=(count,),
        in_specs=[
            rows(L, QKV, start),
            pl.BlockSpec((None, HEADS, L, L), lambda i: (i + start, 0, 0, 0)),
            pl.BlockSpec((None, 16, L), lambda i: (i + start, 0, 0)),
            pl.BlockSpec((None, D, L), lambda i: (i + start, 0, 0)),
            rows(L, D, start),
        ]
        + [ANY] * len(passed),
        out_specs=rows(L, QKV, start),
        out_shape=shaped((height, QKV), bf16),
        scratch_shapes=[pltpu.VMEM((D, L), f32)],
        input_output_aliases={5: 0} if passed else {},
        compiler_params=params(),
        cost_estimate=pl.CostEstimate(flops=count * 32 * L * L * D, bytes_accessed=count * 14_000_000, transcendentals=0),
    )(qkv, raised, inverse, turned, grad_context, *passed)


def heads_kernel(
    table, x, marks, mixed, second_sums, inner_sums, bias_rows, mine, other,
    keep, send,
    total, staged, columns, weight, sems, out_sems, vec_sems,
):
    step = pl.program_id(0)

    @pl.when(step == 0)
    def _():
        start_all(fetch_copies(table, mine, other, weight, sems, D // BLOCKS, 0, QKV // 2))
        total[...] = jnp.zeros_like(total)

    turned = jnp.concatenate([x[...].T, marks[...]], axis=0)
    for piece in range(3):
        span = slice(D * piece, D * (piece + 1))
        total[:, span] += dot(turned, mixed[:, span], NN)

    @pl.when(step == pl.num_programs(0) - 1)
    def _():
        wait_all(fetch_copies(table, mine, other, weight, sems, D // BLOCKS, 0, QKV // 2))
        staged[...] = total[:D, :].astype(bf16)
        copies = spread_copies(table, staged, keep, send, out_sems, D // BLOCKS, 0, QKV // 2)
        start_all(copies)
        whole_sums = total[D : D + 1, :]
        masked_sums = total[D + 1 : D + 2, :]
        high = masked_sums.astype(bf16)
        low = (masked_sums - high.astype(f32)).astype(bf16)
        split = jnp.concatenate([high, low, jnp.zeros((14, QKV), bf16)], axis=0)
        reached = jnp.sum(dot(split, weight[...], NT), axis=0, keepdims=True)

        def line(ref, group):
            return jnp.sum(ref[8 * group : 8 * (group + 1), :], axis=0, keepdims=True)

        lines = [
            reached + line(inner_sums, 3),
            whole_sums[:, :D],
            whole_sums[:, 2 * D :],
            line(inner_sums, 2),
            line(inner_sums, 0),
            line(inner_sums, 1),
            bias_rows[...],
            line(second_sums, 2),
            line(second_sums, 0),
            line(second_sums, 1),
            jnp.zeros((LANES - VECTORS, D), f32),
        ]
        columns[...] = jnp.concatenate(lines, axis=0).T.astype(bf16)
        height = D // BLOCKS
        more = []
        for half, target in ((0, keep), (1, send)):
            for block in range(BLOCKS):
                owner = table[32 + 16 * half + block]
                more.append(
                    pltpu.make_async_copy(
                        columns.at[pl.ds(pl.multiple_of(owner * height, 16), height), :],
                        target.at[pl.ds(block * height, height), pl.ds(QKV // 2, LANES)],
                        vec_sems.at[16 * half + block],
                    )
                )
        start_all(more)
        wait_all(copies + more)


def heads_grad(table, x, marks, mixed, second_sums, inner_sums, bias_rows, mine, other, size):
    height = x.shape[0]
    wide = QKV // 2 + LANES
    return pl.pallas_call(
        heads_kernel,
        name="heads_grad",
        grid=(height // size,),
        in_specs=[
            SMEM,
            rows(size, D),
            pl.BlockSpec((16, size), lambda i: (0, i)),
            rows(size, QKV),
            whole((24, D)),
            whole((32, D)),
            whole((4, D)),
            ANY,
            ANY,
        ],
        out_specs=[ANY, ANY],
        out_shape=[shaped((D, wide), bf16), shaped((D, wide), bf16)],
        scratch_shapes=[
            pltpu.VMEM((D + 16, QKV), f32),
            pltpu.VMEM((D, QKV), bf16),
            pltpu.VMEM((D, LANES), bf16),
            pltpu.VMEM((D, QKV), bf16),
            pltpu.SemaphoreType.DMA((32,)),
            pltpu.SemaphoreType.DMA((32,)),
            pltpu.SemaphoreType.DMA((32,)),
        ],
        compiler_params=params(),
        cost_estimate=pl.CostEstimate(flops=height * 2 * D * QKV, bytes_accessed=height * 10_000, transcendentals=0),
    )(table, x, marks, mixed, second_sums, inner_sums, bias_rows, mine, other)


def rows_kernel(table, mixed, inner, mask, mine, other, grad_out, weight, sems):
    @pl.when(pl.program_id(0) == 0)
    def _():
        copies = fetch_copies(table, mine, other, weight, sems, D // BLOCKS, 0, QKV // 2)
        start_all(copies)
        wait_all(copies)

    grad = inner[...] + dot(mixed[...], weight[...], NT)
    grad_out[...] = jnp.where(six(mask[...]) > 0, 0.0, grad).astype(bf16)


def rows_grad(table, mixed, inner, mask, mine, other, size):
    height = mixed.shape[0]
    return pl.pallas_call(
        rows_kernel,
        name="rows_grad",
        grid=(height // size,),
        in_specs=[SMEM, rows(size, QKV), rows(size, D), rows(size, LANES), ANY, ANY],
        out_specs=rows(size, D),
        out_shape=shaped((height, D), bf16),
        scratch_shapes=[pltpu.VMEM((D, QKV), bf16), pltpu.SemaphoreType.DMA((32,))],
        compiler_params=params(),
        cost_estimate=pl.CostEstimate(flops=height * 2 * D * QKV, bytes_accessed=height * 10_000, transcendentals=0),
    )(table, mixed, inner, mask, mine, other)


def around_z(hops):
    return [(i, (i + 8 * hops) % 32) for i in range(32)]


def across(turn):
    return [(i, i ^ (2 if (i & 1) == turn else 4)) for i in range(32)]


def between_cores():
    return [(i, i ^ 1) for i in range(32)]


def make_table():
    table = np.zeros((32, 65), np.int32)
    for device in range(32):
        core, x, y, z = device & 1, (device >> 1) & 1, (device >> 2) & 1, device >> 3
        table[device, 64] = core
        for half in range(2):
            turn = core ^ half
            for block in range(16):
                hops, near, far = block & 3, (block >> 2) & 1, block >> 3
                there_x, there_y = (x ^ near, y ^ far) if turn == 0 else (x ^ far, y ^ near)
                table[device, 16 * half + block] = ((z - hops) % 4) * 4 + there_y * 2 + there_x
                near, far = far, near
                there_x, there_y = (x ^ near, y ^ far) if turn == 0 else (x ^ far, y ^ near)
                table[device, 32 + 16 * half + block] = ((z + hops) % 4) * 4 + there_y * 2 + there_x
    return table


def gather_blocks(block):
    parts = [block] + [lax.ppermute(block, ALL, around_z(hops)) for hops in (1, 2, 3)]
    held = jnp.concatenate(parts, axis=0)
    held = jnp.concatenate([held, lax.ppermute(held, ALL, across(0))], axis=0)
    held = jnp.concatenate([held, lax.ppermute(held, ALL, across(1))], axis=0)
    return held, lax.ppermute(held, ALL, between_cores())


def add_low(*terms):
    total = terms[0].astype(f32)
    for term in terms[1:]:
        total = total + term.astype(f32)
    return total


def scatter_blocks(keep, send):
    height = keep.shape[0]
    arrived = lax.ppermute(send, ALL, between_cores())
    for turn in (0, 1):
        half = height // 2
        kept = add_low(keep[:half], arrived[:half]).astype(bf16)
        sent = add_low(keep[half:], arrived[half:]).astype(bf16)
        keep, arrived = kept, lax.ppermute(sent, ALL, across(turn))
        height = half
    quarter = height // 4
    pieces = [
        add_low(keep[quarter * hops : quarter * (hops + 1)], arrived[quarter * hops : quarter * (hops + 1)])
        for hops in range(4)
    ]
    moved = [lax.ppermute(pieces[hops].astype(bf16), ALL, around_z(hops)) for hops in (1, 2, 3)]
    return add_low(pieces[0], *moved)


def gather_plain(mine, other):
    return (
        lax.all_gather(mine, "fsdp", axis=0, tiled=True),
        lax.all_gather(other, "fsdp", axis=0, tiled=True),
    )


def scatter_plain(keep, send):
    both = add_low(keep, lax.ppermute(send, "rep", [(0, 1), (1, 0)]))
    return lax.psum_scatter(both, "fsdp", scatter_dimension=0, tiled=True)


def join(core, mine):
    other = lax.ppermute(mine, "rep", [(0, 1), (1, 0)])
    low = jnp.where(core == 0, mine, other)
    high = jnp.where(core == 0, other, mine)
    return jnp.concatenate([low, high], axis=1)


def half_of(weight, place):
    width = weight.shape[1] // 2
    return lax.dynamic_slice_in_dim(weight, place * width, width, axis=1)


def local(
    chips,
    tokens,
    masked,
    cotangent,
    mask_vector,
    heads_weight,
    query_bias,
    value_bias,
    output_weight,
    output_bias,
    first_gain,
    first_shift,
    expand_weight,
    expand_bias,
    reduce_weight,
    reduce_bias,
    second_gain,
    second_shift,
):
    core = lax.axis_index("rep")
    layout = tokens.shape
    height = layout[0] * layout[1] * layout[2]
    share = mask_vector.shape[0]
    by_hops = chips == BLOCKS
    if by_hops:
        table = lax.dynamic_index_in_dim(
            jnp.asarray(make_table()), lax.axis_index("fsdp") * 2 + core, axis=0, keepdims=False
        )
    else:
        table = jnp.concatenate([jnp.tile(jnp.arange(BLOCKS, dtype=jnp.int32), 4), core[None].astype(jnp.int32)])

    vector_rows = jnp.concatenate(
        [
            mask_vector[None],
            query_bias[None],
            value_bias[None],
            output_bias[None],
            first_gain[None],
            first_shift[None],
            expand_bias.reshape(4, share),
            reduce_bias[None],
            second_gain[None],
            second_shift[None],
        ],
        axis=0,
    )
    vector_columns = jnp.pad(vector_rows.T, ((0, 0), (0, LANES - VECTORS)))

    def payloads(place):
        return (
            jnp.concatenate([half_of(heads_weight, place), vector_columns], axis=1),
            jnp.concatenate([half_of(output_weight, place), half_of(expand_weight, place)], axis=1),
            half_of(reduce_weight, place),
        )

    if by_hops:
        gathered = [gather_blocks(payload) for payload in payloads(core)]
    else:
        gathered = [gather_plain(a, b) for a, b in zip(payloads(core), payloads(1 - core))]
    heads, middle, last = gathered
    scatter = scatter_blocks if by_hops else scatter_plain

    flat_tokens = tokens.reshape(height, D)
    flat_cotangent = cotangent.reshape(height, D)
    flags = masked.reshape(height).astype(bf16)
    mask = jnp.broadcast_to(flags[:, None], (height, LANES))
    marks = jnp.concatenate([jnp.ones((1, height), bf16), flags[None], jnp.zeros((14, height), bf16)], axis=0)

    sequences = height // L
    half = sequences // 2
    done = attend(table, flat_tokens, mask, *heads, None, 0, half)
    vec = done[6]
    done = attend(table, flat_tokens, mask, *heads, done, half, sequences - half)
    x, qkv, raised, inverse, context, turned = done[:6]
    bias = vec[6:10].reshape(4, D // share, share).transpose(1, 0, 2).reshape(1, FF)

    size = 512
    steps = height // size
    early = steps // 2
    opened = expand(table, context, x, vec, bias, *middle, None, 0, early, size)
    opened = expand(table, context, x, vec, bias, *middle, opened, early, steps - early, size)
    unit, rate, low, active, slope = opened

    outputs, outer, hidden, second_sums, bias_sums, keep, send = reduce(
        table, active, slope, unit, flat_cotangent, mask, vec, *last, size
    )
    last_grad = scatter(keep, send)
    bias_rows = jnp.sum(bias_sums, axis=0).reshape(D // share, 4, share).transpose(1, 0, 2).reshape(4, D)

    inner, grad_context, inner_sums, keep, send = inner_pass(
        table, hidden, outer, unit, rate, low, context, mask, vec, *middle, size
    )
    middle_grad = scatter(keep, send)

    mixed = attend_back(qkv, raised, inverse, turned, grad_context, None, 0, half)
    mixed = attend_back(qkv, raised, inverse, turned, grad_context, mixed, half, sequences - half)

    keep, send = heads_grad(table, x, marks, mixed, second_sums, inner_sums, bias_rows, *heads, size)
    heads_share = scatter(keep, send)
    grad_tokens = rows_grad(table, mixed, inner, mask, *heads, size)

    vector_grads = heads_share[:, QKV // 2 :]

    def vector(index):
        return vector_grads[:, index]

    return (
        outputs.reshape(layout),
        grad_tokens.reshape(layout),
        vector(0),
        join(core, heads_share[:, : QKV // 2]),
        vector(1),
        vector(2),
        join(core, middle_grad[:, : D // 2]),
        vector(3),
        vector(4),
        vector(5),
        join(core, middle_grad[:, D // 2 :]),
        vector_grads[:, 6:10].T.reshape(-1),
        join(core, last_grad),
        vector(10),
        vector(11),
        vector(12),
    )


def solution(mesh):
    in_specs = (
        P(None, ("fsdp", "rep"), None, None),
        P(None, ("fsdp", "rep"), None),
        P(None, ("fsdp", "rep"), None, None),
        P("fsdp"),
        P("fsdp", None),
        P("fsdp"),
        P("fsdp"),
        P("fsdp", None),
        P("fsdp"),
        P("fsdp"),
        P("fsdp"),
        P("fsdp", None),
        P("fsdp"),
        P("fsdp", None),
        P("fsdp"),
        P("fsdp"),
        P("fsdp"),
    )
    out_specs = (
        P(None, ("fsdp", "rep"), None, None),
        P(None, ("fsdp", "rep"), None, None),
        P("fsdp"),
        P("fsdp", None),
        P("fsdp"),
        P("fsdp"),
        P("fsdp", None),
        P("fsdp"),
        P("fsdp"),
        P("fsdp"),
        P("fsdp", None),
        P("fsdp"),
        P("fsdp", None),
        P("fsdp"),
        P("fsdp"),
        P("fsdp"),
    )
    return jax.shard_map(
        functools.partial(local, mesh.shape["fsdp"]),
        mesh=mesh,
        in_specs=in_specs,
        out_specs=out_specs,
        check_vma=False,
    )
```

```python
import functools

import jax
import jax.numpy as jnp
import numpy as np
from jax import lax
from jax.experimental import pallas as pl
from jax.experimental.pallas import tpu as pltpu
from jax.sharding import PartitionSpec as P

D = 768
HEADS = 12
HEAD_DIM = 64
FF = 3072
L = 512
QKV = 3 * D
LANES = 128
BLOCKS = 16
EPSILON = 1e-06
ALL = ("fsdp", "rep")
VECTORS = 13

bf16 = jnp.bfloat16
f32 = jnp.float32

NN = ((1,), (0,))
NT = ((1,), (1,))
TN = ((0,), (0,))


def dot(left, right, dims):
    return lax.dot_general(left, right, (dims, ((), ())), preferred_element_type=f32)


def params():
    return pltpu.CompilerParams(vmem_limit_bytes=60 << 20)


def shaped(shape, dtype):
    return jax.ShapeDtypeStruct(shape, dtype)


def rows(size, width, shift=0):
    return pl.BlockSpec((size, width), lambda i: (i + shift, 0))


def whole(shape):
    return pl.BlockSpec(shape, lambda i: (0,) * len(shape), pipeline_mode=pl.Buffered(1))


SMEM = pl.BlockSpec(memory_space=pltpu.SMEM)
ANY = pl.BlockSpec(memory_space=pl.ANY)


def fetch_copies(table, pieces, target, sems, height, source_column, width):
    core = table[64]
    copies = []
    for half in range(2):
        place = core if half == 0 else 1 - core
        column = pl.multiple_of(place * width, LANES)
        for block in range(BLOCKS):
            owner = table[16 * half + block]
            source = pieces[2 * half + block // 8]
            copies.append(
                pltpu.make_async_copy(
                    source.at[pl.ds(block % 8 * height, height), pl.ds(source_column, width)],
                    target.at[pl.ds(pl.multiple_of(owner * height, 16), height), pl.ds(column, width)],
                    sems.at[16 * half + block],
                )
            )
    return copies


def spread_copies(table, staged, keep, send, sems, height, target_column, width):
    core = table[64]
    copies = []
    for half, target in ((0, keep), (1, send)):
        place = core if half == 0 else 1 - core
        column = pl.multiple_of(place * width, LANES)
        for block in range(BLOCKS):
            owner = table[32 + 16 * half + block]
            copies.append(
                pltpu.make_async_copy(
                    staged.at[pl.ds(pl.multiple_of(owner * height, 16), height), pl.ds(column, width)],
                    target.at[pl.ds(block * height, height), pl.ds(target_column, width)],
                    sems.at[16 * half + block],
                )
            )
    return copies


def start_all(copies):
    for copy in copies:
        copy.start()


def wait_all(copies):
    for copy in copies:
        copy.wait()


def fold(values):
    height, width = values.shape
    return jnp.sum(values.reshape(height // 8, 8, width), axis=0)


def six(column):
    return jnp.concatenate([column] * (D // LANES), axis=1)


def lane_first(height):
    return lax.broadcasted_iota(jnp.int32, (height, LANES), 1) < HEAD_DIM


def normalise(values):
    mean = jnp.mean(values, axis=1, keepdims=True)
    centred = values - mean
    spread = jnp.mean(centred * centred, axis=1, keepdims=True)
    rate = lax.rsqrt(spread + EPSILON)
    return centred * rate, rate


def norm_back(weighted, unit, rate):
    return rate * (
        weighted
        - jnp.mean(weighted, axis=1, keepdims=True)
        - unit * jnp.mean(weighted * unit, axis=1, keepdims=True)
    )


def attend_kernel(table, tokens, mask, *refs):
    pieces = refs[:4]
    x_out, qkv_out, raised_out, inverse_out, context_out, turned_out, vec_out, weight_out = refs[-14:-6]
    weight, columns, vectors, sems, vec_sems, out_sem = refs[-6:]

    @pl.when(pl.program_id(0) == 0)
    def _():
        copies = fetch_copies(table, pieces, weight, sems, D // BLOCKS, 0, QKV // 2)
        height = D // BLOCKS
        for block in range(BLOCKS):
            copies.append(
                pltpu.make_async_copy(
                    pieces[block // 8].at[pl.ds(block % 8 * height, height), pl.ds(QKV // 2, LANES)],
                    columns.at[pl.ds(pl.multiple_of(table[block] * height, 16), height), :],
                    vec_sems.at[block],
                )
            )
        start_all(copies)
        wait_all(copies)
        vectors[...] = columns[...].astype(f32).T[:16]
        vec_out[...] = vectors[...]
        pltpu.make_async_copy(weight, weight_out, out_sem).start()

    @pl.when(pl.program_id(0) == pl.num_programs(0) - 1)
    def _():
        pltpu.make_async_copy(weight, weight_out, out_sem).wait()

    chosen = six(mask[...]) > 0
    x = jnp.where(chosen, jnp.broadcast_to(vectors[0:1, :].astype(bf16), (L, D)), tokens[...])
    x_out[...] = x
    queries = dot(x, weight[:, :D], NN) + vectors[1:2, :]
    qkv_out[:, :D] = queries.astype(bf16) * jnp.asarray(HEAD_DIM**-0.5, bf16)
    qkv_out[:, D : 2 * D] = dot(x, weight[:, D : 2 * D], NN).astype(bf16)
    qkv_out[:, 2 * D :] = (dot(x, weight[:, 2 * D :], NN) + vectors[2:3, :]).astype(bf16)
    first = lane_first(L)
    scores = {}
    raised = {}

    def score(head):
        low = LANES * (head // 2)
        queries = qkv_out[:, low : low + LANES]
        lanes = first if head % 2 == 0 else ~first
        keys = qkv_out[:, D + low : D + low + LANES]
        scores[head] = dot(keys, jnp.where(lanes, queries, jnp.zeros_like(queries)), NT)

    def raise_scores(head):
        own = scores.pop(head)
        raised[head] = jnp.exp(own - jnp.max(own, axis=0, keepdims=True)).astype(bf16)
        raised_out[head] = raised[head]

    def mix(head, values):
        part = head % 2
        stacked = jnp.concatenate(
            [values[HEAD_DIM * part : HEAD_DIM * (part + 1)], jnp.ones((16, L), bf16)], axis=0
        )
        mixed = dot(stacked, raised.pop(head), NN)
        inverse = 1.0 / mixed[HEAD_DIM : HEAD_DIM + 1]
        inverse_out[head : head + 1, :] = inverse
        turned_out[HEAD_DIM * head : HEAD_DIM * (head + 1), :] = (mixed[:HEAD_DIM] * inverse).astype(bf16)

    score(0)
    score(1)
    for pair in range(HEADS // 2):
        for head in (2 * pair, 2 * pair + 1):
            raise_scores(head)
            if head + 2 < HEADS:
                score(head + 2)
        low = 2 * D + LANES * pair
        values = qkv_out[:, low : low + LANES].T
        mix(2 * pair, values)
        mix(2 * pair + 1, values)
    context_out[...] = turned_out[...].T


def attend(table, tokens, mask, pieces, earlier, start, count, after=()):
    height = tokens.shape[0]
    total = height // L
    passed = list(earlier[:6]) if earlier else []
    return pl.pallas_call(
        attend_kernel,
        name="attend",
        grid=(count,),
        in_specs=[SMEM, rows(L, D, start), rows(L, LANES, start)] + [ANY] * (4 + len(passed) + len(after)),
        out_specs=[
            rows(L, D, start),
            rows(L, QKV, start),
            pl.BlockSpec((None, HEADS, L, L), lambda i: (i + start, 0, 0, 0)),
            pl.BlockSpec((None, 16, L), lambda i: (i + start, 0, 0)),
            rows(L, D, start),
            pl.BlockSpec((None, D, L), lambda i: (i + start, 0, 0)),
            whole((16, D)),
            ANY,
        ],
        out_shape=[
            shaped((height, D), bf16),
            shaped((height, QKV), bf16),
            shaped((total, HEADS, L, L), bf16),
            shaped((total, 16, L), f32),
            shaped((height, D), bf16),
            shaped((total, D, L), bf16),
            shaped((16, D), f32),
            shaped((D, QKV), bf16),
        ],
        scratch_shapes=[
            pltpu.VMEM((D, QKV), bf16),
            pltpu.VMEM((D, LANES), bf16),
            pltpu.VMEM((16, D), f32),
            pltpu.SemaphoreType.DMA((32,)),
            pltpu.SemaphoreType.DMA((16,)),
            pltpu.SemaphoreType.DMA,
        ],
        input_output_aliases={7 + i: i for i in range(len(passed))},
        compiler_params=params(),
        cost_estimate=pl.CostEstimate(
            flops=10 * count * (2 * L * D * QKV + 16 * L * L * D), bytes_accessed=count * 14_000_000, transcendentals=0
        ),
    )(table, tokens, mask, *pieces, *passed, *after)


def expand_kernel(table, context, x, vec, bias, *refs):
    pieces = refs[:4]
    unit_out, rate_out, low_out, active_out, slope_out, out_weight_out, weight_out = refs[-13:-6]
    out_weight, weight, sems, more_sems, out_sem, more_out_sem = refs[-6:]
    step = pl.program_id(0)

    @pl.when(step == 0)
    def _():
        copies = fetch_copies(table, pieces, out_weight, sems, D // BLOCKS, 0, D // 2)
        start_all(copies)
        start_all(fetch_copies(table, pieces, weight, more_sems, D // BLOCKS, D // 2, FF // 2))
        wait_all(copies)

    first_sum = x[...].astype(f32) + (dot(context[...], out_weight[...], NN) + vec[3:4, :])
    unit, rate = normalise(first_sum)
    unit_out[...] = unit
    rate_out[...] = jnp.broadcast_to(rate, rate_out.shape)
    low = (unit * vec[4:5, :] + vec[5:6, :]).astype(bf16)
    low_out[...] = low

    @pl.when(step == 0)
    def _():
        wait_all(fetch_copies(table, pieces, weight, more_sems, D // BLOCKS, D // 2, FF // 2))
        pltpu.make_async_copy(out_weight, out_weight_out, out_sem).start()
        pltpu.make_async_copy(weight, weight_out, more_out_sem).start()

    @pl.when(step == 1)
    def _():
        pltpu.make_async_copy(out_weight, out_weight_out, out_sem).wait()
        pltpu.make_async_copy(weight, weight_out, more_out_sem).wait()

    width = 1024
    for part in range(FF // width):
        span = slice(width * part, width * (part + 1))
        hidden = dot(low, weight[:, span], NN) + bias[0:1, span]
        scaled = hidden * 2.0**-0.5
        share = 0.5 * lax.erf(scaled) + 0.5
        active_out[:, span] = (hidden * share).astype(bf16)
        slope_out[:, span] = (share + scaled * jnp.exp(-(scaled * scaled)) * np.pi**-0.5).astype(bf16)


def expand(table, context, x, vec, bias, pieces, size, after=()):
    height = x.shape[0]
    return pl.pallas_call(
        expand_kernel,
        name="expand",
        grid=(height // size,),
        in_specs=[SMEM, rows(size, D), rows(size, D), whole((16, D)), whole((1, FF))] + [ANY] * (4 + len(after)),
        out_specs=[rows(size, D), rows(size, LANES), rows(size, D), rows(size, FF), rows(size, FF), ANY, ANY],
        out_shape=[
            shaped((height, D), f32),
            shaped((height, LANES), f32),
            shaped((height, D), bf16),
            shaped((height, FF), bf16),
            shaped((height, FF), bf16),
            shaped((D, D), bf16),
            shaped((D, FF), bf16),
        ],
        scratch_shapes=[
            pltpu.VMEM((D, D), bf16),
            pltpu.VMEM((D, FF), bf16),
            pltpu.SemaphoreType.DMA((32,)),
            pltpu.SemaphoreType.DMA((32,)),
            pltpu.SemaphoreType.DMA,
            pltpu.SemaphoreType.DMA,
        ],
        compiler_params=params(),
        cost_estimate=pl.CostEstimate(
            flops=10 * height * 2 * D * (D + FF), bytes_accessed=height * 20_000, transcendentals=0
        ),
    )(table, context, x, vec, bias, *pieces, *after)


def reduce_kernel(table, active, slope, unit_in, low_in, cotangent, mask, vec, *refs):
    pieces = refs[:4]
    outputs, outer_out, hidden_out, sums, bias_sums, keep, send = refs[-13:-6]
    weight, total, expand_total, expand_staged, sems, out_sems = refs[-6:]
    staged = weight
    step = pl.program_id(0)

    @pl.when(step == 0)
    def _():
        copies = fetch_copies(table, pieces, weight, sems, FF // BLOCKS, 0, D // 2)
        start_all(copies)
        sums[...] = jnp.zeros_like(sums)
        bias_sums[...] = jnp.zeros_like(bias_sums)
        total[...] = jnp.zeros_like(total)
        expand_total[...] = jnp.zeros_like(expand_total)
        wait_all(copies)

    height = active.shape[0]
    parts = 2
    share = height // parts
    lows = []
    for part in range(parts):
        span = slice(share * part, share * (part + 1))
        normed = unit_in[span, :] * vec[4:5, :] + vec[5:6, :]
        second = normed + (dot(active[span, :], weight[...], NN) + vec[10:11, :])
        unit, rate = normalise(second)
        outputs[span, :] = (unit * vec[11:12, :] + vec[12:13, :]).astype(bf16)
        upstream = jnp.where(six(mask[span, :]) > 0, cotangent[span, :].astype(f32), 0.0)
        outer = norm_back(upstream * vec[11:12, :], unit, rate)
        outer_out[span, :] = outer
        low = outer.astype(bf16)
        sums[0:8, :] += fold(upstream * unit)
        sums[8:16, :] += fold(upstream)
        sums[16:24, :] += fold(low.astype(f32))
        lows.append(low)
    low = jnp.concatenate(lows, axis=0)
    groups = FF // D
    for group in range(groups):
        units = slice(D * group, D * (group + 1))
        total[units, :] += dot(active[:, units], low, TN)
        for part in range(parts):
            span = slice(share * part, share * (part + 1))
            grad = dot(lows[part], weight[units, :], NT) * slope[span, units].astype(f32)
            grad_low = grad.astype(bf16)
            hidden_out[span, units] = grad_low
            bias_sums[:, units] += fold(grad_low.astype(f32))
        if group:
            before = slice(D * (group - 1), D * group)
            expand_total[:, before] += dot(low_in[...], hidden_out[:, before], TN)
    before = slice(D * (groups - 1), D * groups)
    expand_total[:, before] += dot(low_in[...], hidden_out[:, before], TN)

    @pl.when(step == pl.num_programs(0) - 1)
    def _():
        staged[...] = total[...].astype(bf16)
        expand_staged[...] = expand_total[...].astype(bf16)
        core = table[64]
        height = D // BLOCKS
        copies = spread_copies(table, expand_staged, keep, send, out_sems, height, FF // 2, FF // 2)
        for half, target in ((0, keep), (1, send)):
            column = pl.multiple_of((core if half == 0 else 1 - core) * (D // 2), LANES)
            for block in range(BLOCKS):
                owner = table[32 + 16 * half + block]
                for group in range(groups):
                    row = pl.multiple_of((owner * groups + group) * height, 16)
                    copies.append(
                        pltpu.make_async_copy(
                            staged.at[pl.ds(row, height), pl.ds(column, D // 2)],
                            target.at[pl.ds(block * height, height), pl.ds(D // 2 * group, D // 2)],
                            out_sems.at[32 + (16 * half + block) * groups + group],
                        )
                    )
        start_all(copies)
        wait_all(copies)


def reduce(table, active, slope, unit, low, cotangent, mask, vec, pieces, size, after=()):
    height = active.shape[0]
    return pl.pallas_call(
        reduce_kernel,
        name="reduce",
        grid=(height // size,),
        in_specs=[
            SMEM,
            rows(size, FF),
            rows(size, FF),
            rows(size, D),
            rows(size, D),
            rows(size, D),
            rows(size, LANES),
            whole((16, D)),
        ]
        + [ANY] * (4 + len(after)),
        out_specs=[rows(size, D), rows(size, D), rows(size, FF), whole((24, D)), whole((8, FF)), ANY, ANY],
        out_shape=[
            shaped((height, D), bf16),
            shaped((height, D), f32),
            shaped((height, FF), bf16),
            shaped((24, D), f32),
            shaped((8, FF), f32),
            shaped((D, FF), bf16),
            shaped((D, FF), bf16),
        ],
        scratch_shapes=[
            pltpu.VMEM((FF, D), bf16),
            pltpu.VMEM((FF, D), f32),
            pltpu.VMEM((D, FF), f32),
            pltpu.VMEM((D, FF), bf16),
            pltpu.SemaphoreType.DMA((32,)),
            pltpu.SemaphoreType.DMA((160,)),
        ],
        compiler_params=params(),
        cost_estimate=pl.CostEstimate(
            flops=10 * height * 8 * D * FF, bytes_accessed=height * 30_000, transcendentals=0
        ),
    )(table, active, slope, unit, low, cotangent, mask, vec, *pieces, *after)


def inner_kernel(hidden, outer, unit_in, rate_in, context, mask, vec, out_weight, weight, *refs):
    inner_out, context_out, sums, grad_out, total = refs[-5:]
    step = pl.program_id(0)

    @pl.when(step == 0)
    def _():
        sums[...] = jnp.zeros_like(sums)
        total[...] = jnp.zeros_like(total)

    height = hidden.shape[0]
    parts = 2
    share = height // parts
    spans = [slice(share * part, share * (part + 1)) for part in range(parts)]
    raw = {0: dot(hidden[spans[0], :], weight[...], NT)}
    for part in range(parts):
        span = spans[part]
        if part + 1 < parts:
            raw[part + 1] = dot(hidden[spans[part + 1], :], weight[...], NT)
        grad_normed = outer[span, :] + raw[part]
        unit = unit_in[span, :]
        sums[0:8, :] += fold(grad_normed * unit)
        sums[8:16, :] += fold(grad_normed)
        inner = norm_back(grad_normed * vec[4:5, :], unit, six(rate_in[span, :]))
        inner_out[span, :] = inner
        branch = inner.astype(bf16)
        sums[16:24, :] += fold(branch.astype(f32))
        sums[24:32, :] += fold(jnp.where(six(mask[span, :]) > 0, inner, 0.0))
        context_out[span, :] = dot(branch, out_weight[...], NT).astype(bf16)
        total[...] += dot(context[span, :], branch, TN)

    @pl.when(step == pl.num_programs(0) - 1)
    def _():
        grad_out[...] = total[...].astype(bf16)


def inner_pass(hidden, outer, unit, rate, context, mask, vec, weights, size, after=()):
    height = hidden.shape[0]
    return pl.pallas_call(
        inner_kernel,
        name="inner",
        grid=(height // size,),
        in_specs=[
            rows(size, FF),
            rows(size, D),
            rows(size, D),
            rows(size, LANES),
            rows(size, D),
            rows(size, LANES),
            whole((16, D)),
            whole((D, D)),
            whole((D, FF)),
        ]
        + [ANY] * len(after),
        out_specs=[rows(size, D), rows(size, D), whole((32, D)), whole((D, D))],
        out_shape=[
            shaped((height, D), f32),
            shaped((height, D), bf16),
            shaped((32, D), f32),
            shaped((D, D), bf16),
        ],
        scratch_shapes=[pltpu.VMEM((D, D), f32)],
        compiler_params=params(),
        cost_estimate=pl.CostEstimate(
            flops=10 * height * 2 * D * (2 * D + FF), bytes_accessed=height * 20_000, transcendentals=0
        ),
    )(hidden, outer, unit, rate, context, mask, vec, *weights, *after)


def attend_back_kernel(qkv, raised_in, inverse_in, turned, grad_context, *refs):
    mixed_out, turned_grad = refs[-2:]
    first = lane_first(L)
    blank = jnp.zeros((HEAD_DIM, L), bf16)
    pairs = {}
    padded = {}
    levels = {}
    probs_grads = {}
    score_grads = {}
    value_terms = {}
    key_terms = {}

    def open_head(head):
        pair, part = divmod(head, 2)
        low = LANES * pair
        if part == 0:
            pairs[pair] = (grad_context[:, low : low + LANES].T.astype(f32), qkv[:, D + low : D + low + LANES].T)
        grads = pairs[pair][0]
        grad = grads[HEAD_DIM * part : HEAD_DIM * (part + 1)] * inverse_in[head : head + 1, :]
        context = turned[HEAD_DIM * head : HEAD_DIM * (head + 1), :].astype(f32)
        levels[head] = jnp.sum(grad * context, axis=0, keepdims=True)
        grad_low = grad.astype(bf16)
        padded[head] = jnp.concatenate([grad_low, blank] if part == 0 else [blank, grad_low], axis=0)
        probs_grads[head] = dot(qkv[:, 2 * D + low : 2 * D + low + LANES], padded[head], NN)

    def scale_head(head):
        score_grads[head] = (raised_in[head].astype(f32) * (probs_grads.pop(head) - levels[head])).astype(bf16)

    def close_head(head):
        pair, part = divmod(head, 2)
        low = LANES * pair
        value_terms[head] = dot(raised_in[head], padded.pop(head), NT)
        queries = qkv[:, low : low + LANES]
        lanes = first if part == 0 else ~first
        grads = score_grads.pop(head)
        key_terms[head] = dot(grads, jnp.where(lanes, queries, jnp.zeros_like(queries)), NN)
        keys = pairs[pair][1][HEAD_DIM * part : HEAD_DIM * (part + 1)]
        turned_grad[HEAD_DIM * head : HEAD_DIM * (head + 1), :] = dot(keys, grads, NN) * HEAD_DIM**-0.5
        if part:
            span = slice(low, low + LANES)
            mixed_out[:, span] = turned_grad[span, :].T.astype(bf16)
            mixed_out[:, D + low : D + low + LANES] = (key_terms.pop(head - 1) + key_terms.pop(head)).astype(bf16)
            mixed_out[:, 2 * D + low : 2 * D + low + LANES] = (
                value_terms.pop(head - 1) + value_terms.pop(head)
            ).astype(bf16)

    open_head(0)
    open_head(1)
    scale_head(0)
    for head in range(HEADS):
        if head + 2 < HEADS:
            open_head(head + 2)
        if head + 1 < HEADS:
            scale_head(head + 1)
        close_head(head)


def attend_back(qkv, raised, inverse, turned, grad_context, after=()):
    height = qkv.shape[0]
    count = height // L
    return pl.pallas_call(
        attend_back_kernel,
        name="attend_back",
        grid=(count,),
        in_specs=[
            rows(L, QKV),
            pl.BlockSpec((None, HEADS, L, L), lambda i: (i, 0, 0, 0)),
            pl.BlockSpec((None, 16, L), lambda i: (i, 0, 0)),
            pl.BlockSpec((None, D, L), lambda i: (i, 0, 0)),
            rows(L, D),
        ]
        + [ANY] * len(after),
        out_specs=rows(L, QKV),
        out_shape=shaped((height, QKV), bf16),
        scratch_shapes=[pltpu.VMEM((D, L), f32)],
        compiler_params=params(),
        cost_estimate=pl.CostEstimate(
            flops=10 * count * 32 * L * L * D, bytes_accessed=count * 14_000_000, transcendentals=0
        ),
    )(qkv, raised, inverse, turned, grad_context, *after)


def heads_kernel(table, x, marks, mixed, second_sums, inner_sums, bias_rows, weight, out_grad, *refs):
    keep, send, total, staged, columns, out_sems, more_out_sems, vec_sems = refs[-8:]
    step = pl.program_id(0)

    @pl.when(step == 0)
    def _():
        total[...] = jnp.zeros_like(total)

    turned = jnp.concatenate([x[...].T, marks[...]], axis=0)
    for piece in range(3):
        span = slice(D * piece, D * (piece + 1))
        total[:, span] += dot(turned, mixed[:, span], NN)

    @pl.when(step == pl.num_programs(0) - 1)
    def _():
        staged[...] = total[:D, :].astype(bf16)
        copies = spread_copies(table, out_grad, keep, send, more_out_sems, D // BLOCKS, QKV // 2 + LANES, D // 2)
        copies += spread_copies(table, staged, keep, send, out_sems, D // BLOCKS, 0, QKV // 2)
        start_all(copies)
        whole_sums = total[D : D + 1, :]
        masked_sums = total[D + 1 : D + 2, :]
        high = masked_sums.astype(bf16)
        low = (masked_sums - high.astype(f32)).astype(bf16)
        split = jnp.concatenate([high, low, jnp.zeros((14, QKV), bf16)], axis=0)
        reached = jnp.sum(dot(split, weight[...], NT), axis=0, keepdims=True)

        def line(ref, group):
            return jnp.sum(ref[8 * group : 8 * (group + 1), :], axis=0, keepdims=True)

        lines = [
            reached + line(inner_sums, 3),
            whole_sums[:, :D],
            whole_sums[:, 2 * D :],
            line(inner_sums, 2),
            line(inner_sums, 0),
            line(inner_sums, 1),
            bias_rows[...],
            line(second_sums, 2),
            line(second_sums, 0),
            line(second_sums, 1),
            jnp.zeros((LANES - VECTORS, D), f32),
        ]
        columns[...] = jnp.concatenate(lines, axis=0).T.astype(bf16)
        height = D // BLOCKS
        more = []
        for half, target in ((0, keep), (1, send)):
            for block in range(BLOCKS):
                owner = table[32 + 16 * half + block]
                more.append(
                    pltpu.make_async_copy(
                        columns.at[pl.ds(pl.multiple_of(owner * height, 16), height), :],
                        target.at[pl.ds(block * height, height), pl.ds(QKV // 2, LANES)],
                        vec_sems.at[16 * half + block],
                    )
                )
        start_all(more)
        wait_all(copies + more)


def heads_grad(table, x, marks, mixed, second_sums, inner_sums, bias_rows, weight, out_grad, size, after=()):
    height = x.shape[0]
    wide = QKV // 2 + LANES + D // 2
    return pl.pallas_call(
        heads_kernel,
        name="heads_grad",
        grid=(height // size,),
        in_specs=[
            SMEM,
            rows(size, D),
            pl.BlockSpec((16, size), lambda i: (0, i)),
            rows(size, QKV),
            whole((24, D)),
            whole((32, D)),
            whole((4, D)),
            whole((D, QKV)),
            whole((D, D)),
        ]
        + [ANY] * len(after),
        out_specs=[ANY, ANY],
        out_shape=[shaped((D, wide), bf16), shaped((D, wide), bf16)],
        scratch_shapes=[
            pltpu.VMEM((D + 16, QKV), f32),
            pltpu.VMEM((D, QKV), bf16),
            pltpu.VMEM((D, LANES), bf16),
            pltpu.SemaphoreType.DMA((32,)),
            pltpu.SemaphoreType.DMA((32,)),
            pltpu.SemaphoreType.DMA((32,)),
        ],
        compiler_params=params(),
        cost_estimate=pl.CostEstimate(flops=10 * height * 2 * D * QKV, bytes_accessed=height * 10_000, transcendentals=0),
    )(table, x, marks, mixed, second_sums, inner_sums, bias_rows, weight, out_grad, *after)


def rows_kernel(mixed, inner, mask, weight, *refs):
    grad = inner[...] + dot(mixed[...], weight[...], NT)
    refs[-1][...] = jnp.where(six(mask[...]) > 0, 0.0, grad).astype(bf16)


def rows_grad(mixed, inner, mask, weight, size, after=()):
    height = mixed.shape[0]
    return pl.pallas_call(
        rows_kernel,
        name="rows_grad",
        grid=(height // size,),
        in_specs=[rows(size, QKV), rows(size, D), rows(size, LANES), whole((D, QKV))] + [ANY] * len(after),
        out_specs=rows(size, D),
        out_shape=shaped((height, D), bf16),
        compiler_params=params(),
        cost_estimate=pl.CostEstimate(
            flops=10 * height * 2 * D * QKV, bytes_accessed=height * 10_000, transcendentals=0
        ),
    )(mixed, inner, mask, weight, *after)


def pile_kernel(*refs):
    height = refs[0].shape[0]
    for index, piece in enumerate(refs[:-1]):
        refs[-1][height * index : height * (index + 1), :] = piece[...]


def pile(pieces):
    height, width = pieces[0].shape
    return pl.pallas_call(
        pile_kernel,
        name="pile",
        out_shape=shaped((height * len(pieces), width), bf16),
        compiler_params=pltpu.CompilerParams(vmem_limit_bytes=16 << 20),
        cost_estimate=pl.CostEstimate(flops=0, bytes_accessed=2_000_000, transcendentals=0),
    )(*pieces)


def around_z(hops):
    return [(i, (i + 8 * hops) % 32) for i in range(32)]


def across(turn):
    return [(i, i ^ (2 if (i & 1) == turn else 4)) for i in range(32)]


def between_cores():
    return [(i, i ^ 1) for i in range(32)]


def make_table():
    table = np.zeros((32, 65), np.int32)
    for device in range(32):
        core, x, y, z = device & 1, (device >> 1) & 1, (device >> 2) & 1, device >> 3
        table[device, 64] = core
        for half in range(2):
            turn = core ^ half
            for block in range(16):
                hops, near, far = block & 3, (block >> 2) & 1, block >> 3
                there_x, there_y = (x ^ near, y ^ far) if turn == 0 else (x ^ far, y ^ near)
                table[device, 16 * half + block] = ((z - hops) % 4) * 4 + there_y * 2 + there_x
                near, far = far, near
                there_x, there_y = (x ^ near, y ^ far) if turn == 0 else (x ^ far, y ^ near)
                table[device, 32 + 16 * half + block] = ((z + hops) % 4) * 4 + there_y * 2 + there_x
    return table


def hop_parts(block):
    return [block] + [lax.ppermute(block, ALL, around_z(hops)) for hops in (1, 2, 3)]


def hop_across(held, turn):
    return lax.ppermute(held, ALL, across(turn))


def hop_core(held):
    return lax.ppermute(held, ALL, between_cores())


def follow(value, earlier):
    return lax.optimization_barrier((value, earlier))[0]


def add_low(*terms):
    total = terms[0].astype(f32)
    for term in terms[1:]:
        total = total + term.astype(f32)
    return total


def add_halves(keep, arrived):
    half = keep.shape[0] // 2
    sent = add_low(keep[half:], arrived[half:]).astype(bf16)
    return add_low(keep[:half], arrived[:half]).astype(bf16), sent


def add_quarters(keep, arrived):
    quarter = keep.shape[0] // 4
    pieces = []
    for hops in range(4):
        span = slice(quarter * hops, quarter * (hops + 1))
        piece = add_low(keep[span], arrived[span])
        pieces.append(piece.astype(bf16) if hops else piece)
    return pieces


def hop_quarters(pieces):
    return [lax.ppermute(pieces[hops], ALL, around_z(hops)) for hops in (1, 2, 3)]


def gather_plain(mine, other):
    pieces = []
    for block in (mine, other):
        full = lax.all_gather(block, "fsdp", axis=0, tiled=True)
        half = full.shape[0] // 2
        pieces += [full[:half], full[half:]]
    return pieces


def scatter_plain(keep, send):
    both = add_low(keep, lax.ppermute(send, "rep", [(0, 1), (1, 0)]))
    return lax.psum_scatter(both, "fsdp", scatter_dimension=0, tiled=True)


def join(core, mine):
    other = lax.ppermute(mine, "rep", [(0, 1), (1, 0)])
    low = jnp.where(core == 0, mine, other)
    high = jnp.where(core == 0, other, mine)
    return jnp.concatenate([low, high], axis=1)


def half_of(weight, place):
    width = weight.shape[1] // 2
    return lax.dynamic_slice_in_dim(weight, place * width, width, axis=1)


def local(
    chips,
    tokens,
    masked,
    cotangent,
    mask_vector,
    heads_weight,
    query_bias,
    value_bias,
    output_weight,
    output_bias,
    first_gain,
    first_shift,
    expand_weight,
    expand_bias,
    reduce_weight,
    reduce_bias,
    second_gain,
    second_shift,
):
    core = lax.axis_index("rep")
    layout = tokens.shape
    height = layout[0] * layout[1] * layout[2]
    share = mask_vector.shape[0]
    by_hops = chips == BLOCKS
    if by_hops:
        table = lax.dynamic_index_in_dim(
            jnp.asarray(make_table()), lax.axis_index("fsdp") * 2 + core, axis=0, keepdims=False
        )
    else:
        table = jnp.concatenate([jnp.tile(jnp.arange(BLOCKS, dtype=jnp.int32), 4), core[None].astype(jnp.int32)])

    vector_rows = jnp.concatenate(
        [
            mask_vector[None],
            query_bias[None],
            value_bias[None],
            output_bias[None],
            first_gain[None],
            first_shift[None],
            *[expand_bias[None, share * group : share * (group + 1)] for group in range(4)],
            reduce_bias[None],
            second_gain[None],
            second_shift[None],
        ],
        axis=0,
    )
    vector_columns = jnp.pad(vector_rows.T, ((0, 0), (0, LANES - VECTORS)))

    def payloads(place):
        return (
            jnp.concatenate([half_of(heads_weight, place), vector_columns], axis=1),
            jnp.concatenate([half_of(output_weight, place), half_of(expand_weight, place)], axis=1),
            half_of(reduce_weight, place),
        )

    flat_tokens = tokens.reshape(height, D)
    flat_cotangent = cotangent.reshape(height, D)
    flags = masked.reshape(height).astype(bf16)
    mask = jnp.broadcast_to(flags[:, None], (height, LANES))
    marks = jnp.concatenate([jnp.ones((1, height), bf16), flags[None], jnp.zeros((14, height), bf16)], axis=0)
    size = 512
    sequences = height // L
    half = sequences // 2

    if by_hops:
        first_load, middle_load, last_load = payloads(core)
        held = pile(hop_parts(first_load))
        middle_parts = hop_parts(follow(middle_load, held))
        near = pile([held, follow(hop_across(held, 0), middle_parts[1])])
        far = hop_across(near, 1)
        middle_held = pile(middle_parts)
        heads = (near, far, hop_core(near), hop_core(follow(far, middle_parts)))
        middle_near = pile([middle_held, hop_across(middle_held, 0)])
        done = attend(table, flat_tokens, mask, heads, None, 0, half, after=(middle_near,))
        vec = done[6]
        last_held = pile(follow(hop_parts(follow(last_load, middle_held)), vec))
        middle_far = hop_across(middle_near, 1)
        middle_near_other = hop_core(middle_near)
        middle_far_other = hop_core(follow(middle_far, vec))
        done = attend(
            table, flat_tokens, mask, heads, done, half, sequences - half, after=(middle_far, middle_near_other, last_held)
        )
        last_near = pile([last_held, hop_across(last_held, 0)])
        middle = (middle_near, middle_far, middle_near_other, middle_far_other)
        after = (last_near,)
    else:
        heads, middle, last = [gather_plain(a, b) for a, b in zip(payloads(core), payloads(1 - core))]
        done = attend(table, flat_tokens, mask, heads, None, 0, sequences)
        vec = done[6]
        after = ()
    x, qkv, raised, inverse, context, turned, _, heads_whole = done
    bias = vec[6:10].reshape(4, D // share, share).transpose(1, 0, 2).reshape(1, FF)
    unit, rate, low, active, slope, *middle_whole = expand(table, context, x, vec, bias, middle, size, after=after)
    if by_hops:
        last_far = hop_across(last_near, 1)
        last = (last_near, last_far, hop_core(last_near), hop_core(follow(last_far, unit)))

    outputs, outer, hidden, second_sums, bias_sums, keep, send = reduce(
        table, active, slope, unit, low, flat_cotangent, mask, vec, last, size
    )
    bias_rows = jnp.sum(bias_sums, axis=0).reshape(D // share, 4, share).transpose(1, 0, 2).reshape(4, D)

    def inner_call(after=()):
        return inner_pass(hidden, outer, unit, rate, context, mask, vec, middle_whole, size, after=after)

    def back_call(after=()):
        return attend_back(qkv, raised, inverse, turned, grad_context, after=after)

    def heads_call(after=()):
        return heads_grad(
            table, x, marks, mixed, second_sums, inner_sums, bias_rows, heads_whole, out_grad, size, after=after
        )

    def rows_call(after=()):
        return rows_grad(mixed, inner, mask, heads_whole, size, after=after)

    if by_hops:
        arrived = hop_core(send)
        inner, grad_context, inner_sums, out_grad = inner_call()
        rest_keep, sent = add_halves(keep, arrived)
        arrived = hop_across(sent, 0)
        mixed = back_call(after=(rest_keep, sent))
        rest_keep, sent = add_halves(rest_keep, arrived)
        arrived = hop_across(sent, 1)
        keep, send = heads_call(after=(rest_keep, sent))
        send = follow(send, arrived)
        rest_pieces = add_quarters(rest_keep, arrived)
        arrived = hop_core(send)
        keep, sent = add_halves(keep, arrived)
        arrived = hop_across(sent, 0)
        grad_tokens = rows_call(after=(sent, *rest_pieces))
        rest_moved = follow(hop_quarters(rest_pieces), grad_tokens)
        keep, sent = add_halves(follow(keep, grad_tokens), arrived)
        arrived = hop_across(sent, 1)
        rest_share = add_low(rest_pieces[0], *rest_moved)
        pieces = add_quarters(keep, arrived)
        heads_share = add_low(pieces[0], *hop_quarters(pieces))
    else:
        rest_share = scatter_plain(keep, send)
        inner, grad_context, inner_sums, out_grad = inner_call()
        mixed = back_call()
        heads_share = scatter_plain(*heads_call())
        grad_tokens = rows_call()

    last_share = jnp.concatenate([rest_share[:, D // 2 * group : D // 2 * (group + 1)] for group in range(4)], axis=0)
    vector_grads = heads_share[:, QKV // 2 : QKV // 2 + LANES]

    def vector(index):
        return vector_grads[:, index]

    return (
        outputs.reshape(layout),
        grad_tokens.reshape(layout),
        vector(0),
        join(core, heads_share[:, : QKV // 2]),
        vector(1),
        vector(2),
        join(core, heads_share[:, QKV // 2 + LANES :]),
        vector(3),
        vector(4),
        vector(5),
        join(core, rest_share[:, FF // 2 :]),
        vector_grads[:, 6:10].T.reshape(-1),
        join(core, last_share),
        vector(10),
        vector(11),
        vector(12),
    )


def solution(mesh):
    in_specs = (
        P(None, ("fsdp", "rep"), None, None),
        P(None, ("fsdp", "rep"), None),
        P(None, ("fsdp", "rep"), None, None),
        P("fsdp"),
        P("fsdp", None),
        P("fsdp"),
        P("fsdp"),
        P("fsdp", None),
        P("fsdp"),
        P("fsdp"),
        P("fsdp"),
        P("fsdp", None),
        P("fsdp"),
        P("fsdp", None),
        P("fsdp"),
        P("fsdp"),
        P("fsdp"),
    )
    out_specs = (
        P(None, ("fsdp", "rep"), None, None),
        P(None, ("fsdp", "rep"), None, None),
        P("fsdp"),
        P("fsdp", None),
        P("fsdp"),
        P("fsdp"),
        P("fsdp", None),
        P("fsdp"),
        P("fsdp"),
        P("fsdp"),
        P("fsdp", None),
        P("fsdp"),
        P("fsdp", None),
        P("fsdp"),
        P("fsdp"),
        P("fsdp"),
    )
    return jax.shard_map(
        functools.partial(local, mesh.shape["fsdp"]),
        mesh=mesh,
        in_specs=in_specs,
        out_specs=out_specs,
        check_vma=False,
    )
```

```python
import functools

import jax
import jax.numpy as jnp
import numpy as np
from jax import lax
from jax.experimental import pallas as pl
from jax.experimental.pallas import tpu as pltpu
from jax.sharding import PartitionSpec as P

D = 768
HEADS = 12
HEAD_DIM = 64
FF = 3072
L = 512
QKV = 3 * D
LANES = 128
BLOCKS = 16
EPSILON = 1e-06
ALL = ("fsdp", "rep")
VECTORS = 13

bf16 = jnp.bfloat16
f32 = jnp.float32

NN = ((1,), (0,))
NT = ((1,), (1,))
TN = ((0,), (0,))


def dot(left, right, dims):
    return lax.dot_general(left, right, (dims, ((), ())), preferred_element_type=f32)


def params(mebibytes=60):
    return pltpu.CompilerParams(vmem_limit_bytes=mebibytes << 20)


def shaped(shape, dtype):
    return jax.ShapeDtypeStruct(shape, dtype)


def rows(size, width, shift=0):
    return pl.BlockSpec((size, width), lambda i: (i + shift, 0))


def whole(shape):
    return pl.BlockSpec(shape, lambda i: (0,) * len(shape), pipeline_mode=pl.Buffered(1))


SMEM = pl.BlockSpec(memory_space=pltpu.SMEM)
ANY = pl.BlockSpec(memory_space=pl.ANY)


def fetch_copies(table, pieces, target, sems, height, source_column, width, base=65):
    core = table[64]
    copies = []
    for half in range(2):
        place = core if half == 0 else 1 - core
        column = pl.multiple_of(place * width, LANES)
        for block in range(BLOCKS):
            owner = table[base + 16 * half + block]
            source = pieces[2 * half + block // 8]
            copies.append(
                pltpu.make_async_copy(
                    source.at[pl.ds(block % 8 * height, height), pl.ds(source_column, width)],
                    target.at[pl.ds(pl.multiple_of(owner * height, 16), height), pl.ds(column, width)],
                    sems.at[16 * half + block],
                )
            )
    return copies


def spread_copies(table, staged, keep, send, sems, height, target_column, width):
    core = table[64]
    copies = []
    for half, target in ((0, keep), (1, send)):
        place = core if half == 0 else 1 - core
        column = pl.multiple_of(place * width, LANES)
        for block in range(BLOCKS):
            owner = table[32 + 16 * half + block]
            copies.append(
                pltpu.make_async_copy(
                    staged.at[pl.ds(pl.multiple_of(owner * height, 16), height), pl.ds(column, width)],
                    target.at[pl.ds(block * height, height), pl.ds(target_column, width)],
                    sems.at[16 * half + block],
                )
            )
    return copies


def start_all(copies):
    for copy in copies:
        copy.start()


def wait_all(copies):
    for copy in copies:
        copy.wait()


def fold(values):
    height, width = values.shape
    return jnp.sum(values.reshape(height // 8, 8, width), axis=0)


def six(column):
    return jnp.concatenate([column] * (D // LANES), axis=1)


def lane_first(height):
    return lax.broadcasted_iota(jnp.int32, (height, LANES), 1) < HEAD_DIM


def normalise(values):
    mean = jnp.mean(values, axis=1, keepdims=True)
    centred = values - mean
    spread = jnp.mean(centred * centred, axis=1, keepdims=True)
    rate = lax.rsqrt(spread + EPSILON)
    return centred * rate, rate


def norm_back(weighted, unit, rate):
    return rate * (
        weighted
        - jnp.mean(weighted, axis=1, keepdims=True)
        - unit * jnp.mean(weighted * unit, axis=1, keepdims=True)
    )


def attend_kernel(start, table, tokens, mask, *refs):
    pieces = refs[:4]
    x_out, qkv_out, raised_out, inverse_out, context_out, turned_out, vec_out, weight_out = refs[-19:-11]
    weight, columns, vectors, x_held, qkv, held, sems, vec_sems, out_sem, row_sems, held_sems = refs[-11:]
    step = pl.program_id(0)
    sequence = step + start
    place = pl.ds(pl.multiple_of(sequence * L, L), L)
    row_copies = [
        pltpu.make_async_copy(x_held, x_out.at[place, :], row_sems.at[0]),
        pltpu.make_async_copy(qkv, qkv_out.at[place, :], row_sems.at[1]),
    ]

    def held_copy(head, index):
        return pltpu.make_async_copy(held.at[head], raised_out.at[index, head], held_sems.at[head])

    @pl.when(step > 0)
    def _():
        wait_all([held_copy(head, sequence - 1) for head in range(HEADS)])

    @pl.when(step == 0)
    def _():
        copies = fetch_copies(table, pieces, weight, sems, D // BLOCKS, 0, QKV // 2, base=0)
        height = D // BLOCKS
        for block in range(BLOCKS):
            copies.append(
                pltpu.make_async_copy(
                    pieces[block // 8].at[pl.ds(block % 8 * height, height), pl.ds(QKV // 2, LANES)],
                    columns.at[pl.ds(pl.multiple_of(table[block] * height, 16), height), :],
                    vec_sems.at[block],
                )
            )
        start_all(copies)
        wait_all(copies)
        vectors[...] = columns[...].astype(f32).T[:16]
        vec_out[...] = vectors[...]
        pltpu.make_async_copy(weight, weight_out, out_sem).start()

    chosen = six(mask[...]) > 0
    x = jnp.where(chosen, jnp.broadcast_to(vectors[0:1, :].astype(bf16), (L, D)), tokens[...])
    x_held[...] = x
    row_copies[0].start()
    queries = dot(x, weight[:, :D], NN) + vectors[1:2, :]
    qkv[:, :D] = queries.astype(bf16) * jnp.asarray(HEAD_DIM**-0.5, bf16)
    qkv[:, D : 2 * D] = dot(x, weight[:, D : 2 * D], NN).astype(bf16)
    qkv[:, 2 * D :] = (dot(x, weight[:, 2 * D :], NN) + vectors[2:3, :]).astype(bf16)
    row_copies[1].start()
    first = lane_first(L)
    scores = {}
    raised = {}

    def score(head):
        low = LANES * (head // 2)
        queries = qkv[:, low : low + LANES]
        lanes = first if head % 2 == 0 else ~first
        keys = qkv[:, D + low : D + low + LANES]
        scores[head] = dot(keys, jnp.where(lanes, queries, jnp.zeros_like(queries)), NT)

    def raise_scores(head):
        own = scores.pop(head)
        raised[head] = jnp.exp(own - jnp.max(own, axis=0, keepdims=True)).astype(bf16)
        held[head] = raised[head]
        held_copy(head, sequence).start()

    def mix(head, values):
        part = head % 2
        stacked = jnp.concatenate(
            [values[HEAD_DIM * part : HEAD_DIM * (part + 1)], jnp.ones((16, L), bf16)], axis=0
        )
        mixed = dot(stacked, raised.pop(head), NN)
        inverse = 1.0 / mixed[HEAD_DIM : HEAD_DIM + 1]
        inverse_out[head : head + 1, :] = inverse
        turned_out[HEAD_DIM * head : HEAD_DIM * (head + 1), :] = (mixed[:HEAD_DIM] * inverse).astype(bf16)

    score(0)
    score(1)
    for pair in range(HEADS // 2):
        for head in (2 * pair, 2 * pair + 1):
            raise_scores(head)
            if head + 2 < HEADS:
                score(head + 2)
        low = 2 * D + LANES * pair
        values = qkv[:, low : low + LANES].T
        mix(2 * pair, values)
        mix(2 * pair + 1, values)
    context_out[...] = turned_out[...].T
    wait_all(row_copies)

    @pl.when(step == pl.num_programs(0) - 1)
    def _():
        pltpu.make_async_copy(weight, weight_out, out_sem).wait()
        wait_all([held_copy(head, sequence) for head in range(HEADS)])


def attend(table, tokens, mask, pieces, earlier, start, count, after=()):
    height = tokens.shape[0]
    total = height // L
    passed = list(earlier[:6]) if earlier else []
    return pl.pallas_call(
        functools.partial(attend_kernel, start),
        name="attend",
        grid=(count,),
        in_specs=[SMEM, rows(L, D, start), rows(L, LANES, start)] + [ANY] * (4 + len(passed) + len(after)),
        out_specs=[
            ANY,
            ANY,
            ANY,
            pl.BlockSpec((None, 16, L), lambda i: (i + start, 0, 0)),
            rows(L, D, start),
            pl.BlockSpec((None, D, L), lambda i: (i + start, 0, 0)),
            whole((16, D)),
            ANY,
        ],
        out_shape=[
            shaped((height, D), bf16),
            shaped((height, QKV), bf16),
            shaped((total, HEADS, L, L), bf16),
            shaped((total, 16, L), f32),
            shaped((height, D), bf16),
            shaped((total, D, L), bf16),
            shaped((16, D), f32),
            shaped((D, QKV), bf16),
        ],
        scratch_shapes=[
            pltpu.VMEM((D, QKV), bf16),
            pltpu.VMEM((D, LANES), bf16),
            pltpu.VMEM((16, D), f32),
            pltpu.VMEM((L, D), bf16),
            pltpu.VMEM((L, QKV), bf16),
            pltpu.VMEM((HEADS, L, L), bf16),
            pltpu.SemaphoreType.DMA((32,)),
            pltpu.SemaphoreType.DMA((16,)),
            pltpu.SemaphoreType.DMA,
            pltpu.SemaphoreType.DMA((2,)),
            pltpu.SemaphoreType.DMA((HEADS,)),
        ],
        input_output_aliases={7 + i: i for i in range(len(passed))},
        compiler_params=params(),
        cost_estimate=pl.CostEstimate(
            flops=10 * count * (2 * L * D * QKV + 16 * L * L * D), bytes_accessed=count * 14_000_000, transcendentals=0
        ),
    )(table, tokens, mask, *pieces, *passed, *after)


def expand_kernel(table, context, x, vec, bias, *refs):
    pieces = refs[:4]
    unit_out, rate_out, low_out, active_out, slope_out, out_weight_out, weight_out = refs[-13:-6]
    out_weight, weight, sems, more_sems, out_sem, more_out_sem = refs[-6:]
    step = pl.program_id(0)

    @pl.when(step == 0)
    def _():
        copies = fetch_copies(table, pieces, out_weight, sems, D // BLOCKS, 0, D // 2)
        start_all(copies)
        start_all(fetch_copies(table, pieces, weight, more_sems, D // BLOCKS, D // 2, FF // 2))
        wait_all(copies)

    first_sum = x[...].astype(f32) + (dot(context[...], out_weight[...], NN) + vec[3:4, :])
    unit, rate = normalise(first_sum)
    unit_out[...] = unit
    rate_out[...] = jnp.broadcast_to(rate, rate_out.shape)
    low = (unit * vec[4:5, :] + vec[5:6, :]).astype(bf16)
    low_out[...] = low

    @pl.when(step == 0)
    def _():
        wait_all(fetch_copies(table, pieces, weight, more_sems, D // BLOCKS, D // 2, FF // 2))
        pltpu.make_async_copy(out_weight, out_weight_out, out_sem).start()
        pltpu.make_async_copy(weight, weight_out, more_out_sem).start()

    @pl.when(step == 1)
    def _():
        pltpu.make_async_copy(out_weight, out_weight_out, out_sem).wait()
        pltpu.make_async_copy(weight, weight_out, more_out_sem).wait()

    width = 1024
    for part in range(FF // width):
        span = slice(width * part, width * (part + 1))
        hidden = dot(low, weight[:, span], NN) + bias[0:1, span]
        scaled = hidden * 2.0**-0.5
        share = 0.5 * lax.erf(scaled) + 0.5
        active_out[:, span] = (hidden * share).astype(bf16)
        slope_out[:, span] = (share + scaled * jnp.exp(-(scaled * scaled)) * np.pi**-0.5).astype(bf16)


def expand(table, context, x, vec, bias, pieces, size, after=()):
    height = x.shape[0]
    return pl.pallas_call(
        expand_kernel,
        name="expand",
        grid=(height // size,),
        in_specs=[SMEM, rows(size, D), rows(size, D), whole((16, D)), whole((1, FF))] + [ANY] * (4 + len(after)),
        out_specs=[rows(size, D), rows(size, LANES), rows(size, D), rows(size, FF), rows(size, FF), ANY, ANY],
        out_shape=[
            shaped((height, D), f32),
            shaped((height, LANES), f32),
            shaped((height, D), bf16),
            shaped((height, FF), bf16),
            shaped((height, FF), bf16),
            shaped((D, D), bf16),
            shaped((D, FF), bf16),
        ],
        scratch_shapes=[
            pltpu.VMEM((D, D), bf16),
            pltpu.VMEM((D, FF), bf16),
            pltpu.SemaphoreType.DMA((32,)),
            pltpu.SemaphoreType.DMA((32,)),
            pltpu.SemaphoreType.DMA,
            pltpu.SemaphoreType.DMA,
        ],
        compiler_params=params(),
        cost_estimate=pl.CostEstimate(
            flops=10 * height * 2 * D * (D + FF), bytes_accessed=height * 20_000, transcendentals=0
        ),
    )(table, context, x, vec, bias, *pieces, *after)


def reduce_kernel(table, active, slope, unit_in, low_in, cotangent, mask, vec, *refs):
    pieces = refs[:4]
    outputs, outer_out, hidden_out, sums, bias_sums, keep, send = refs[-13:-6]
    weight, total, expand_total, expand_staged, sems, out_sems = refs[-6:]
    staged = weight
    step = pl.program_id(0)

    @pl.when(step == 0)
    def _():
        copies = fetch_copies(table, pieces, weight, sems, FF // BLOCKS, 0, D // 2, base=97)
        start_all(copies)
        sums[...] = jnp.zeros_like(sums)
        bias_sums[...] = jnp.zeros_like(bias_sums)
        total[...] = jnp.zeros_like(total)
        expand_total[...] = jnp.zeros_like(expand_total)
        wait_all(copies)

    height = active.shape[0]
    parts = 2
    share = height // parts
    lows = []
    for part in range(parts):
        span = slice(share * part, share * (part + 1))
        normed = unit_in[span, :] * vec[4:5, :] + vec[5:6, :]
        second = normed + (dot(active[span, :], weight[...], NN) + vec[10:11, :])
        unit, rate = normalise(second)
        outputs[span, :] = (unit * vec[11:12, :] + vec[12:13, :]).astype(bf16)
        upstream = jnp.where(six(mask[span, :]) > 0, cotangent[span, :].astype(f32), 0.0)
        outer = norm_back(upstream * vec[11:12, :], unit, rate)
        outer_out[span, :] = outer
        low = outer.astype(bf16)
        sums[0:8, :] += fold(upstream * unit)
        sums[8:16, :] += fold(upstream)
        sums[16:24, :] += fold(low.astype(f32))
        lows.append(low)
    low = jnp.concatenate(lows, axis=0)
    groups = FF // D
    for group in range(groups):
        units = slice(D * group, D * (group + 1))
        total[units, :] += dot(active[:, units], low, TN)
        for part in range(parts):
            span = slice(share * part, share * (part + 1))
            grad = dot(lows[part], weight[units, :], NT) * slope[span, units].astype(f32)
            grad_low = grad.astype(bf16)
            hidden_out[span, units] = grad_low
            bias_sums[:, units] += fold(grad_low.astype(f32))
        if group:
            before = slice(D * (group - 1), D * group)
            expand_total[:, before] += dot(low_in[...], hidden_out[:, before], TN)
    before = slice(D * (groups - 1), D * groups)
    expand_total[:, before] += dot(low_in[...], hidden_out[:, before], TN)

    @pl.when(step == pl.num_programs(0) - 1)
    def _():
        staged[...] = total[...].astype(bf16)
        expand_staged[...] = expand_total[...].astype(bf16)
        core = table[64]
        height = D // BLOCKS
        copies = spread_copies(table, expand_staged, keep, send, out_sems, height, FF // 2, FF // 2)
        for half, target in ((0, keep), (1, send)):
            column = pl.multiple_of((core if half == 0 else 1 - core) * (D // 2), LANES)
            for block in range(BLOCKS):
                owner = table[32 + 16 * half + block]
                for group in range(groups):
                    row = pl.multiple_of((owner * groups + group) * height, 16)
                    copies.append(
                        pltpu.make_async_copy(
                            staged.at[pl.ds(row, height), pl.ds(column, D // 2)],
                            target.at[pl.ds(block * height, height), pl.ds(D // 2 * group, D // 2)],
                            out_sems.at[32 + (16 * half + block) * groups + group],
                        )
                    )
        start_all(copies)
        wait_all(copies)


def reduce(table, active, slope, unit, low, cotangent, mask, vec, pieces, size, after=()):
    height = active.shape[0]
    return pl.pallas_call(
        reduce_kernel,
        name="reduce",
        grid=(height // size,),
        in_specs=[
            SMEM,
            rows(size, FF),
            rows(size, FF),
            rows(size, D),
            rows(size, D),
            rows(size, D),
            rows(size, LANES),
            whole((16, D)),
        ]
        + [ANY] * (4 + len(after)),
        out_specs=[rows(size, D), rows(size, D), rows(size, FF), whole((24, D)), whole((8, FF)), ANY, ANY],
        out_shape=[
            shaped((height, D), bf16),
            shaped((height, D), f32),
            shaped((height, FF), bf16),
            shaped((24, D), f32),
            shaped((8, FF), f32),
            shaped((D, FF), bf16),
            shaped((D, FF), bf16),
        ],
        scratch_shapes=[
            pltpu.VMEM((FF, D), bf16),
            pltpu.VMEM((FF, D), f32),
            pltpu.VMEM((D, FF), f32),
            pltpu.VMEM((D, FF), bf16),
            pltpu.SemaphoreType.DMA((32,)),
            pltpu.SemaphoreType.DMA((160,)),
        ],
        compiler_params=params(),
        cost_estimate=pl.CostEstimate(
            flops=10 * height * 8 * D * FF, bytes_accessed=height * 30_000, transcendentals=0
        ),
    )(table, active, slope, unit, low, cotangent, mask, vec, *pieces, *after)


def inner_kernel(hidden, outer, unit_in, rate_in, mask, vec, out_weight, weight, *refs):
    inner_out, context_out, sums = refs[-3:]

    @pl.when(pl.program_id(0) == 0)
    def _():
        sums[...] = jnp.zeros_like(sums)

    height = hidden.shape[0]
    parts = 2
    share = height // parts
    spans = [slice(share * part, share * (part + 1)) for part in range(parts)]
    raw = {0: dot(hidden[spans[0], :], weight[...], NT)}
    for part in range(parts):
        span = spans[part]
        if part + 1 < parts:
            raw[part + 1] = dot(hidden[spans[part + 1], :], weight[...], NT)
        grad_normed = outer[span, :] + raw[part]
        unit = unit_in[span, :]
        sums[0:8, :] += fold(grad_normed * unit)
        sums[8:16, :] += fold(grad_normed)
        inner = norm_back(grad_normed * vec[4:5, :], unit, six(rate_in[span, :]))
        inner_out[span, :] = inner
        branch = inner.astype(bf16)
        sums[16:24, :] += fold(branch.astype(f32))
        sums[24:32, :] += fold(jnp.where(six(mask[span, :]) > 0, inner, 0.0))
        context_out[span, :] = dot(branch, out_weight[...], NT).astype(bf16)


def inner_pass(hidden, outer, unit, rate, mask, vec, weights, size, after=()):
    height = hidden.shape[0]
    return pl.pallas_call(
        inner_kernel,
        name="inner",
        grid=(height // size,),
        in_specs=[
            rows(size, FF),
            rows(size, D),
            rows(size, D),
            rows(size, LANES),
            rows(size, LANES),
            whole((16, D)),
            whole((D, D)),
            whole((D, FF)),
        ]
        + [ANY] * len(after),
        out_specs=[rows(size, D), rows(size, D), whole((32, D))],
        out_shape=[
            shaped((height, D), f32),
            shaped((height, D), bf16),
            shaped((32, D), f32),
        ],
        compiler_params=params(40),
        cost_estimate=pl.CostEstimate(
            flops=10 * height * 2 * D * (D + FF), bytes_accessed=height * 20_000, transcendentals=0
        ),
    )(hidden, outer, unit, rate, mask, vec, *weights, *after)


def out_kernel(table, context, inner, *refs):
    keep, send, total, staged, out_sems = refs[-5:]
    step = pl.program_id(0)

    @pl.when(step == 0)
    def _():
        total[...] = jnp.zeros_like(total)

    total[...] += dot(context[...], inner[...].astype(bf16), TN)

    @pl.when(step == pl.num_programs(0) - 1)
    def _():
        staged[...] = total[...].astype(bf16)
        copies = spread_copies(table, staged, keep, send, out_sems, D // BLOCKS, 0, D // 2)
        start_all(copies)
        wait_all(copies)


def out_grad(table, context, inner, size, after=()):
    height = context.shape[0]
    return pl.pallas_call(
        out_kernel,
        name="out_grad",
        grid=(height // size,),
        in_specs=[SMEM, rows(size, D), rows(size, D)] + [ANY] * len(after),
        out_specs=[ANY, ANY],
        out_shape=[shaped((D, D // 2), bf16), shaped((D, D // 2), bf16)],
        scratch_shapes=[
            pltpu.VMEM((D, D), f32),
            pltpu.VMEM((D, D), bf16),
            pltpu.SemaphoreType.DMA((32,)),
        ],
        compiler_params=params(24),
        cost_estimate=pl.CostEstimate(
            flops=10 * height * 2 * D * D, bytes_accessed=height * 5_000, transcendentals=0
        ),
    )(table, context, inner, *after)


def attend_back_kernel(qkv, raised_in, inverse_in, turned, grad_context, *refs):
    mixed_out, turned_grad = refs[-2:]
    first = lane_first(L)
    blank = jnp.zeros((HEAD_DIM, L), bf16)
    pairs = {}
    padded = {}
    levels = {}
    probs_grads = {}
    score_grads = {}
    value_terms = {}
    key_terms = {}

    def open_head(head):
        pair, part = divmod(head, 2)
        low = LANES * pair
        if part == 0:
            pairs[pair] = (grad_context[:, low : low + LANES].T.astype(f32), qkv[:, D + low : D + low + LANES].T)
        grads = pairs[pair][0]
        grad = grads[HEAD_DIM * part : HEAD_DIM * (part + 1)] * inverse_in[head : head + 1, :]
        context = turned[HEAD_DIM * head : HEAD_DIM * (head + 1), :].astype(f32)
        levels[head] = jnp.sum(grad * context, axis=0, keepdims=True)
        grad_low = grad.astype(bf16)
        padded[head] = jnp.concatenate([grad_low, blank] if part == 0 else [blank, grad_low], axis=0)
        probs_grads[head] = dot(qkv[:, 2 * D + low : 2 * D + low + LANES], padded[head], NN)

    def scale_head(head):
        score_grads[head] = (raised_in[head].astype(f32) * (probs_grads.pop(head) - levels[head])).astype(bf16)

    def close_head(head):
        pair, part = divmod(head, 2)
        low = LANES * pair
        value_terms[head] = dot(raised_in[head], padded.pop(head), NT)
        queries = qkv[:, low : low + LANES]
        lanes = first if part == 0 else ~first
        grads = score_grads.pop(head)
        key_terms[head] = dot(grads, jnp.where(lanes, queries, jnp.zeros_like(queries)), NN)
        keys = pairs[pair][1][HEAD_DIM * part : HEAD_DIM * (part + 1)]
        turned_grad[HEAD_DIM * head : HEAD_DIM * (head + 1), :] = dot(keys, grads, NN) * HEAD_DIM**-0.5
        if part:
            span = slice(low, low + LANES)
            mixed_out[:, span] = turned_grad[span, :].T.astype(bf16)
            mixed_out[:, D + low : D + low + LANES] = (key_terms.pop(head - 1) + key_terms.pop(head)).astype(bf16)
            mixed_out[:, 2 * D + low : 2 * D + low + LANES] = (
                value_terms.pop(head - 1) + value_terms.pop(head)
            ).astype(bf16)

    open_head(0)
    open_head(1)
    scale_head(0)
    for head in range(HEADS):
        if head + 2 < HEADS:
            open_head(head + 2)
        if head + 1 < HEADS:
            scale_head(head + 1)
        close_head(head)


def attend_back(qkv, raised, inverse, turned, grad_context, after=()):
    height = qkv.shape[0]
    count = height // L
    return pl.pallas_call(
        attend_back_kernel,
        name="attend_back",
        grid=(count,),
        in_specs=[
            rows(L, QKV),
            pl.BlockSpec((None, HEADS, L, L), lambda i: (i, 0, 0, 0)),
            pl.BlockSpec((None, 16, L), lambda i: (i, 0, 0)),
            pl.BlockSpec((None, D, L), lambda i: (i, 0, 0)),
            rows(L, D),
        ]
        + [ANY] * len(after),
        out_specs=rows(L, QKV),
        out_shape=shaped((height, QKV), bf16),
        scratch_shapes=[pltpu.VMEM((D, L), f32)],
        compiler_params=params(40),
        cost_estimate=pl.CostEstimate(
            flops=10 * count * 32 * L * L * D, bytes_accessed=count * 14_000_000, transcendentals=0
        ),
    )(qkv, raised, inverse, turned, grad_context, *after)


def heads_kernel(table, x, marks, mixed, second_sums, inner_sums, bias_rows, weight, *refs):
    keep, send, total, staged, columns, out_sems, vec_sems = refs[-7:]
    step = pl.program_id(0)

    @pl.when(step == 0)
    def _():
        total[...] = jnp.zeros_like(total)

    turned = jnp.concatenate([x[...].T, marks[...]], axis=0)
    for piece in range(3):
        span = slice(D * piece, D * (piece + 1))
        total[:, span] += dot(turned, mixed[:, span], NN)

    @pl.when(step == pl.num_programs(0) - 1)
    def _():
        staged[...] = total[:D, :].astype(bf16)
        copies = spread_copies(table, staged, keep, send, out_sems, D // BLOCKS, 0, QKV // 2)
        start_all(copies)
        whole_sums = total[D : D + 1, :]
        masked_sums = total[D + 1 : D + 2, :]
        high = masked_sums.astype(bf16)
        low = (masked_sums - high.astype(f32)).astype(bf16)
        split = jnp.concatenate([high, low, jnp.zeros((14, QKV), bf16)], axis=0)
        reached = jnp.sum(dot(split, weight[...], NT), axis=0, keepdims=True)

        def line(ref, group):
            return jnp.sum(ref[8 * group : 8 * (group + 1), :], axis=0, keepdims=True)

        lines = [
            reached + line(inner_sums, 3),
            whole_sums[:, :D],
            whole_sums[:, 2 * D :],
            line(inner_sums, 2),
            line(inner_sums, 0),
            line(inner_sums, 1),
            bias_rows[...],
            line(second_sums, 2),
            line(second_sums, 0),
            line(second_sums, 1),
            jnp.zeros((LANES - VECTORS, D), f32),
        ]
        columns[...] = jnp.concatenate(lines, axis=0).T.astype(bf16)
        height = D // BLOCKS
        more = []
        for half, target in ((0, keep), (1, send)):
            for block in range(BLOCKS):
                owner = table[32 + 16 * half + block]
                more.append(
                    pltpu.make_async_copy(
                        columns.at[pl.ds(pl.multiple_of(owner * height, 16), height), :],
                        target.at[pl.ds(block * height, height), pl.ds(QKV // 2, LANES)],
                        vec_sems.at[16 * half + block],
                    )
                )
        start_all(more)
        wait_all(copies + more)


def heads_grad(table, x, marks, mixed, second_sums, inner_sums, bias_rows, weight, size, after=()):
    height = x.shape[0]
    wide = QKV // 2 + LANES
    return pl.pallas_call(
        heads_kernel,
        name="heads_grad",
        grid=(height // size,),
        in_specs=[
            SMEM,
            rows(size, D),
            pl.BlockSpec((16, size), lambda i: (0, i)),
            rows(size, QKV),
            whole((24, D)),
            whole((32, D)),
            whole((4, D)),
            whole((D, QKV)),
        ]
        + [ANY] * len(after),
        out_specs=[ANY, ANY],
        out_shape=[shaped((D, wide), bf16), shaped((D, wide), bf16)],
        scratch_shapes=[
            pltpu.VMEM((D + 16, QKV), f32),
            pltpu.VMEM((D, QKV), bf16),
            pltpu.VMEM((D, LANES), bf16),
            pltpu.SemaphoreType.DMA((32,)),
            pltpu.SemaphoreType.DMA((32,)),
        ],
        compiler_params=params(36),
        cost_estimate=pl.CostEstimate(flops=10 * height * 2 * D * QKV, bytes_accessed=height * 10_000, transcendentals=0),
    )(table, x, marks, mixed, second_sums, inner_sums, bias_rows, weight, *after)


def rows_kernel(mixed, inner, mask, weight, *refs):
    grad = inner[...] + dot(mixed[...], weight[...], NT)
    refs[-1][...] = jnp.where(six(mask[...]) > 0, 0.0, grad).astype(bf16)


def rows_grad(mixed, inner, mask, weight, size, after=()):
    height = mixed.shape[0]
    return pl.pallas_call(
        rows_kernel,
        name="rows_grad",
        grid=(height // size,),
        in_specs=[rows(size, QKV), rows(size, D), rows(size, LANES), whole((D, QKV))] + [ANY] * len(after),
        out_specs=rows(size, D),
        out_shape=shaped((height, D), bf16),
        compiler_params=params(24),
        cost_estimate=pl.CostEstimate(
            flops=10 * height * 2 * D * QKV, bytes_accessed=height * 10_000, transcendentals=0
        ),
    )(mixed, inner, mask, weight, *after)


def pile_kernel(*refs):
    height = refs[0].shape[0]
    for index, piece in enumerate(refs[:-1]):
        refs[-1][height * index : height * (index + 1), :] = piece[...]


def pile(pieces):
    height, width = pieces[0].shape
    return pl.pallas_call(
        pile_kernel,
        name="pile",
        out_shape=shaped((height * len(pieces), width), bf16),
        compiler_params=pltpu.CompilerParams(vmem_limit_bytes=16 << 20),
        cost_estimate=pl.CostEstimate(flops=0, bytes_accessed=2_000_000, transcendentals=0),
    )(*pieces)


def around_z(hops):
    return [(i, (i + 8 * hops) % 32) for i in range(32)]


def across(turn):
    return [(i, i ^ (2 if (i & 1) == turn else 4)) for i in range(32)]


def along_z(bit):
    return [(i, i ^ (8 * bit)) for i in range(32)]


def between_cores():
    return [(i, i ^ 1) for i in range(32)]


def make_table():
    table = np.zeros((32, 129), np.int32)
    for device in range(32):
        core, x, y, z = device & 1, (device >> 1) & 1, (device >> 2) & 1, device >> 3
        table[device, 64] = core
        for half in range(2):
            turn = core ^ half

            def owner(there_z, first, second):
                there_x, there_y = (x ^ first, y ^ second) if turn == 0 else (x ^ second, y ^ first)
                return there_z * 4 + there_y * 2 + there_x

            for block in range(16):
                hops, middle, high = block & 3, (block >> 2) & 1, block >> 3
                turned = z ^ (0, 2, 1, 3)[hops]
                table[device, 16 * half + block] = owner((z - hops) % 4, middle, high)
                table[device, 32 + 16 * half + block] = owner(turned, high, middle)
                table[device, 65 + 16 * half + block] = owner(turned, middle, high)
                turned = z ^ (0, 2, 1, 3)[block >> 2]
                table[device, 97 + 16 * half + block] = owner(turned, block & 1, (block >> 1) & 1)
    return table


def hop_parts(block):
    return [block] + [lax.ppermute(block, ALL, around_z(hops)) for hops in (1, 2, 3)]


def hop_across(held, turn):
    return lax.ppermute(held, ALL, across(turn))


def hop_core(held):
    return lax.ppermute(held, ALL, between_cores())


def follow(value, earlier):
    return lax.optimization_barrier((value, earlier))[0]


def add_low(*terms):
    total = terms[0].astype(f32)
    for term in terms[1:]:
        total = total + term.astype(f32)
    return total


def add_halves(keep, arrived):
    half = keep.shape[0] // 2
    sent = add_low(keep[half:], arrived[half:]).astype(bf16)
    return add_low(keep[:half], arrived[:half]).astype(bf16), sent


def hop_z(held, bit):
    return lax.ppermute(held, ALL, along_z(bit))


def gather_plain(mine, other):
    pieces = []
    for block in (mine, other):
        full = lax.all_gather(block, "fsdp", axis=0, tiled=True)
        half = full.shape[0] // 2
        pieces += [full[:half], full[half:]]
    return pieces


def scatter_plain(keep, send):
    both = add_low(keep, lax.ppermute(send, "rep", [(0, 1), (1, 0)]))
    return lax.psum_scatter(both, "fsdp", scatter_dimension=0, tiled=True)


def join(core, mine):
    other = lax.ppermute(mine, "rep", [(0, 1), (1, 0)])
    low = jnp.where(core == 0, mine, other)
    high = jnp.where(core == 0, other, mine)
    return jnp.concatenate([low, high], axis=1)


def half_of(weight, place):
    width = weight.shape[1] // 2
    return lax.dynamic_slice_in_dim(weight, place * width, width, axis=1)


def local(
    chips,
    tokens,
    masked,
    cotangent,
    mask_vector,
    heads_weight,
    query_bias,
    value_bias,
    output_weight,
    output_bias,
    first_gain,
    first_shift,
    expand_weight,
    expand_bias,
    reduce_weight,
    reduce_bias,
    second_gain,
    second_shift,
):
    core = lax.axis_index("rep")
    layout = tokens.shape
    height = layout[0] * layout[1] * layout[2]
    share = mask_vector.shape[0]
    by_hops = chips == BLOCKS
    if by_hops:
        table = lax.dynamic_index_in_dim(
            jnp.asarray(make_table()), lax.axis_index("fsdp") * 2 + core, axis=0, keepdims=False
        )
    else:
        table = jnp.tile(jnp.arange(BLOCKS, dtype=jnp.int32), 4)
        table = jnp.concatenate([table, core[None].astype(jnp.int32), table])

    vector_rows = jnp.concatenate(
        [
            mask_vector[None],
            query_bias[None],
            value_bias[None],
            output_bias[None],
            first_gain[None],
            first_shift[None],
            *[expand_bias[None, share * group : share * (group + 1)] for group in range(4)],
            reduce_bias[None],
            second_gain[None],
            second_shift[None],
        ],
        axis=0,
    )
    vector_columns = jnp.pad(vector_rows.T, ((0, 0), (0, LANES - VECTORS)))

    def payloads(place):
        return (
            jnp.concatenate([half_of(heads_weight, place), vector_columns], axis=1),
            jnp.concatenate([half_of(output_weight, place), half_of(expand_weight, place)], axis=1),
            half_of(reduce_weight, place),
        )

    flat_tokens = tokens.reshape(height, D)
    flat_cotangent = cotangent.reshape(height, D)
    flags = masked.reshape(height).astype(bf16)
    mask = jnp.broadcast_to(flags[:, None], (height, LANES))
    marks = jnp.concatenate([jnp.ones((1, height), bf16), flags[None], jnp.zeros((14, height), bf16)], axis=0)
    size = 512
    sequences = height // L
    half = sequences // 2

    if by_hops:
        first_load, middle_load, last_load = payloads(core)
        held = pile(hop_parts(first_load))
        last_held = pile([last_load, hop_across(last_load, 0)])
        last_held = pile([last_held, hop_across(last_held, 1)])
        middle_held = follow(middle_load, held)
        middle_moved = hop_z(middle_held, 2)
        near = pile([held, follow(hop_across(held, 0), (middle_moved, last_held, mask, marks, table))])
        far = hop_across(near, 1)
        middle_held = pile([middle_held, middle_moved])
        middle_moved = hop_z(middle_held, 1)
        heads = (near, far, hop_core(near), hop_core(follow(far, middle_moved)))
        middle_held = pile([middle_held, middle_moved])
        done = attend(table, flat_tokens, mask, heads, None, 0, half)
        middle_near = pile([middle_held, follow(hop_across(follow(middle_held, far), 0), done[6])])
        vec = done[6]
        done = attend(table, flat_tokens, mask, heads, done, half, sequences - half, after=(middle_near,))
        middle_far = hop_across(middle_near, 1)
        last_near = pile([last_held, follow(hop_z(follow(last_held, far), 2), done[6])])
        middle_far_other = hop_core(follow(middle_far, (done[6], last_near)))
        middle = (middle_near, middle_far, hop_core(middle_near), middle_far_other)
        after = (last_near,)
    else:
        heads, middle, last = [gather_plain(a, b) for a, b in zip(payloads(core), payloads(1 - core))]
        done = attend(table, flat_tokens, mask, heads, None, 0, sequences)
        vec = done[6]
        after = ()
    x, qkv, raised, inverse, context, turned, _, heads_whole = done
    bias = vec[6:10].reshape(4, D // share, share).transpose(1, 0, 2).reshape(1, FF)
    unit, rate, low, active, slope, *middle_whole = expand(table, context, x, vec, bias, middle, size, after=after)
    if by_hops:
        last_far = hop_z(last_near, 1)
        last = (last_near, last_far, hop_core(last_near), hop_core(follow(last_far, unit)))

    outputs, outer, hidden, second_sums, bias_sums, keep, send = reduce(
        table, active, slope, unit, low, flat_cotangent, mask, vec, last, size
    )
    bias_rows = jnp.sum(bias_sums, axis=0).reshape(D // share, 4, share).transpose(1, 0, 2).reshape(4, D)

    def inner_call(after=()):
        return inner_pass(hidden, outer, unit, rate, mask, vec, middle_whole, size, after=after)

    def back_call(after=()):
        return attend_back(qkv, raised, inverse, turned, grad_context, after=after)

    def heads_call(after=()):
        return heads_grad(table, x, marks, mixed, second_sums, inner_sums, bias_rows, heads_whole, size, after=after)

    def rows_call(after=()):
        return rows_grad(mixed, inner, mask, heads_whole, size, after=after)

    if by_hops:
        arrived = hop_core(send)
        inner, grad_context, inner_sums = inner_call()
        rest_keep, sent = add_halves(keep, arrived)
        arrived = hop_across(sent, 0)
        mixed = back_call(after=(rest_keep, sent))
        rest_keep, sent = add_halves(rest_keep, arrived)
        rest_arrived = hop_across(sent, 1)
        keep, send = heads_call(after=(rest_keep, sent))
        arrived = hop_core(send)
        rest_keep, rest_sent = add_halves(follow(rest_keep, keep), rest_arrived)
        rest_arrived = hop_z(rest_sent, 1)
        out_keep, out_send = out_grad(table, context, inner, size, after=(keep, rest_keep, rest_sent))
        out_arrived = hop_core(out_send)
        keep, sent = add_halves(keep, follow(arrived, out_keep))
        arrived = hop_across(sent, 0)
        out_keep, out_sent = add_halves(follow(out_keep, sent), out_arrived)
        out_arrived = hop_across(out_sent, 0)
        grad_tokens = rows_call(after=(sent, out_keep, out_sent))
        keep, sent = add_halves(follow(keep, grad_tokens), arrived)
        arrived = hop_across(sent, 1)
        rest_keep, rest_sent = add_halves(follow(rest_keep, sent), rest_arrived)
        rest_arrived = hop_z(rest_sent, 2)
        out_keep, out_sent = add_halves(follow(out_keep, rest_sent), out_arrived)
        out_arrived = hop_across(out_sent, 1)
        keep, sent = add_halves(follow(keep, out_sent), arrived)
        arrived = hop_z(sent, 1)
        rest_share = add_low(follow(rest_keep, sent), rest_arrived)
        out_keep, out_sent = add_halves(follow(out_keep, sent), out_arrived)
        out_arrived = hop_z(out_sent, 1)
        keep, sent = add_halves(keep, arrived)
        arrived = hop_z(sent, 2)
        out_keep, out_sent = add_halves(follow(out_keep, sent), out_arrived)
        out_share = add_low(out_keep, hop_z(out_sent, 2))
        heads_share = add_low(keep, arrived)
    else:
        rest_share = scatter_plain(keep, send)
        inner, grad_context, inner_sums = inner_call()
        out_share = scatter_plain(*out_grad(table, context, inner, size))
        mixed = back_call()
        heads_share = scatter_plain(*heads_call())
        grad_tokens = rows_call()

    last_share = jnp.concatenate([rest_share[:, D // 2 * group : D // 2 * (group + 1)] for group in range(4)], axis=0)
    vector_grads = heads_share[:, QKV // 2 :]

    def vector(index):
        return vector_grads[:, index]

    return (
        outputs.reshape(layout),
        grad_tokens.reshape(layout),
        vector(0),
        join(core, heads_share[:, : QKV // 2]),
        vector(1),
        vector(2),
        join(core, out_share),
        vector(3),
        vector(4),
        vector(5),
        join(core, rest_share[:, FF // 2 :]),
        vector_grads[:, 6:10].T.reshape(-1),
        join(core, last_share),
        vector(10),
        vector(11),
        vector(12),
    )


def solution(mesh):
    in_specs = (
        P(None, ("fsdp", "rep"), None, None),
        P(None, ("fsdp", "rep"), None),
        P(None, ("fsdp", "rep"), None, None),
        P("fsdp"),
        P("fsdp", None),
        P("fsdp"),
        P("fsdp"),
        P("fsdp", None),
        P("fsdp"),
        P("fsdp"),
        P("fsdp"),
        P("fsdp", None),
        P("fsdp"),
        P("fsdp", None),
        P("fsdp"),
        P("fsdp"),
        P("fsdp"),
    )
    out_specs = (
        P(None, ("fsdp", "rep"), None, None),
        P(None, ("fsdp", "rep"), None, None),
        P("fsdp"),
        P("fsdp", None),
        P("fsdp"),
        P("fsdp"),
        P("fsdp", None),
        P("fsdp"),
        P("fsdp"),
        P("fsdp"),
        P("fsdp", None),
        P("fsdp"),
        P("fsdp", None),
        P("fsdp"),
        P("fsdp"),
        P("fsdp"),
    )
    return jax.shard_map(
        functools.partial(local, mesh.shape["fsdp"]),
        mesh=mesh,
        in_specs=in_specs,
        out_specs=out_specs,
        check_vma=False,
    )
```

```python
import functools

import jax
import jax.numpy as jnp
import numpy as np
from jax import lax
from jax.experimental import pallas as pl
from jax.experimental.pallas import tpu as pltpu
from jax.sharding import PartitionSpec as P

D = 768
HEADS = 12
HEAD_DIM = 64
FF = 3072
L = 512
QKV = 3 * D
LANES = 128
BLOCKS = 16
EPSILON = 1e-06
ALL = ("fsdp", "rep")
VECTORS = 13

bf16 = jnp.bfloat16
f32 = jnp.float32

NN = ((1,), (0,))
NT = ((1,), (1,))
TN = ((0,), (0,))


def dot(left, right, dims):
    return lax.dot_general(left, right, (dims, ((), ())), preferred_element_type=f32)


def params(mebibytes=60):
    return pltpu.CompilerParams(vmem_limit_bytes=mebibytes << 20)


def shaped(shape, dtype):
    return jax.ShapeDtypeStruct(shape, dtype)


def rows(size, width, shift=0):
    return pl.BlockSpec((size, width), lambda i: (i + shift, 0))


def whole(shape):
    return pl.BlockSpec(shape, lambda i: (0,) * len(shape), pipeline_mode=pl.Buffered(1))


SMEM = pl.BlockSpec(memory_space=pltpu.SMEM)
ANY = pl.BlockSpec(memory_space=pl.ANY)


def fetch_copies(table, pieces, target, sems, height, source_column, width, base=65):
    core = table[64]
    copies = []
    for half in range(2):
        place = core if half == 0 else 1 - core
        column = pl.multiple_of(place * width, LANES)
        for block in range(BLOCKS):
            owner = table[base + 16 * half + block]
            source = pieces[2 * half + block // 8]
            copies.append(
                pltpu.make_async_copy(
                    source.at[pl.ds(block % 8 * height, height), pl.ds(source_column, width)],
                    target.at[pl.ds(pl.multiple_of(owner * height, 16), height), pl.ds(column, width)],
                    sems.at[16 * half + block],
                )
            )
    return copies


def spread_copies(table, staged, keep, send, sems, height, target_column, width):
    core = table[64]
    copies = []
    for half, target in ((0, keep), (1, send)):
        place = core if half == 0 else 1 - core
        column = pl.multiple_of(place * width, LANES)
        for block in range(BLOCKS):
            owner = table[32 + 16 * half + block]
            copies.append(
                pltpu.make_async_copy(
                    staged.at[pl.ds(pl.multiple_of(owner * height, 16), height), pl.ds(column, width)],
                    target.at[pl.ds(block * height, height), pl.ds(target_column, width)],
                    sems.at[16 * half + block],
                )
            )
    return copies


def start_all(copies):
    for copy in copies:
        copy.start()


def wait_all(copies):
    for copy in copies:
        copy.wait()


def fold(values):
    height, width = values.shape
    return jnp.sum(values.reshape(height // 8, 8, width), axis=0)


def six(column):
    return jnp.concatenate([column] * (D // LANES), axis=1)


def lane_first(height):
    return lax.broadcasted_iota(jnp.int32, (height, LANES), 1) < HEAD_DIM


def normalise(values):
    mean = jnp.mean(values, axis=1, keepdims=True)
    centred = values - mean
    spread = jnp.mean(centred * centred, axis=1, keepdims=True)
    rate = lax.rsqrt(spread + EPSILON)
    return centred * rate, rate


def norm_back(weighted, unit, rate):
    return rate * (
        weighted
        - jnp.mean(weighted, axis=1, keepdims=True)
        - unit * jnp.mean(weighted * unit, axis=1, keepdims=True)
    )


def attend_kernel(start, table, tokens, mask, *refs):
    pieces = refs[:4]
    x_out, qkv_out, raised_out, inverse_out, context_out, turned_out, vec_out, weight_out = refs[-19:-11]
    weight, columns, vectors, x_held, qkv, held, sems, vec_sems, out_sem, row_sems, held_sems = refs[-11:]
    step = pl.program_id(0)
    sequence = step + start
    place = pl.ds(pl.multiple_of(sequence * L, L), L)
    row_copies = [
        pltpu.make_async_copy(x_held, x_out.at[place, :], row_sems.at[0]),
        pltpu.make_async_copy(qkv, qkv_out.at[place, :], row_sems.at[1]),
    ]

    def held_copy(head, index):
        return pltpu.make_async_copy(held.at[head], raised_out.at[index, head], held_sems.at[head])

    @pl.when(step > 0)
    def _():
        wait_all([held_copy(head, sequence - 1) for head in range(HEADS)])

    @pl.when(step == 0)
    def _():
        copies = fetch_copies(table, pieces, weight, sems, D // BLOCKS, 0, QKV // 2, base=0)
        height = D // BLOCKS
        for block in range(BLOCKS):
            copies.append(
                pltpu.make_async_copy(
                    pieces[block // 8].at[pl.ds(block % 8 * height, height), pl.ds(QKV // 2, LANES)],
                    columns.at[pl.ds(pl.multiple_of(table[block] * height, 16), height), :],
                    vec_sems.at[block],
                )
            )
        start_all(copies)
        wait_all(copies)
        vectors[...] = columns[...].astype(f32).T[:16]
        vec_out[...] = vectors[...]
        pltpu.make_async_copy(weight, weight_out, out_sem).start()

    chosen = six(mask[...]) > 0
    x = jnp.where(chosen, jnp.broadcast_to(vectors[0:1, :].astype(bf16), (L, D)), tokens[...])
    x_held[...] = x
    row_copies[0].start()
    queries = dot(x, weight[:, :D], NN) + vectors[1:2, :]
    qkv[:, :D] = queries.astype(bf16) * jnp.asarray(HEAD_DIM**-0.5, bf16)
    qkv[:, D : 2 * D] = dot(x, weight[:, D : 2 * D], NN).astype(bf16)
    qkv[:, 2 * D :] = (dot(x, weight[:, 2 * D :], NN) + vectors[2:3, :]).astype(bf16)
    row_copies[1].start()
    first = lane_first(L)
    scores = {}
    raised = {}

    def score(head):
        low = LANES * (head // 2)
        queries = qkv[:, low : low + LANES]
        lanes = first if head % 2 == 0 else ~first
        keys = qkv[:, D + low : D + low + LANES]
        scores[head] = dot(keys, jnp.where(lanes, queries, jnp.zeros_like(queries)), NT)

    def raise_scores(head):
        own = scores.pop(head)
        raised[head] = jnp.exp(own - jnp.max(own, axis=0, keepdims=True)).astype(bf16)
        held[head] = raised[head]
        held_copy(head, sequence).start()

    def mix(head, values):
        part = head % 2
        stacked = jnp.concatenate(
            [values[HEAD_DIM * part : HEAD_DIM * (part + 1)], jnp.ones((16, L), bf16)], axis=0
        )
        mixed = dot(stacked, raised.pop(head), NN)
        inverse = 1.0 / mixed[HEAD_DIM : HEAD_DIM + 1]
        inverse_out[head : head + 1, :] = inverse
        turned_out[HEAD_DIM * head : HEAD_DIM * (head + 1), :] = (mixed[:HEAD_DIM] * inverse).astype(bf16)

    score(0)
    score(1)
    for pair in range(HEADS // 2):
        for head in (2 * pair, 2 * pair + 1):
            raise_scores(head)
            if head + 2 < HEADS:
                score(head + 2)
        low = 2 * D + LANES * pair
        values = qkv[:, low : low + LANES].T
        mix(2 * pair, values)
        mix(2 * pair + 1, values)
    context_out[...] = turned_out[...].T
    wait_all(row_copies)

    @pl.when(step == pl.num_programs(0) - 1)
    def _():
        pltpu.make_async_copy(weight, weight_out, out_sem).wait()
        wait_all([held_copy(head, sequence) for head in range(HEADS)])


def attend(table, tokens, mask, pieces, earlier, start, count, after=()):
    height = tokens.shape[0]
    total = height // L
    passed = list(earlier[:6]) if earlier else []
    return pl.pallas_call(
        functools.partial(attend_kernel, start),
        name="attend",
        grid=(count,),
        in_specs=[SMEM, rows(L, D, start), rows(L, LANES, start)] + [ANY] * (4 + len(passed) + len(after)),
        out_specs=[
            ANY,
            ANY,
            ANY,
            pl.BlockSpec((None, 16, L), lambda i: (i + start, 0, 0)),
            rows(L, D, start),
            pl.BlockSpec((None, D, L), lambda i: (i + start, 0, 0)),
            whole((16, D)),
            ANY,
        ],
        out_shape=[
            shaped((height, D), bf16),
            shaped((height, QKV), bf16),
            shaped((total, HEADS, L, L), bf16),
            shaped((total, 16, L), f32),
            shaped((height, D), bf16),
            shaped((total, D, L), bf16),
            shaped((16, D), f32),
            shaped((D, QKV), bf16),
        ],
        scratch_shapes=[
            pltpu.VMEM((D, QKV), bf16),
            pltpu.VMEM((D, LANES), bf16),
            pltpu.VMEM((16, D), f32),
            pltpu.VMEM((L, D), bf16),
            pltpu.VMEM((L, QKV), bf16),
            pltpu.VMEM((HEADS, L, L), bf16),
            pltpu.SemaphoreType.DMA((32,)),
            pltpu.SemaphoreType.DMA((16,)),
            pltpu.SemaphoreType.DMA,
            pltpu.SemaphoreType.DMA((2,)),
            pltpu.SemaphoreType.DMA((HEADS,)),
        ],
        input_output_aliases={7 + i: i for i in range(len(passed))},
        compiler_params=params(),
        cost_estimate=pl.CostEstimate(
            flops=10 * count * (2 * L * D * QKV + 16 * L * L * D), bytes_accessed=count * 14_000_000, transcendentals=0
        ),
    )(table, tokens, mask, *pieces, *passed, *after)


def expand_kernel(table, context, x, vec, bias, *refs):
    pieces = refs[:4]
    unit_out, rate_out, low_out, active_out, slope_out, out_weight_out, weight_out = refs[-13:-6]
    out_weight, weight, sems, more_sems, out_sem, more_out_sem = refs[-6:]
    step = pl.program_id(0)

    @pl.when(step == 0)
    def _():
        copies = fetch_copies(table, pieces, out_weight, sems, D // BLOCKS, 0, D // 2)
        start_all(copies)
        start_all(fetch_copies(table, pieces, weight, more_sems, D // BLOCKS, D // 2, FF // 2))
        wait_all(copies)

    first_sum = x[...].astype(f32) + (dot(context[...], out_weight[...], NN) + vec[3:4, :])
    unit, rate = normalise(first_sum)
    unit_out[...] = unit
    rate_out[...] = jnp.broadcast_to(rate, rate_out.shape)
    low = (unit * vec[4:5, :] + vec[5:6, :]).astype(bf16)
    low_out[...] = low

    @pl.when(step == 0)
    def _():
        wait_all(fetch_copies(table, pieces, weight, more_sems, D // BLOCKS, D // 2, FF // 2))
        pltpu.make_async_copy(out_weight, out_weight_out, out_sem).start()
        pltpu.make_async_copy(weight, weight_out, more_out_sem).start()

    @pl.when(step == 1)
    def _():
        pltpu.make_async_copy(out_weight, out_weight_out, out_sem).wait()
        pltpu.make_async_copy(weight, weight_out, more_out_sem).wait()

    width = 1024
    for part in range(FF // width):
        span = slice(width * part, width * (part + 1))
        hidden = dot(low, weight[:, span], NN) + bias[0:1, span]
        scaled = hidden * 2.0**-0.5
        share = 0.5 * lax.erf(scaled) + 0.5
        active_out[:, span] = (hidden * share).astype(bf16)
        slope_out[:, span] = (share + scaled * jnp.exp(-(scaled * scaled)) * np.pi**-0.5).astype(bf16)


def expand(table, context, x, vec, bias, pieces, size, after=()):
    height = x.shape[0]
    return pl.pallas_call(
        expand_kernel,
        name="expand",
        grid=(height // size,),
        in_specs=[SMEM, rows(size, D), rows(size, D), whole((16, D)), whole((1, FF))] + [ANY] * (4 + len(after)),
        out_specs=[rows(size, D), rows(size, LANES), rows(size, D), rows(size, FF), rows(size, FF), ANY, ANY],
        out_shape=[
            shaped((height, D), f32),
            shaped((height, LANES), f32),
            shaped((height, D), bf16),
            shaped((height, FF), bf16),
            shaped((height, FF), bf16),
            shaped((D, D), bf16),
            shaped((D, FF), bf16),
        ],
        scratch_shapes=[
            pltpu.VMEM((D, D), bf16),
            pltpu.VMEM((D, FF), bf16),
            pltpu.SemaphoreType.DMA((32,)),
            pltpu.SemaphoreType.DMA((32,)),
            pltpu.SemaphoreType.DMA,
            pltpu.SemaphoreType.DMA,
        ],
        compiler_params=params(),
        cost_estimate=pl.CostEstimate(
            flops=10 * height * 2 * D * (D + FF), bytes_accessed=height * 20_000, transcendentals=0
        ),
    )(table, context, x, vec, bias, *pieces, *after)


def reduce_kernel(table, active, slope, unit_in, low_in, cotangent, mask, vec, *refs):
    pieces = refs[:4]
    outputs, outer_out, hidden_out, sums, bias_sums, keep, send = refs[-13:-6]
    weight, total, expand_total, expand_staged, sems, out_sems = refs[-6:]
    staged = weight
    step = pl.program_id(0)

    @pl.when(step == 0)
    def _():
        copies = fetch_copies(table, pieces, weight, sems, FF // BLOCKS, 0, D // 2, base=97)
        start_all(copies)
        sums[...] = jnp.zeros_like(sums)
        bias_sums[...] = jnp.zeros_like(bias_sums)
        total[...] = jnp.zeros_like(total)
        expand_total[...] = jnp.zeros_like(expand_total)
        wait_all(copies)

    height = active.shape[0]
    parts = 2
    share = height // parts
    lows = []
    for part in range(parts):
        span = slice(share * part, share * (part + 1))
        normed = unit_in[span, :] * vec[4:5, :] + vec[5:6, :]
        second = normed + (dot(active[span, :], weight[...], NN) + vec[10:11, :])
        unit, rate = normalise(second)
        outputs[span, :] = (unit * vec[11:12, :] + vec[12:13, :]).astype(bf16)
        upstream = jnp.where(six(mask[span, :]) > 0, cotangent[span, :].astype(f32), 0.0)
        outer = norm_back(upstream * vec[11:12, :], unit, rate)
        outer_out[span, :] = outer
        low = outer.astype(bf16)
        sums[0:8, :] += fold(upstream * unit)
        sums[8:16, :] += fold(upstream)
        sums[16:24, :] += fold(low.astype(f32))
        lows.append(low)
    low = jnp.concatenate(lows, axis=0)
    groups = FF // D

    def hidden_grads(group):
        units = slice(D * group, D * (group + 1))
        grad = dot(low, weight[units, :], NT) * slope[:, units].astype(f32)
        grad_low = grad.astype(bf16)
        hidden_out[:, units] = grad_low
        bias_sums[:, units] += fold(grad_low.astype(f32))

    hidden_grads(0)
    for group in range(groups):
        units = slice(D * group, D * (group + 1))
        total[units, :] += dot(active[:, units], low, TN)
        if group + 1 < groups:
            hidden_grads(group + 1)

    def total_copies():
        core = table[64]
        height = D // BLOCKS
        copies = []
        for half, target in ((0, keep), (1, send)):
            column = pl.multiple_of((core if half == 0 else 1 - core) * (D // 2), LANES)
            for block in range(BLOCKS):
                owner = table[32 + 16 * half + block]
                for group in range(groups):
                    row = pl.multiple_of((owner * groups + group) * height, 16)
                    copies.append(
                        pltpu.make_async_copy(
                            staged.at[pl.ds(row, height), pl.ds(column, D // 2)],
                            target.at[pl.ds(block * height, height), pl.ds(D // 2 * group, D // 2)],
                            out_sems.at[32 + (16 * half + block) * groups + group],
                        )
                    )
        return copies

    last = step == pl.num_programs(0) - 1

    @pl.when(last)
    def _():
        staged[...] = total[...].astype(bf16)
        start_all(total_copies())

    low_turned = low_in[...].T
    for group in range(groups):
        units = slice(D * group, D * (group + 1))
        expand_total[:, units] += dot(low_turned, hidden_out[:, units], NN)

    @pl.when(last)
    def _():
        expand_staged[...] = expand_total[...].astype(bf16)
        copies = spread_copies(table, expand_staged, keep, send, out_sems, D // BLOCKS, FF // 2, FF // 2)
        start_all(copies)
        wait_all(total_copies() + copies)


def reduce(table, active, slope, unit, low, cotangent, mask, vec, pieces, size, after=()):
    height = active.shape[0]
    return pl.pallas_call(
        reduce_kernel,
        name="reduce",
        grid=(height // size,),
        in_specs=[
            SMEM,
            rows(size, FF),
            rows(size, FF),
            rows(size, D),
            rows(size, D),
            rows(size, D),
            rows(size, LANES),
            whole((16, D)),
        ]
        + [ANY] * (4 + len(after)),
        out_specs=[rows(size, D), rows(size, D), rows(size, FF), whole((24, D)), whole((8, FF)), ANY, ANY],
        out_shape=[
            shaped((height, D), bf16),
            shaped((height, D), f32),
            shaped((height, FF), bf16),
            shaped((24, D), f32),
            shaped((8, FF), f32),
            shaped((D, FF), bf16),
            shaped((D, FF), bf16),
        ],
        scratch_shapes=[
            pltpu.VMEM((FF, D), bf16),
            pltpu.VMEM((FF, D), f32),
            pltpu.VMEM((D, FF), f32),
            pltpu.VMEM((D, FF), bf16),
            pltpu.SemaphoreType.DMA((32,)),
            pltpu.SemaphoreType.DMA((160,)),
        ],
        compiler_params=params(),
        cost_estimate=pl.CostEstimate(
            flops=10 * height * 8 * D * FF, bytes_accessed=height * 30_000, transcendentals=0
        ),
    )(table, active, slope, unit, low, cotangent, mask, vec, *pieces, *after)


def inner_kernel(hidden, outer, unit_in, rate_in, mask, vec, out_weight, weight, *refs):
    inner_out, context_out, sums = refs[-3:]

    @pl.when(pl.program_id(0) == 0)
    def _():
        sums[...] = jnp.zeros_like(sums)

    height = hidden.shape[0]
    parts = 2
    share = height // parts
    spans = [slice(share * part, share * (part + 1)) for part in range(parts)]
    raw = {0: dot(hidden[spans[0], :], weight[...], NT)}
    for part in range(parts):
        span = spans[part]
        if part + 1 < parts:
            raw[part + 1] = dot(hidden[spans[part + 1], :], weight[...], NT)
        grad_normed = outer[span, :] + raw[part]
        unit = unit_in[span, :]
        sums[0:8, :] += fold(grad_normed * unit)
        sums[8:16, :] += fold(grad_normed)
        inner = norm_back(grad_normed * vec[4:5, :], unit, six(rate_in[span, :]))
        inner_out[span, :] = inner
        branch = inner.astype(bf16)
        sums[16:24, :] += fold(branch.astype(f32))
        sums[24:32, :] += fold(jnp.where(six(mask[span, :]) > 0, inner, 0.0))
        context_out[span, :] = dot(branch, out_weight[...], NT).astype(bf16)


def inner_pass(hidden, outer, unit, rate, mask, vec, weights, size, after=()):
    height = hidden.shape[0]
    return pl.pallas_call(
        inner_kernel,
        name="inner",
        grid=(height // size,),
        in_specs=[
            rows(size, FF),
            rows(size, D),
            rows(size, D),
            rows(size, LANES),
            rows(size, LANES),
            whole((16, D)),
            whole((D, D)),
            whole((D, FF)),
        ]
        + [ANY] * len(after),
        out_specs=[rows(size, D), rows(size, D), whole((32, D))],
        out_shape=[
            shaped((height, D), f32),
            shaped((height, D), bf16),
            shaped((32, D), f32),
        ],
        compiler_params=params(60),
        cost_estimate=pl.CostEstimate(
            flops=10 * height * 2 * D * (D + FF), bytes_accessed=height * 20_000, transcendentals=0
        ),
    )(hidden, outer, unit, rate, mask, vec, *weights, *after)


def out_kernel(table, context, inner, *refs):
    keep, send, total, staged, out_sems = refs[-5:]
    step = pl.program_id(0)

    @pl.when(step == 0)
    def _():
        total[...] = jnp.zeros_like(total)

    total[...] += dot(context[...], inner[...].astype(bf16), TN)

    @pl.when(step == pl.num_programs(0) - 1)
    def _():
        staged[...] = total[...].astype(bf16)
        copies = spread_copies(table, staged, keep, send, out_sems, D // BLOCKS, 0, D // 2)
        start_all(copies)
        wait_all(copies)


def out_grad(table, context, inner, size, after=()):
    height = context.shape[0]
    return pl.pallas_call(
        out_kernel,
        name="out_grad",
        grid=(height // size,),
        in_specs=[SMEM, rows(size, D), rows(size, D)] + [ANY] * len(after),
        out_specs=[ANY, ANY],
        out_shape=[shaped((D, D // 2), bf16), shaped((D, D // 2), bf16)],
        scratch_shapes=[
            pltpu.VMEM((D, D), f32),
            pltpu.VMEM((D, D), bf16),
            pltpu.SemaphoreType.DMA((32,)),
        ],
        compiler_params=params(24),
        cost_estimate=pl.CostEstimate(
            flops=10 * height * 2 * D * D, bytes_accessed=height * 5_000, transcendentals=0
        ),
    )(table, context, inner, *after)


def attend_back_kernel(qkv, raised_in, inverse_in, turned, grad_context, *refs):
    mixed_out, turned_grad = refs[-2:]
    first = lane_first(L)
    blank = jnp.zeros((HEAD_DIM, L), bf16)
    pairs = {}
    padded = {}
    levels = {}
    probs_grads = {}
    score_grads = {}
    value_terms = {}
    key_terms = {}

    def open_head(head):
        pair, part = divmod(head, 2)
        low = LANES * pair
        if part == 0:
            pairs[pair] = (grad_context[:, low : low + LANES].T.astype(f32), qkv[:, D + low : D + low + LANES].T)
        grads = pairs[pair][0]
        grad = grads[HEAD_DIM * part : HEAD_DIM * (part + 1)] * inverse_in[head : head + 1, :]
        context = turned[HEAD_DIM * head : HEAD_DIM * (head + 1), :].astype(f32)
        levels[head] = jnp.sum(grad * context, axis=0, keepdims=True)
        grad_low = grad.astype(bf16)
        padded[head] = jnp.concatenate([grad_low, blank] if part == 0 else [blank, grad_low], axis=0)
        probs_grads[head] = dot(qkv[:, 2 * D + low : 2 * D + low + LANES], padded[head], NN)

    def scale_head(head):
        score_grads[head] = (raised_in[head].astype(f32) * (probs_grads.pop(head) - levels[head])).astype(bf16)

    def close_head(head):
        pair, part = divmod(head, 2)
        low = LANES * pair
        value_terms[head] = dot(raised_in[head], padded.pop(head), NT)
        queries = qkv[:, low : low + LANES]
        lanes = first if part == 0 else ~first
        grads = score_grads.pop(head)
        key_terms[head] = dot(grads, jnp.where(lanes, queries, jnp.zeros_like(queries)), NN)
        keys = pairs[pair][1][HEAD_DIM * part : HEAD_DIM * (part + 1)]
        turned_grad[HEAD_DIM * head : HEAD_DIM * (head + 1), :] = dot(keys, grads, NN) * HEAD_DIM**-0.5
        if part:
            span = slice(low, low + LANES)
            mixed_out[:, span] = turned_grad[span, :].T.astype(bf16)
            mixed_out[:, D + low : D + low + LANES] = (key_terms.pop(head - 1) + key_terms.pop(head)).astype(bf16)
            mixed_out[:, 2 * D + low : 2 * D + low + LANES] = (
                value_terms.pop(head - 1) + value_terms.pop(head)
            ).astype(bf16)

    open_head(0)
    open_head(1)
    scale_head(0)
    for head in range(HEADS):
        if head + 2 < HEADS:
            open_head(head + 2)
        if head + 1 < HEADS:
            scale_head(head + 1)
        close_head(head)


def attend_back(qkv, raised, inverse, turned, grad_context, after=()):
    height = qkv.shape[0]
    count = height // L
    return pl.pallas_call(
        attend_back_kernel,
        name="attend_back",
        grid=(count,),
        in_specs=[
            rows(L, QKV),
            pl.BlockSpec((None, HEADS, L, L), lambda i: (i, 0, 0, 0)),
            pl.BlockSpec((None, 16, L), lambda i: (i, 0, 0)),
            pl.BlockSpec((None, D, L), lambda i: (i, 0, 0)),
            rows(L, D),
        ]
        + [ANY] * len(after),
        out_specs=rows(L, QKV),
        out_shape=shaped((height, QKV), bf16),
        scratch_shapes=[pltpu.VMEM((D, L), f32)],
        compiler_params=params(40),
        cost_estimate=pl.CostEstimate(
            flops=10 * count * 32 * L * L * D, bytes_accessed=count * 14_000_000, transcendentals=0
        ),
    )(qkv, raised, inverse, turned, grad_context, *after)


def heads_kernel(table, x, marks, mixed, second_sums, inner_sums, bias_rows, weight, *refs):
    keep, send, total, staged, columns, out_sems, vec_sems = refs[-7:]
    step = pl.program_id(0)

    @pl.when(step == 0)
    def _():
        total[...] = jnp.zeros_like(total)

    turned = jnp.concatenate([x[...].T, marks[...]], axis=0)
    for piece in range(3):
        span = slice(D * piece, D * (piece + 1))
        total[:, span] += dot(turned, mixed[:, span], NN)

    @pl.when(step == pl.num_programs(0) - 1)
    def _():
        staged[...] = total[:D, :].astype(bf16)
        copies = spread_copies(table, staged, keep, send, out_sems, D // BLOCKS, 0, QKV // 2)
        start_all(copies)
        whole_sums = total[D : D + 1, :]
        masked_sums = total[D + 1 : D + 2, :]
        high = masked_sums.astype(bf16)
        low = (masked_sums - high.astype(f32)).astype(bf16)
        split = jnp.concatenate([high, low, jnp.zeros((14, QKV), bf16)], axis=0)
        reached = jnp.sum(dot(split, weight[...], NT), axis=0, keepdims=True)

        def line(ref, group):
            return jnp.sum(ref[8 * group : 8 * (group + 1), :], axis=0, keepdims=True)

        lines = [
            reached + line(inner_sums, 3),
            whole_sums[:, :D],
            whole_sums[:, 2 * D :],
            line(inner_sums, 2),
            line(inner_sums, 0),
            line(inner_sums, 1),
            bias_rows[...],
            line(second_sums, 2),
            line(second_sums, 0),
            line(second_sums, 1),
            jnp.zeros((LANES - VECTORS, D), f32),
        ]
        columns[...] = jnp.concatenate(lines, axis=0).T.astype(bf16)
        height = D // BLOCKS
        more = []
        for half, target in ((0, keep), (1, send)):
            for block in range(BLOCKS):
                owner = table[32 + 16 * half + block]
                more.append(
                    pltpu.make_async_copy(
                        columns.at[pl.ds(pl.multiple_of(owner * height, 16), height), :],
                        target.at[pl.ds(block * height, height), pl.ds(QKV // 2, LANES)],
                        vec_sems.at[16 * half + block],
                    )
                )
        start_all(more)
        wait_all(copies + more)


def heads_grad(table, x, marks, mixed, second_sums, inner_sums, bias_rows, weight, size, after=()):
    height = x.shape[0]
    wide = QKV // 2 + LANES
    return pl.pallas_call(
        heads_kernel,
        name="heads_grad",
        grid=(height // size,),
        in_specs=[
            SMEM,
            rows(size, D),
            pl.BlockSpec((16, size), lambda i: (0, i)),
            rows(size, QKV),
            whole((24, D)),
            whole((32, D)),
            whole((4, D)),
            whole((D, QKV)),
        ]
        + [ANY] * len(after),
        out_specs=[ANY, ANY],
        out_shape=[shaped((D, wide), bf16), shaped((D, wide), bf16)],
        scratch_shapes=[
            pltpu.VMEM((D + 16, QKV), f32),
            pltpu.VMEM((D, QKV), bf16),
            pltpu.VMEM((D, LANES), bf16),
            pltpu.SemaphoreType.DMA((32,)),
            pltpu.SemaphoreType.DMA((32,)),
        ],
        compiler_params=params(36),
        cost_estimate=pl.CostEstimate(flops=10 * height * 2 * D * QKV, bytes_accessed=height * 10_000, transcendentals=0),
    )(table, x, marks, mixed, second_sums, inner_sums, bias_rows, weight, *after)


def rows_kernel(mixed, inner, mask, weight, *refs):
    grad = inner[...] + dot(mixed[...], weight[...], NT)
    refs[-1][...] = jnp.where(six(mask[...]) > 0, 0.0, grad).astype(bf16)


def rows_grad(mixed, inner, mask, weight, size, after=()):
    height = mixed.shape[0]
    return pl.pallas_call(
        rows_kernel,
        name="rows_grad",
        grid=(height // size,),
        in_specs=[rows(size, QKV), rows(size, D), rows(size, LANES), whole((D, QKV))] + [ANY] * len(after),
        out_specs=rows(size, D),
        out_shape=shaped((height, D), bf16),
        compiler_params=params(24),
        cost_estimate=pl.CostEstimate(
            flops=10 * height * 2 * D * QKV, bytes_accessed=height * 10_000, transcendentals=0
        ),
    )(mixed, inner, mask, weight, *after)


def pile_kernel(*refs):
    height = refs[0].shape[0]
    for index, piece in enumerate(refs[:-1]):
        refs[-1][height * index : height * (index + 1), :] = piece[...]


def pile(pieces):
    height, width = pieces[0].shape
    return pl.pallas_call(
        pile_kernel,
        name="pile",
        out_shape=shaped((height * len(pieces), width), bf16),
        compiler_params=pltpu.CompilerParams(vmem_limit_bytes=16 << 20),
        cost_estimate=pl.CostEstimate(flops=0, bytes_accessed=2_000_000, transcendentals=0),
    )(*pieces)


def around_z(hops):
    return [(i, (i + 8 * hops) % 32) for i in range(32)]


def across(turn):
    return [(i, i ^ (2 if (i & 1) == turn else 4)) for i in range(32)]


def along_z(bit):
    return [(i, i ^ (8 * bit)) for i in range(32)]


def between_cores():
    return [(i, i ^ 1) for i in range(32)]


def make_table():
    table = np.zeros((32, 129), np.int32)
    for device in range(32):
        core, x, y, z = device & 1, (device >> 1) & 1, (device >> 2) & 1, device >> 3
        table[device, 64] = core
        for half in range(2):
            turn = core ^ half

            def owner(there_z, first, second):
                there_x, there_y = (x ^ first, y ^ second) if turn == 0 else (x ^ second, y ^ first)
                return there_z * 4 + there_y * 2 + there_x

            for block in range(16):
                hops, middle, high = block & 3, (block >> 2) & 1, block >> 3
                turned = z ^ (0, 2, 1, 3)[hops]
                table[device, 16 * half + block] = owner((z - hops) % 4, middle, high)
                table[device, 32 + 16 * half + block] = owner(turned, high, middle)
                table[device, 65 + 16 * half + block] = owner(turned, middle, high)
                turned = z ^ (0, 2, 1, 3)[block >> 2]
                table[device, 97 + 16 * half + block] = owner(turned, block & 1, (block >> 1) & 1)
    return table


def hop_parts(block):
    return [block] + [lax.ppermute(block, ALL, around_z(hops)) for hops in (1, 2, 3)]


def hop_across(held, turn):
    return lax.ppermute(held, ALL, across(turn))


def hop_core(held):
    return lax.ppermute(held, ALL, between_cores())


def follow(value, earlier):
    return lax.optimization_barrier((value, earlier))[0]


def add_low(*terms):
    total = terms[0].astype(f32)
    for term in terms[1:]:
        total = total + term.astype(f32)
    return total


def add_halves(keep, arrived):
    half = keep.shape[0] // 2
    sent = add_low(keep[half:], arrived[half:]).astype(bf16)
    return add_low(keep[:half], arrived[:half]).astype(bf16), sent


def hop_z(held, bit):
    return lax.ppermute(held, ALL, along_z(bit))


def gather_plain(mine, other):
    pieces = []
    for block in (mine, other):
        full = lax.all_gather(block, "fsdp", axis=0, tiled=True)
        half = full.shape[0] // 2
        pieces += [full[:half], full[half:]]
    return pieces


def scatter_plain(keep, send):
    both = add_low(keep, lax.ppermute(send, "rep", [(0, 1), (1, 0)]))
    return lax.psum_scatter(both, "fsdp", scatter_dimension=0, tiled=True)


def join(core, mine):
    other = lax.ppermute(mine, "rep", [(0, 1), (1, 0)])
    low = jnp.where(core == 0, mine, other)
    high = jnp.where(core == 0, other, mine)
    return jnp.concatenate([low, high], axis=1)


def half_of(weight, place):
    width = weight.shape[1] // 2
    return lax.dynamic_slice_in_dim(weight, place * width, width, axis=1)


def local(
    chips,
    tokens,
    masked,
    cotangent,
    mask_vector,
    heads_weight,
    query_bias,
    value_bias,
    output_weight,
    output_bias,
    first_gain,
    first_shift,
    expand_weight,
    expand_bias,
    reduce_weight,
    reduce_bias,
    second_gain,
    second_shift,
):
    core = lax.axis_index("rep")
    layout = tokens.shape
    height = layout[0] * layout[1] * layout[2]
    share = mask_vector.shape[0]
    by_hops = chips == BLOCKS
    if by_hops:
        table = lax.dynamic_index_in_dim(
            jnp.asarray(make_table()), lax.axis_index("fsdp") * 2 + core, axis=0, keepdims=False
        )
    else:
        table = jnp.tile(jnp.arange(BLOCKS, dtype=jnp.int32), 4)
        table = jnp.concatenate([table, core[None].astype(jnp.int32), table])

    vector_rows = jnp.concatenate(
        [
            mask_vector[None],
            query_bias[None],
            value_bias[None],
            output_bias[None],
            first_gain[None],
            first_shift[None],
            *[expand_bias[None, share * group : share * (group + 1)] for group in range(4)],
            reduce_bias[None],
            second_gain[None],
            second_shift[None],
        ],
        axis=0,
    )
    vector_columns = jnp.pad(vector_rows.T, ((0, 0), (0, LANES - VECTORS)))

    def payloads(place):
        return (
            jnp.concatenate([half_of(heads_weight, place), vector_columns], axis=1),
            jnp.concatenate([half_of(output_weight, place), half_of(expand_weight, place)], axis=1),
            half_of(reduce_weight, place),
        )

    flat_tokens = tokens.reshape(height, D)
    flat_cotangent = cotangent.reshape(height, D)
    flags = masked.reshape(height).astype(bf16)
    mask = jnp.broadcast_to(flags[:, None], (height, LANES))
    marks = jnp.concatenate([jnp.ones((1, height), bf16), flags[None], jnp.zeros((14, height), bf16)], axis=0)
    size = 512
    sequences = height // L
    half = sequences // 2

    if by_hops:
        first_load, middle_load, last_load = payloads(core)
        held = pile(hop_parts(first_load))
        last_held = pile([last_load, hop_across(last_load, 0)])
        last_held = pile([last_held, hop_across(last_held, 1)])
        middle_held = follow(middle_load, held)
        middle_moved = hop_z(middle_held, 2)
        near = pile([held, follow(hop_across(held, 0), (middle_moved, last_held, mask, marks, table))])
        far = hop_across(near, 1)
        middle_held = pile([middle_held, middle_moved])
        middle_moved = hop_z(middle_held, 1)
        heads = (near, far, hop_core(near), hop_core(follow(far, middle_moved)))
        middle_held = pile([middle_held, middle_moved])
        done = attend(table, flat_tokens, mask, heads, None, 0, half)
        middle_near = pile([middle_held, follow(hop_across(follow(middle_held, far), 0), done[6])])
        vec = done[6]
        done = attend(table, flat_tokens, mask, heads, done, half, sequences - half, after=(middle_near,))
        middle_far = hop_across(middle_near, 1)
        last_near = pile([last_held, follow(hop_z(follow(last_held, far), 2), done[6])])
        middle_far_other = hop_core(follow(middle_far, (done[6], last_near)))
        middle = (middle_near, middle_far, hop_core(middle_near), middle_far_other)
        after = (last_near,)
    else:
        heads, middle, last = [gather_plain(a, b) for a, b in zip(payloads(core), payloads(1 - core))]
        done = attend(table, flat_tokens, mask, heads, None, 0, sequences)
        vec = done[6]
        after = ()
    x, qkv, raised, inverse, context, turned, _, heads_whole = done
    bias = vec[6:10].reshape(4, D // share, share).transpose(1, 0, 2).reshape(1, FF)
    unit, rate, low, active, slope, *middle_whole = expand(table, context, x, vec, bias, middle, size, after=after)
    if by_hops:
        last_far = hop_z(last_near, 1)
        last = (last_near, last_far, hop_core(last_near), hop_core(follow(last_far, unit)))

    outputs, outer, hidden, second_sums, bias_sums, keep, send = reduce(
        table, active, slope, unit, low, flat_cotangent, mask, vec, last, size
    )
    bias_rows = jnp.sum(bias_sums, axis=0).reshape(D // share, 4, share).transpose(1, 0, 2).reshape(4, D)

    def inner_call(after=()):
        return inner_pass(hidden, outer, unit, rate, mask, vec, middle_whole, size, after=after)

    def back_call(after=()):
        return attend_back(qkv, raised, inverse, turned, grad_context, after=after)

    def heads_call(after=()):
        return heads_grad(table, x, marks, mixed, second_sums, inner_sums, bias_rows, heads_whole, size, after=after)

    def rows_call(after=()):
        return rows_grad(mixed, inner, mask, heads_whole, size, after=after)

    if by_hops:
        arrived = hop_core(send)
        inner, grad_context, inner_sums = inner_call()
        rest_keep, sent = add_halves(keep, arrived)
        arrived = hop_across(sent, 0)
        mixed = back_call(after=(rest_keep, sent))
        rest_keep, sent = add_halves(rest_keep, arrived)
        rest_arrived = hop_across(sent, 1)
        keep, send = heads_call(after=(rest_keep, sent))
        arrived = hop_core(send)
        rest_keep, rest_sent = add_halves(follow(rest_keep, keep), rest_arrived)
        rest_arrived = hop_z(rest_sent, 1)
        out_keep, out_send = out_grad(table, context, inner, size, after=(keep, rest_keep, rest_sent))
        out_arrived = hop_core(out_send)
        keep, sent = add_halves(keep, follow(arrived, out_keep))
        arrived = hop_across(sent, 0)
        out_keep, out_sent = add_halves(follow(out_keep, sent), out_arrived)
        out_arrived = hop_across(out_sent, 0)
        grad_tokens = rows_call(after=(sent, out_keep, out_sent))
        keep, sent = add_halves(follow(keep, grad_tokens), arrived)
        arrived = hop_across(sent, 1)
        rest_keep, rest_sent = add_halves(follow(rest_keep, sent), rest_arrived)
        rest_arrived = hop_z(rest_sent, 2)
        out_keep, out_sent = add_halves(follow(out_keep, rest_sent), out_arrived)
        out_arrived = hop_across(out_sent, 1)
        keep, sent = add_halves(follow(keep, out_sent), arrived)
        arrived = hop_z(sent, 1)
        rest_share = add_low(follow(rest_keep, sent), rest_arrived)
        out_keep, out_sent = add_halves(follow(out_keep, sent), out_arrived)
        out_arrived = hop_z(out_sent, 1)
        keep, sent = add_halves(keep, arrived)
        arrived = hop_z(sent, 2)
        out_keep, out_sent = add_halves(follow(out_keep, sent), out_arrived)
        out_share = add_low(out_keep, hop_z(out_sent, 2))
        heads_share = add_low(keep, arrived)
    else:
        rest_share = scatter_plain(keep, send)
        inner, grad_context, inner_sums = inner_call()
        out_share = scatter_plain(*out_grad(table, context, inner, size))
        mixed = back_call()
        heads_share = scatter_plain(*heads_call())
        grad_tokens = rows_call()

    last_share = jnp.concatenate([rest_share[:, D // 2 * group : D // 2 * (group + 1)] for group in range(4)], axis=0)
    vector_grads = heads_share[:, QKV // 2 :]

    def vector(index):
        return vector_grads[:, index]

    return (
        outputs.reshape(layout),
        grad_tokens.reshape(layout),
        vector(0),
        join(core, heads_share[:, : QKV // 2]),
        vector(1),
        vector(2),
        join(core, out_share),
        vector(3),
        vector(4),
        vector(5),
        join(core, rest_share[:, FF // 2 :]),
        vector_grads[:, 6:10].T.reshape(-1),
        join(core, last_share),
        vector(10),
        vector(11),
        vector(12),
    )


def solution(mesh):
    in_specs = (
        P(None, ("fsdp", "rep"), None, None),
        P(None, ("fsdp", "rep"), None),
        P(None, ("fsdp", "rep"), None, None),
        P("fsdp"),
        P("fsdp", None),
        P("fsdp"),
        P("fsdp"),
        P("fsdp", None),
        P("fsdp"),
        P("fsdp"),
        P("fsdp"),
        P("fsdp", None),
        P("fsdp"),
        P("fsdp", None),
        P("fsdp"),
        P("fsdp"),
        P("fsdp"),
    )
    out_specs = (
        P(None, ("fsdp", "rep"), None, None),
        P(None, ("fsdp", "rep"), None, None),
        P("fsdp"),
        P("fsdp", None),
        P("fsdp"),
        P("fsdp"),
        P("fsdp", None),
        P("fsdp"),
        P("fsdp"),
        P("fsdp"),
        P("fsdp", None),
        P("fsdp"),
        P("fsdp", None),
        P("fsdp"),
        P("fsdp"),
        P("fsdp"),
    )
    return jax.shard_map(
        functools.partial(local, mesh.shape["fsdp"]),
        mesh=mesh,
        in_specs=in_specs,
        out_specs=out_specs,
        check_vma=False,
    )
```

```python
import functools

import jax
import jax.numpy as jnp
import numpy as np
from jax import lax
from jax.experimental import pallas as pl
from jax.experimental.pallas import tpu as pltpu
from jax.sharding import PartitionSpec as P

D = 768
HEADS = 12
HEAD_DIM = 64
FF = 3072
L = 512
QKV = 3 * D
LANES = 128
BLOCKS = 16
EPSILON = 1e-06
ALL = ("fsdp", "rep")
VECTORS = 13

bf16 = jnp.bfloat16
f32 = jnp.float32

NN = ((1,), (0,))
NT = ((1,), (1,))
TN = ((0,), (0,))


def dot(left, right, dims):
    return lax.dot_general(left, right, (dims, ((), ())), preferred_element_type=f32)


def params(mebibytes=60):
    return pltpu.CompilerParams(vmem_limit_bytes=mebibytes << 20)


def shaped(shape, dtype):
    return jax.ShapeDtypeStruct(shape, dtype)


def rows(size, width, shift=0):
    return pl.BlockSpec((size, width), lambda i: (i + shift, 0))


def whole(shape):
    return pl.BlockSpec(shape, lambda i: (0,) * len(shape), pipeline_mode=pl.Buffered(1))


SMEM = pl.BlockSpec(memory_space=pltpu.SMEM)
ANY = pl.BlockSpec(memory_space=pl.ANY)


def fetch_copies(table, pieces, target, sems, height, source_column, width, base=65):
    core = table[64]
    copies = []
    for half in range(2):
        place = core if half == 0 else 1 - core
        column = pl.multiple_of(place * width, LANES)
        for block in range(BLOCKS):
            owner = table[base + 16 * half + block]
            source = pieces[2 * half + block // 8]
            copies.append(
                pltpu.make_async_copy(
                    source.at[pl.ds(block % 8 * height, height), pl.ds(source_column, width)],
                    target.at[pl.ds(pl.multiple_of(owner * height, 16), height), pl.ds(column, width)],
                    sems.at[16 * half + block],
                )
            )
    return copies


def spread_copies(table, staged, keep, send, sems, height, target_column, width):
    core = table[64]
    copies = []
    for half, target in ((0, keep), (1, send)):
        place = core if half == 0 else 1 - core
        column = pl.multiple_of(place * width, LANES)
        for block in range(BLOCKS):
            owner = table[32 + 16 * half + block]
            copies.append(
                pltpu.make_async_copy(
                    staged.at[pl.ds(pl.multiple_of(owner * height, 16), height), pl.ds(column, width)],
                    target.at[pl.ds(block * height, height), pl.ds(target_column, width)],
                    sems.at[16 * half + block],
                )
            )
    return copies


def start_all(copies):
    for copy in copies:
        copy.start()


def wait_all(copies):
    for copy in copies:
        copy.wait()


def fold(values):
    height, width = values.shape
    return jnp.sum(values.reshape(height // 8, 8, width), axis=0)


def six(column):
    return jnp.concatenate([column] * (D // LANES), axis=1)


def lane_first(height):
    return lax.broadcasted_iota(jnp.int32, (height, LANES), 1) < HEAD_DIM


def normalise(values):
    mean = jnp.mean(values, axis=1, keepdims=True)
    centred = values - mean
    spread = jnp.mean(centred * centred, axis=1, keepdims=True)
    rate = lax.rsqrt(spread + EPSILON)
    return centred * rate, rate


def norm_back(weighted, unit, rate):
    return rate * (
        weighted
        - jnp.mean(weighted, axis=1, keepdims=True)
        - unit * jnp.mean(weighted * unit, axis=1, keepdims=True)
    )


def attend_kernel(start, table, tokens, mask, *refs):
    pieces = refs[:4]
    x_out, qkv_out, raised_out, inverse_out, context_out, turned_out, vec_out, weight_out = refs[-19:-11]
    weight, columns, vectors, x_held, qkv, held, sems, vec_sems, out_sem, row_sems, held_sems = refs[-11:]
    step = pl.program_id(0)
    sequence = step + start
    place = pl.ds(pl.multiple_of(sequence * L, L), L)
    row_copies = [
        pltpu.make_async_copy(x_held, x_out.at[place, :], row_sems.at[0]),
        pltpu.make_async_copy(qkv, qkv_out.at[place, :], row_sems.at[1]),
    ]

    def held_copy(head, index):
        return pltpu.make_async_copy(held.at[head], raised_out.at[index, head], held_sems.at[head])

    @pl.when(step > 0)
    def _():
        wait_all([held_copy(head, sequence - 1) for head in range(HEADS)])

    @pl.when(step == 0)
    def _():
        copies = fetch_copies(table, pieces, weight, sems, D // BLOCKS, 0, QKV // 2, base=0)
        height = D // BLOCKS
        for block in range(BLOCKS):
            copies.append(
                pltpu.make_async_copy(
                    pieces[block // 8].at[pl.ds(block % 8 * height, height), pl.ds(QKV // 2, LANES)],
                    columns.at[pl.ds(pl.multiple_of(table[block] * height, 16), height), :],
                    vec_sems.at[block],
                )
            )
        start_all(copies)
        wait_all(copies)
        vectors[...] = columns[...].astype(f32).T[:16]
        vec_out[...] = vectors[...]
        pltpu.make_async_copy(weight, weight_out, out_sem).start()

    chosen = six(mask[...]) > 0
    x = jnp.where(chosen, jnp.broadcast_to(vectors[0:1, :].astype(bf16), (L, D)), tokens[...])
    x_held[...] = x
    row_copies[0].start()
    queries = dot(x, weight[:, :D], NN) + vectors[1:2, :]
    qkv[:, :D] = queries.astype(bf16) * jnp.asarray(HEAD_DIM**-0.5, bf16)
    qkv[:, D : 2 * D] = dot(x, weight[:, D : 2 * D], NN).astype(bf16)
    qkv[:, 2 * D :] = (dot(x, weight[:, 2 * D :], NN) + vectors[2:3, :]).astype(bf16)
    row_copies[1].start()
    first = lane_first(L)
    scores = {}
    raised = {}

    def score(head):
        low = LANES * (head // 2)
        queries = qkv[:, low : low + LANES]
        lanes = first if head % 2 == 0 else ~first
        keys = qkv[:, D + low : D + low + LANES]
        scores[head] = dot(keys, jnp.where(lanes, queries, jnp.zeros_like(queries)), NT)

    def raise_scores(head):
        own = scores.pop(head)
        raised[head] = jnp.exp(own - jnp.max(own, axis=0, keepdims=True)).astype(bf16)
        held[head] = raised[head]
        held_copy(head, sequence).start()

    def mix(head, values):
        part = head % 2
        stacked = jnp.concatenate(
            [values[HEAD_DIM * part : HEAD_DIM * (part + 1)], jnp.ones((16, L), bf16)], axis=0
        )
        mixed = dot(stacked, raised.pop(head), NN)
        inverse = 1.0 / mixed[HEAD_DIM : HEAD_DIM + 1]
        inverse_out[head : head + 1, :] = inverse
        turned_out[HEAD_DIM * head : HEAD_DIM * (head + 1), :] = (mixed[:HEAD_DIM] * inverse).astype(bf16)

    score(0)
    score(1)
    for pair in range(HEADS // 2):
        for head in (2 * pair, 2 * pair + 1):
            raise_scores(head)
            if head + 2 < HEADS:
                score(head + 2)
        low = 2 * D + LANES * pair
        values = qkv[:, low : low + LANES].T
        mix(2 * pair, values)
        mix(2 * pair + 1, values)
    context_out[...] = turned_out[...].T
    wait_all(row_copies)

    @pl.when(step == pl.num_programs(0) - 1)
    def _():
        pltpu.make_async_copy(weight, weight_out, out_sem).wait()
        wait_all([held_copy(head, sequence) for head in range(HEADS)])


def attend(table, tokens, mask, pieces, earlier, start, count, after=()):
    height = tokens.shape[0]
    total = height // L
    passed = list(earlier[:6]) if earlier else []
    return pl.pallas_call(
        functools.partial(attend_kernel, start),
        name="attend",
        grid=(count,),
        in_specs=[SMEM, rows(L, D, start), rows(L, LANES, start)] + [ANY] * (4 + len(passed) + len(after)),
        out_specs=[
            ANY,
            ANY,
            ANY,
            pl.BlockSpec((None, 16, L), lambda i: (i + start, 0, 0)),
            rows(L, D, start),
            pl.BlockSpec((None, D, L), lambda i: (i + start, 0, 0)),
            whole((16, D)),
            ANY,
        ],
        out_shape=[
            shaped((height, D), bf16),
            shaped((height, QKV), bf16),
            shaped((total, HEADS, L, L), bf16),
            shaped((total, 16, L), f32),
            shaped((height, D), bf16),
            shaped((total, D, L), bf16),
            shaped((16, D), f32),
            shaped((D, QKV), bf16),
        ],
        scratch_shapes=[
            pltpu.VMEM((D, QKV), bf16),
            pltpu.VMEM((D, LANES), bf16),
            pltpu.VMEM((16, D), f32),
            pltpu.VMEM((L, D), bf16),
            pltpu.VMEM((L, QKV), bf16),
            pltpu.VMEM((HEADS, L, L), bf16),
            pltpu.SemaphoreType.DMA((32,)),
            pltpu.SemaphoreType.DMA((16,)),
            pltpu.SemaphoreType.DMA,
            pltpu.SemaphoreType.DMA((2,)),
            pltpu.SemaphoreType.DMA((HEADS,)),
        ],
        input_output_aliases={7 + i: i for i in range(len(passed))},
        compiler_params=params(),
        cost_estimate=pl.CostEstimate(
            flops=10 * count * (2 * L * D * QKV + 16 * L * L * D), bytes_accessed=count * 14_000_000, transcendentals=0
        ),
    )(table, tokens, mask, *pieces, *passed, *after)


def expand_kernel(table, context, x, vec, bias, *refs):
    pieces = refs[:4]
    unit_out, rate_out, low_out, active_out, slope_out, out_weight_out, weight_out = refs[-13:-6]
    out_weight, weight, sems, more_sems, out_sem, more_out_sem = refs[-6:]
    step = pl.program_id(0)

    @pl.when(step == 0)
    def _():
        copies = fetch_copies(table, pieces, out_weight, sems, D // BLOCKS, 0, D // 2)
        start_all(copies)
        start_all(fetch_copies(table, pieces, weight, more_sems, D // BLOCKS, D // 2, FF // 2))
        wait_all(copies)

    first_sum = x[...].astype(f32) + (dot(context[...], out_weight[...], NN) + vec[3:4, :])
    unit, rate = normalise(first_sum)
    unit_out[...] = unit
    rate_out[...] = jnp.broadcast_to(rate, rate_out.shape)
    low = (unit * vec[4:5, :] + vec[5:6, :]).astype(bf16)
    low_out[...] = low

    @pl.when(step == 0)
    def _():
        wait_all(fetch_copies(table, pieces, weight, more_sems, D // BLOCKS, D // 2, FF // 2))
        pltpu.make_async_copy(out_weight, out_weight_out, out_sem).start()
        pltpu.make_async_copy(weight, weight_out, more_out_sem).start()

    @pl.when(step == 1)
    def _():
        pltpu.make_async_copy(out_weight, out_weight_out, out_sem).wait()
        pltpu.make_async_copy(weight, weight_out, more_out_sem).wait()

    width = 1024
    for part in range(FF // width):
        span = slice(width * part, width * (part + 1))
        hidden = dot(low, weight[:, span], NN) + bias[0:1, span]
        scaled = hidden * 2.0**-0.5
        share = 0.5 * lax.erf(scaled) + 0.5
        active_out[:, span] = (hidden * share).astype(bf16)
        slope_out[:, span] = (share + scaled * jnp.exp2(scaled * scaled * -np.log2(np.e)) * np.pi**-0.5).astype(bf16)


def expand(table, context, x, vec, bias, pieces, size, after=()):
    height = x.shape[0]
    return pl.pallas_call(
        expand_kernel,
        name="expand",
        grid=(height // size,),
        in_specs=[SMEM, rows(size, D), rows(size, D), whole((16, D)), whole((1, FF))] + [ANY] * (4 + len(after)),
        out_specs=[rows(size, D), rows(size, LANES), rows(size, D), rows(size, FF), rows(size, FF), ANY, ANY],
        out_shape=[
            shaped((height, D), f32),
            shaped((height, LANES), f32),
            shaped((height, D), bf16),
            shaped((height, FF), bf16),
            shaped((height, FF), bf16),
            shaped((D, D), bf16),
            shaped((D, FF), bf16),
        ],
        scratch_shapes=[
            pltpu.VMEM((D, D), bf16),
            pltpu.VMEM((D, FF), bf16),
            pltpu.SemaphoreType.DMA((32,)),
            pltpu.SemaphoreType.DMA((32,)),
            pltpu.SemaphoreType.DMA,
            pltpu.SemaphoreType.DMA,
        ],
        compiler_params=params(),
        cost_estimate=pl.CostEstimate(
            flops=10 * height * 2 * D * (D + FF), bytes_accessed=height * 20_000, transcendentals=0
        ),
    )(table, context, x, vec, bias, *pieces, *after)


def reduce_kernel(table, active, slope, unit_in, low_in, cotangent, mask, vec, *refs):
    pieces = refs[:4]
    outputs, outer_out, hidden_out, sums, bias_sums, keep, send = refs[-13:-6]
    weight, total, expand_total, expand_staged, sems, out_sems = refs[-6:]
    staged = weight
    step = pl.program_id(0)

    @pl.when(step == 0)
    def _():
        copies = fetch_copies(table, pieces, weight, sems, FF // BLOCKS, 0, D // 2, base=97)
        start_all(copies)
        sums[...] = jnp.zeros_like(sums)
        bias_sums[...] = jnp.zeros_like(bias_sums)
        total[...] = jnp.zeros_like(total)
        expand_total[...] = jnp.zeros_like(expand_total)
        wait_all(copies)

    height = active.shape[0]
    parts = 2
    share = height // parts
    lows = []
    for part in range(parts):
        span = slice(share * part, share * (part + 1))
        normed = unit_in[span, :] * vec[4:5, :] + vec[5:6, :]
        second = normed + (dot(active[span, :], weight[...], NN) + vec[10:11, :])
        unit, rate = normalise(second)
        outputs[span, :] = (unit * vec[11:12, :] + vec[12:13, :]).astype(bf16)
        upstream = jnp.where(six(mask[span, :]) > 0, cotangent[span, :].astype(f32), 0.0)
        outer = norm_back(upstream * vec[11:12, :], unit, rate)
        outer_out[span, :] = outer
        low = outer.astype(bf16)
        sums[0:8, :] += fold(upstream * unit)
        sums[8:16, :] += fold(upstream)
        sums[16:24, :] += fold(low.astype(f32))
        lows.append(low)
    low = jnp.concatenate(lows, axis=0)
    groups = FF // D

    def hidden_grads(group):
        units = slice(D * group, D * (group + 1))
        grad = dot(low, weight[units, :], NT) * slope[:, units].astype(f32)
        grad_low = grad.astype(bf16)
        hidden_out[:, units] = grad_low
        bias_sums[:, units] += fold(grad_low.astype(f32))

    hidden_grads(0)
    for group in range(groups):
        units = slice(D * group, D * (group + 1))
        total[units, :] += dot(active[:, units], low, TN)
        if group + 1 < groups:
            hidden_grads(group + 1)

    def total_copies():
        core = table[64]
        height = D // BLOCKS
        copies = []
        for half, target in ((0, keep), (1, send)):
            column = pl.multiple_of((core if half == 0 else 1 - core) * (D // 2), LANES)
            for block in range(BLOCKS):
                owner = table[32 + 16 * half + block]
                for group in range(groups):
                    row = pl.multiple_of((owner * groups + group) * height, 16)
                    copies.append(
                        pltpu.make_async_copy(
                            staged.at[pl.ds(row, height), pl.ds(column, D // 2)],
                            target.at[pl.ds(block * height, height), pl.ds(D // 2 * group, D // 2)],
                            out_sems.at[32 + (16 * half + block) * groups + group],
                        )
                    )
        return copies

    last = step == pl.num_programs(0) - 1

    @pl.when(last)
    def _():
        staged[...] = total[...].astype(bf16)
        start_all(total_copies())

    low_turned = low_in[...].T
    for group in range(groups):
        units = slice(D * group, D * (group + 1))
        expand_total[:, units] += dot(low_turned, hidden_out[:, units], NN)

    @pl.when(last)
    def _():
        expand_staged[...] = expand_total[...].astype(bf16)
        copies = spread_copies(table, expand_staged, keep, send, out_sems, D // BLOCKS, FF // 2, FF // 2)
        start_all(copies)
        wait_all(total_copies() + copies)


def reduce(table, active, slope, unit, low, cotangent, mask, vec, pieces, size, after=()):
    height = active.shape[0]
    return pl.pallas_call(
        reduce_kernel,
        name="reduce",
        grid=(height // size,),
        in_specs=[
            SMEM,
            rows(size, FF),
            rows(size, FF),
            rows(size, D),
            rows(size, D),
            rows(size, D),
            rows(size, LANES),
            whole((16, D)),
        ]
        + [ANY] * (4 + len(after)),
        out_specs=[rows(size, D), rows(size, D), rows(size, FF), whole((24, D)), whole((8, FF)), ANY, ANY],
        out_shape=[
            shaped((height, D), bf16),
            shaped((height, D), f32),
            shaped((height, FF), bf16),
            shaped((24, D), f32),
            shaped((8, FF), f32),
            shaped((D, FF), bf16),
            shaped((D, FF), bf16),
        ],
        scratch_shapes=[
            pltpu.VMEM((FF, D), bf16),
            pltpu.VMEM((FF, D), f32),
            pltpu.VMEM((D, FF), f32),
            pltpu.VMEM((D, FF), bf16),
            pltpu.SemaphoreType.DMA((32,)),
            pltpu.SemaphoreType.DMA((160,)),
        ],
        compiler_params=params(),
        cost_estimate=pl.CostEstimate(
            flops=10 * height * 8 * D * FF, bytes_accessed=height * 30_000, transcendentals=0
        ),
    )(table, active, slope, unit, low, cotangent, mask, vec, *pieces, *after)


def inner_kernel(hidden, outer, unit_in, rate_in, mask, vec, out_weight, weight, *refs):
    inner_out, context_out, sums = refs[-3:]

    @pl.when(pl.program_id(0) == 0)
    def _():
        sums[...] = jnp.zeros_like(sums)

    height = hidden.shape[0]
    parts = 2
    share = height // parts
    spans = [slice(share * part, share * (part + 1)) for part in range(parts)]
    raw = {0: dot(hidden[spans[0], :], weight[...], NT)}
    for part in range(parts):
        span = spans[part]
        if part + 1 < parts:
            raw[part + 1] = dot(hidden[spans[part + 1], :], weight[...], NT)
        grad_normed = outer[span, :] + raw[part]
        unit = unit_in[span, :]
        sums[0:8, :] += fold(grad_normed * unit)
        sums[8:16, :] += fold(grad_normed)
        inner = norm_back(grad_normed * vec[4:5, :], unit, six(rate_in[span, :]))
        inner_out[span, :] = inner
        branch = inner.astype(bf16)
        sums[16:24, :] += fold(branch.astype(f32))
        sums[24:32, :] += fold(jnp.where(six(mask[span, :]) > 0, inner, 0.0))
        context_out[span, :] = dot(branch, out_weight[...], NT).astype(bf16)


def inner_pass(hidden, outer, unit, rate, mask, vec, weights, size, after=()):
    height = hidden.shape[0]
    return pl.pallas_call(
        inner_kernel,
        name="inner",
        grid=(height // size,),
        in_specs=[
            rows(size, FF),
            rows(size, D),
            rows(size, D),
            rows(size, LANES),
            rows(size, LANES),
            whole((16, D)),
            whole((D, D)),
            whole((D, FF)),
        ]
        + [ANY] * len(after),
        out_specs=[rows(size, D), rows(size, D), whole((32, D))],
        out_shape=[
            shaped((height, D), f32),
            shaped((height, D), bf16),
            shaped((32, D), f32),
        ],
        compiler_params=params(60),
        cost_estimate=pl.CostEstimate(
            flops=10 * height * 2 * D * (D + FF), bytes_accessed=height * 20_000, transcendentals=0
        ),
    )(hidden, outer, unit, rate, mask, vec, *weights, *after)


def out_kernel(table, context, inner, *refs):
    keep, send, total, staged, out_sems = refs[-5:]
    step = pl.program_id(0)

    @pl.when(step == 0)
    def _():
        total[...] = jnp.zeros_like(total)

    total[...] += dot(context[...], inner[...].astype(bf16), TN)

    @pl.when(step == pl.num_programs(0) - 1)
    def _():
        staged[...] = total[...].astype(bf16)
        copies = spread_copies(table, staged, keep, send, out_sems, D // BLOCKS, 0, D // 2)
        start_all(copies)
        wait_all(copies)


def out_grad(table, context, inner, size, after=()):
    height = context.shape[0]
    return pl.pallas_call(
        out_kernel,
        name="out_grad",
        grid=(height // size,),
        in_specs=[SMEM, rows(size, D), rows(size, D)] + [ANY] * len(after),
        out_specs=[ANY, ANY],
        out_shape=[shaped((D, D // 2), bf16), shaped((D, D // 2), bf16)],
        scratch_shapes=[
            pltpu.VMEM((D, D), f32),
            pltpu.VMEM((D, D), bf16),
            pltpu.SemaphoreType.DMA((32,)),
        ],
        compiler_params=params(24),
        cost_estimate=pl.CostEstimate(
            flops=10 * height * 2 * D * D, bytes_accessed=height * 5_000, transcendentals=0
        ),
    )(table, context, inner, *after)


def attend_back_kernel(qkv, raised_in, inverse_in, turned, grad_context, *refs):
    mixed_out, turned_grad = refs[-2:]
    first = lane_first(L)
    blank = jnp.zeros((HEAD_DIM, L), bf16)
    pairs = {}
    padded = {}
    levels = {}
    probs_grads = {}
    score_grads = {}
    value_terms = {}
    key_terms = {}

    def open_head(head):
        pair, part = divmod(head, 2)
        low = LANES * pair
        if part == 0:
            pairs[pair] = (grad_context[:, low : low + LANES].T.astype(f32), qkv[:, D + low : D + low + LANES].T)
        grads = pairs[pair][0]
        grad = grads[HEAD_DIM * part : HEAD_DIM * (part + 1)] * inverse_in[head : head + 1, :]
        context = turned[HEAD_DIM * head : HEAD_DIM * (head + 1), :].astype(f32)
        levels[head] = jnp.sum(grad * context, axis=0, keepdims=True)
        grad_low = grad.astype(bf16)
        padded[head] = jnp.concatenate([grad_low, blank] if part == 0 else [blank, grad_low], axis=0)
        probs_grads[head] = dot(qkv[:, 2 * D + low : 2 * D + low + LANES], padded[head], NN)

    def scale_head(head):
        score_grads[head] = (raised_in[head].astype(f32) * (probs_grads.pop(head) - levels[head])).astype(bf16)

    def close_head(head):
        pair, part = divmod(head, 2)
        low = LANES * pair
        value_terms[head] = dot(raised_in[head], padded.pop(head), NT)
        queries = qkv[:, low : low + LANES]
        lanes = first if part == 0 else ~first
        grads = score_grads.pop(head)
        key_terms[head] = dot(grads, jnp.where(lanes, queries, jnp.zeros_like(queries)), NN)
        keys = pairs[pair][1][HEAD_DIM * part : HEAD_DIM * (part + 1)]
        turned_grad[HEAD_DIM * head : HEAD_DIM * (head + 1), :] = dot(keys, grads, NN) * HEAD_DIM**-0.5
        if part:
            span = slice(low, low + LANES)
            mixed_out[:, span] = turned_grad[span, :].T.astype(bf16)
            mixed_out[:, D + low : D + low + LANES] = (key_terms.pop(head - 1) + key_terms.pop(head)).astype(bf16)
            mixed_out[:, 2 * D + low : 2 * D + low + LANES] = (
                value_terms.pop(head - 1) + value_terms.pop(head)
            ).astype(bf16)

    open_head(0)
    open_head(1)
    scale_head(0)
    for head in range(HEADS):
        if head + 2 < HEADS:
            open_head(head + 2)
        if head + 1 < HEADS:
            scale_head(head + 1)
        close_head(head)


def attend_back(qkv, raised, inverse, turned, grad_context, after=()):
    height = qkv.shape[0]
    count = height // L
    return pl.pallas_call(
        attend_back_kernel,
        name="attend_back",
        grid=(count,),
        in_specs=[
            rows(L, QKV),
            pl.BlockSpec((None, HEADS, L, L), lambda i: (i, 0, 0, 0)),
            pl.BlockSpec((None, 16, L), lambda i: (i, 0, 0)),
            pl.BlockSpec((None, D, L), lambda i: (i, 0, 0)),
            rows(L, D),
        ]
        + [ANY] * len(after),
        out_specs=rows(L, QKV),
        out_shape=shaped((height, QKV), bf16),
        scratch_shapes=[pltpu.VMEM((D, L), f32)],
        compiler_params=params(40),
        cost_estimate=pl.CostEstimate(
            flops=10 * count * 32 * L * L * D, bytes_accessed=count * 14_000_000, transcendentals=0
        ),
    )(qkv, raised, inverse, turned, grad_context, *after)


def heads_kernel(table, x, marks, mixed, second_sums, inner_sums, bias_rows, weight, *refs):
    keep, send, total, staged, columns, out_sems, vec_sems = refs[-7:]
    step = pl.program_id(0)

    @pl.when(step == 0)
    def _():
        total[...] = jnp.zeros_like(total)

    turned = jnp.concatenate([x[...].T, marks[...]], axis=0)
    for piece in range(3):
        span = slice(D * piece, D * (piece + 1))
        total[:, span] += dot(turned, mixed[:, span], NN)

    @pl.when(step == pl.num_programs(0) - 1)
    def _():
        staged[...] = total[:D, :].astype(bf16)
        copies = spread_copies(table, staged, keep, send, out_sems, D // BLOCKS, 0, QKV // 2)
        start_all(copies)
        whole_sums = total[D : D + 1, :]
        masked_sums = total[D + 1 : D + 2, :]
        high = masked_sums.astype(bf16)
        low = (masked_sums - high.astype(f32)).astype(bf16)
        split = jnp.concatenate([high, low, jnp.zeros((14, QKV), bf16)], axis=0)
        reached = jnp.sum(dot(split, weight[...], NT), axis=0, keepdims=True)

        def line(ref, group):
            return jnp.sum(ref[8 * group : 8 * (group + 1), :], axis=0, keepdims=True)

        lines = [
            reached + line(inner_sums, 3),
            whole_sums[:, :D],
            whole_sums[:, 2 * D :],
            line(inner_sums, 2),
            line(inner_sums, 0),
            line(inner_sums, 1),
            bias_rows[...],
            line(second_sums, 2),
            line(second_sums, 0),
            line(second_sums, 1),
            jnp.zeros((LANES - VECTORS, D), f32),
        ]
        columns[...] = jnp.concatenate(lines, axis=0).T.astype(bf16)
        height = D // BLOCKS
        more = []
        for half, target in ((0, keep), (1, send)):
            for block in range(BLOCKS):
                owner = table[32 + 16 * half + block]
                more.append(
                    pltpu.make_async_copy(
                        columns.at[pl.ds(pl.multiple_of(owner * height, 16), height), :],
                        target.at[pl.ds(block * height, height), pl.ds(QKV // 2, LANES)],
                        vec_sems.at[16 * half + block],
                    )
                )
        start_all(more)
        wait_all(copies + more)


def heads_grad(table, x, marks, mixed, second_sums, inner_sums, bias_rows, weight, size, after=()):
    height = x.shape[0]
    wide = QKV // 2 + LANES
    return pl.pallas_call(
        heads_kernel,
        name="heads_grad",
        grid=(height // size,),
        in_specs=[
            SMEM,
            rows(size, D),
            pl.BlockSpec((16, size), lambda i: (0, i)),
            rows(size, QKV),
            whole((24, D)),
            whole((32, D)),
            whole((4, D)),
            whole((D, QKV)),
        ]
        + [ANY] * len(after),
        out_specs=[ANY, ANY],
        out_shape=[shaped((D, wide), bf16), shaped((D, wide), bf16)],
        scratch_shapes=[
            pltpu.VMEM((D + 16, QKV), f32),
            pltpu.VMEM((D, QKV), bf16),
            pltpu.VMEM((D, LANES), bf16),
            pltpu.SemaphoreType.DMA((32,)),
            pltpu.SemaphoreType.DMA((32,)),
        ],
        compiler_params=params(36),
        cost_estimate=pl.CostEstimate(flops=10 * height * 2 * D * QKV, bytes_accessed=height * 10_000, transcendentals=0),
    )(table, x, marks, mixed, second_sums, inner_sums, bias_rows, weight, *after)


def rows_kernel(mixed, inner, mask, weight, *refs):
    grad = inner[...] + dot(mixed[...], weight[...], NT)
    refs[-1][...] = jnp.where(six(mask[...]) > 0, 0.0, grad).astype(bf16)


def rows_grad(mixed, inner, mask, weight, size, after=()):
    height = mixed.shape[0]
    return pl.pallas_call(
        rows_kernel,
        name="rows_grad",
        grid=(height // size,),
        in_specs=[rows(size, QKV), rows(size, D), rows(size, LANES), whole((D, QKV))] + [ANY] * len(after),
        out_specs=rows(size, D),
        out_shape=shaped((height, D), bf16),
        compiler_params=params(24),
        cost_estimate=pl.CostEstimate(
            flops=10 * height * 2 * D * QKV, bytes_accessed=height * 10_000, transcendentals=0
        ),
    )(mixed, inner, mask, weight, *after)


def pile_kernel(*refs):
    height = refs[0].shape[0]
    for index, piece in enumerate(refs[:-1]):
        refs[-1][height * index : height * (index + 1), :] = piece[...]


def pile(pieces):
    height, width = pieces[0].shape
    return pl.pallas_call(
        pile_kernel,
        name="pile",
        out_shape=shaped((height * len(pieces), width), bf16),
        compiler_params=pltpu.CompilerParams(vmem_limit_bytes=16 << 20),
        cost_estimate=pl.CostEstimate(flops=0, bytes_accessed=2_000_000, transcendentals=0),
    )(*pieces)


def around_z(hops):
    return [(i, (i + 8 * hops) % 32) for i in range(32)]


def across(turn):
    return [(i, i ^ (2 if (i & 1) == turn else 4)) for i in range(32)]


def along_z(bit):
    return [(i, i ^ (8 * bit)) for i in range(32)]


def between_cores():
    return [(i, i ^ 1) for i in range(32)]


def make_table():
    table = np.zeros((32, 129), np.int32)
    for device in range(32):
        core, x, y, z = device & 1, (device >> 1) & 1, (device >> 2) & 1, device >> 3
        table[device, 64] = core
        for half in range(2):
            turn = core ^ half

            def owner(there_z, first, second):
                there_x, there_y = (x ^ first, y ^ second) if turn == 0 else (x ^ second, y ^ first)
                return there_z * 4 + there_y * 2 + there_x

            for block in range(16):
                hops, middle, high = block & 3, (block >> 2) & 1, block >> 3
                turned = z ^ (0, 2, 1, 3)[hops]
                table[device, 16 * half + block] = owner((z - hops) % 4, middle, high)
                table[device, 32 + 16 * half + block] = owner(turned, high, middle)
                table[device, 65 + 16 * half + block] = owner(turned, middle, high)
                turned = z ^ (0, 2, 1, 3)[block >> 2]
                table[device, 97 + 16 * half + block] = owner(turned, block & 1, (block >> 1) & 1)
    return table


def hop_parts(block):
    return [block] + [lax.ppermute(block, ALL, around_z(hops)) for hops in (1, 2, 3)]


def hop_across(held, turn):
    return lax.ppermute(held, ALL, across(turn))


def hop_core(held):
    return lax.ppermute(held, ALL, between_cores())


def follow(value, earlier):
    return lax.optimization_barrier((value, earlier))[0]


def add_low(*terms):
    total = terms[0].astype(f32)
    for term in terms[1:]:
        total = total + term.astype(f32)
    return total


def add_halves(keep, arrived):
    half = keep.shape[0] // 2
    sent = add_low(keep[half:], arrived[half:]).astype(bf16)
    return add_low(keep[:half], arrived[:half]).astype(bf16), sent


def hop_z(held, bit):
    return lax.ppermute(held, ALL, along_z(bit))


def gather_plain(mine, other):
    pieces = []
    for block in (mine, other):
        full = lax.all_gather(block, "fsdp", axis=0, tiled=True)
        half = full.shape[0] // 2
        pieces += [full[:half], full[half:]]
    return pieces


def scatter_plain(keep, send):
    both = add_low(keep, lax.ppermute(send, "rep", [(0, 1), (1, 0)]))
    return lax.psum_scatter(both, "fsdp", scatter_dimension=0, tiled=True)


def join(core, mine):
    other = lax.ppermute(mine, "rep", [(0, 1), (1, 0)])
    low = jnp.where(core == 0, mine, other)
    high = jnp.where(core == 0, other, mine)
    return jnp.concatenate([low, high], axis=1)


def half_of(weight, place):
    width = weight.shape[1] // 2
    return lax.dynamic_slice_in_dim(weight, place * width, width, axis=1)


def local(
    chips,
    tokens,
    masked,
    cotangent,
    mask_vector,
    heads_weight,
    query_bias,
    value_bias,
    output_weight,
    output_bias,
    first_gain,
    first_shift,
    expand_weight,
    expand_bias,
    reduce_weight,
    reduce_bias,
    second_gain,
    second_shift,
):
    core = lax.axis_index("rep")
    layout = tokens.shape
    height = layout[0] * layout[1] * layout[2]
    share = mask_vector.shape[0]
    by_hops = chips == BLOCKS
    if by_hops:
        table = lax.dynamic_index_in_dim(
            jnp.asarray(make_table()), lax.axis_index("fsdp") * 2 + core, axis=0, keepdims=False
        )
    else:
        table = jnp.tile(jnp.arange(BLOCKS, dtype=jnp.int32), 4)
        table = jnp.concatenate([table, core[None].astype(jnp.int32), table])

    vector_rows = jnp.concatenate(
        [
            mask_vector[None],
            query_bias[None],
            value_bias[None],
            output_bias[None],
            first_gain[None],
            first_shift[None],
            *[expand_bias[None, share * group : share * (group + 1)] for group in range(4)],
            reduce_bias[None],
            second_gain[None],
            second_shift[None],
        ],
        axis=0,
    )
    vector_columns = jnp.pad(vector_rows.T, ((0, 0), (0, LANES - VECTORS)))

    def payloads(place):
        return (
            jnp.concatenate([half_of(heads_weight, place), vector_columns], axis=1),
            jnp.concatenate([half_of(output_weight, place), half_of(expand_weight, place)], axis=1),
            half_of(reduce_weight, place),
        )

    flat_tokens = tokens.reshape(height, D)
    flat_cotangent = cotangent.reshape(height, D)
    flags = masked.reshape(height).astype(bf16)
    mask = jnp.broadcast_to(flags[:, None], (height, LANES))
    marks = jnp.concatenate([jnp.ones((1, height), bf16), flags[None], jnp.zeros((14, height), bf16)], axis=0)
    size = 512
    sequences = height // L
    half = sequences // 2

    if by_hops:
        first_load, middle_load, last_load = payloads(core)
        held = pile(hop_parts(first_load))
        last_held = pile([last_load, hop_across(last_load, 0)])
        last_held = pile([last_held, hop_across(last_held, 1)])
        middle_held = follow(middle_load, held)
        middle_moved = hop_z(middle_held, 2)
        near = pile([held, follow(hop_across(held, 0), (middle_moved, last_held, mask, marks, table))])
        far = hop_across(near, 1)
        middle_held = pile([middle_held, middle_moved])
        middle_moved = hop_z(middle_held, 1)
        heads = (near, far, hop_core(near), hop_core(follow(far, middle_moved)))
        middle_held = pile([middle_held, middle_moved])
        done = attend(table, flat_tokens, mask, heads, None, 0, half)
        middle_near = pile([middle_held, follow(hop_across(follow(middle_held, far), 0), done[6])])
        vec = done[6]
        done = attend(table, flat_tokens, mask, heads, done, half, sequences - half, after=(middle_near,))
        middle_far = hop_across(middle_near, 1)
        last_near = pile([last_held, follow(hop_z(follow(last_held, far), 2), done[6])])
        middle_far_other = hop_core(follow(middle_far, (done[6], last_near)))
        middle = (middle_near, middle_far, hop_core(middle_near), middle_far_other)
        after = (last_near,)
    else:
        heads, middle, last = [gather_plain(a, b) for a, b in zip(payloads(core), payloads(1 - core))]
        done = attend(table, flat_tokens, mask, heads, None, 0, sequences)
        vec = done[6]
        after = ()
    x, qkv, raised, inverse, context, turned, _, heads_whole = done
    bias = vec[6:10].reshape(4, D // share, share).transpose(1, 0, 2).reshape(1, FF)
    unit, rate, low, active, slope, *middle_whole = expand(table, context, x, vec, bias, middle, size, after=after)
    if by_hops:
        last_far = hop_z(last_near, 1)
        last = (last_near, last_far, hop_core(last_near), hop_core(follow(last_far, unit)))

    outputs, outer, hidden, second_sums, bias_sums, keep, send = reduce(
        table, active, slope, unit, low, flat_cotangent, mask, vec, last, size
    )
    bias_rows = jnp.sum(bias_sums, axis=0).reshape(D // share, 4, share).transpose(1, 0, 2).reshape(4, D)

    def inner_call(after=()):
        return inner_pass(hidden, outer, unit, rate, mask, vec, middle_whole, size, after=after)

    def back_call(after=()):
        return attend_back(qkv, raised, inverse, turned, grad_context, after=after)

    def heads_call(after=()):
        return heads_grad(table, x, marks, mixed, second_sums, inner_sums, bias_rows, heads_whole, 2 * size, after=after)

    def rows_call(after=()):
        return rows_grad(mixed, inner, mask, heads_whole, size, after=after)

    if by_hops:
        arrived = hop_core(send)
        inner, grad_context, inner_sums = inner_call()
        rest_keep, sent = add_halves(keep, arrived)
        arrived = hop_across(sent, 0)
        mixed = back_call(after=(rest_keep, sent))
        rest_keep, sent = add_halves(rest_keep, arrived)
        rest_arrived = hop_across(sent, 1)
        keep, send = heads_call(after=(rest_keep, sent))
        arrived = hop_core(send)
        rest_keep, rest_sent = add_halves(follow(rest_keep, keep), rest_arrived)
        rest_arrived = hop_z(rest_sent, 1)
        out_keep, out_send = out_grad(table, context, inner, 2 * size, after=(keep, rest_keep, rest_sent))
        out_arrived = hop_core(out_send)
        keep, sent = add_halves(keep, follow(arrived, out_keep))
        arrived = hop_across(sent, 0)
        out_keep, out_sent = add_halves(follow(out_keep, sent), out_arrived)
        out_arrived = hop_across(out_sent, 0)
        grad_tokens = rows_call(after=(sent, out_keep, out_sent))
        keep, sent = add_halves(follow(keep, grad_tokens), arrived)
        arrived = hop_across(sent, 1)
        rest_keep, rest_sent = add_halves(follow(rest_keep, sent), rest_arrived)
        rest_arrived = hop_z(rest_sent, 2)
        out_keep, out_sent = add_halves(follow(out_keep, rest_sent), out_arrived)
        out_arrived = hop_across(out_sent, 1)
        keep, sent = add_halves(follow(keep, out_sent), arrived)
        arrived = hop_z(sent, 1)
        rest_share = add_low(follow(rest_keep, sent), rest_arrived)
        out_keep, out_sent = add_halves(follow(out_keep, sent), out_arrived)
        out_arrived = hop_z(out_sent, 1)
        keep, sent = add_halves(keep, arrived)
        arrived = hop_z(sent, 2)
        out_keep, out_sent = add_halves(follow(out_keep, sent), out_arrived)
        out_share = add_low(out_keep, hop_z(out_sent, 2))
        heads_share = add_low(keep, arrived)
    else:
        rest_share = scatter_plain(keep, send)
        inner, grad_context, inner_sums = inner_call()
        out_share = scatter_plain(*out_grad(table, context, inner, size))
        mixed = back_call()
        heads_share = scatter_plain(*heads_call())
        grad_tokens = rows_call()

    last_share = jnp.concatenate([rest_share[:, D // 2 * group : D // 2 * (group + 1)] for group in range(4)], axis=0)
    vector_grads = heads_share[:, QKV // 2 :]

    def vector(index):
        return vector_grads[:, index]

    return (
        outputs.reshape(layout),
        grad_tokens.reshape(layout),
        vector(0),
        join(core, heads_share[:, : QKV // 2]),
        vector(1),
        vector(2),
        join(core, out_share),
        vector(3),
        vector(4),
        vector(5),
        join(core, rest_share[:, FF // 2 :]),
        vector_grads[:, 6:10].T.reshape(-1),
        join(core, last_share),
        vector(10),
        vector(11),
        vector(12),
    )


def solution(mesh):
    in_specs = (
        P(None, ("fsdp", "rep"), None, None),
        P(None, ("fsdp", "rep"), None),
        P(None, ("fsdp", "rep"), None, None),
        P("fsdp"),
        P("fsdp", None),
        P("fsdp"),
        P("fsdp"),
        P("fsdp", None),
        P("fsdp"),
        P("fsdp"),
        P("fsdp"),
        P("fsdp", None),
        P("fsdp"),
        P("fsdp", None),
        P("fsdp"),
        P("fsdp"),
        P("fsdp"),
    )
    out_specs = (
        P(None, ("fsdp", "rep"), None, None),
        P(None, ("fsdp", "rep"), None, None),
        P("fsdp"),
        P("fsdp", None),
        P("fsdp"),
        P("fsdp"),
        P("fsdp", None),
        P("fsdp"),
        P("fsdp"),
        P("fsdp"),
        P("fsdp", None),
        P("fsdp"),
        P("fsdp", None),
        P("fsdp"),
        P("fsdp"),
        P("fsdp"),
    )
    return jax.shard_map(
        functools.partial(local, mesh.shape["fsdp"]),
        mesh=mesh,
        in_specs=in_specs,
        out_specs=out_specs,
        check_vma=False,
    )
```
